32 devices in a mesh: lat: 4 (over x, core), lon: 8 (over z, y).
Axes of the slice: x: 2, y: 2, z: 4, core: 2. Of those that a mesh axis runs over, the one named last changes fastest.
Arguments:
- features: float32 [4, 24, 96, 192], P(None, 'lat', 'lon'), may hold values from -460 to 460
- cotangent: float32 [4, 24, 96, 192], P(None, 'lat', 'lon'), may hold values from -6 to 6
- norm_gain: float32 [192], replicated, may hold values from 0.1 to 1.9
- norm_shift: float32 [192], replicated, may hold values from -3 to 3
- qkv_weight: float32 [192, 576], replicated, may hold values from -0.4375 to 0.4375
- out_weight: float32 [192, 192], replicated, may hold values from -0.4375 to 0.4375
- bias_table: float32 [4, 2, 6, 23, 144], P('lat'), may hold values from -6 to 305
Outputs:
- grad_features: float32 [4, 24, 96, 192], P(None, 'lat', 'lon')
- grad_weights: float32 [192, 768], P('lat', 'lon')
- grad_bias: float32 [4, 2, 6, 23, 144], P('lat')
- grad_norm: float32 [2, 192], replicated
The draws below stay inside these ranges and needn't reach their ends.
All inputs are finite; a program needn't handle non-finite values.
Results may differ from the reference program's by a relative error of at most 0.0003.
Values sent between devices are 32-bit elements; how exact they have to be, the bound alone decides.
No kernel may reach another device: no remote copies, remote signals or barrier semaphores. Data moves between devices by JAX's collectives and lax.ppermute only.
A program may use at most 128 MiB of HBM per device.

```python
import math
import jax
import jax.numpy as jnp
from jax import lax

D = 192
HEADS = 6
HEAD = 32
ZP = 4
WZ = 2
WLAT = 6
WLON = 12
NLAT = 24
NLON = 96
LATW = 4
PW = 2
WIN = 144
LONREL = 23
PAIRS = 144
TOKENS = 9216


def draw_features(key, part):
    first, second, third, fourth = jax.random.split(key, 4)
    shape = (ZP, NLAT, NLON, D)
    base = jnp.clip(jax.random.normal(first, shape, jnp.float32), -4.0, 4.0)
    row_scale = jnp.exp(jax.random.uniform(second, (ZP, NLAT, NLON, 1), jnp.float32, 0.0, math.log(10.0)))
    column_scale = jnp.exp(jax.random.uniform(third, (D,), jnp.float32, 0.0, math.log(10.0)))
    centre = jnp.clip(jax.random.normal(fourth, (D,), jnp.float32), -3.0, 3.0) * 2.0
    return row_scale * (base * column_scale + centre)


def draw_bias_table(key, part):
    first = jax.random.fold_in(key, 0)
    shape = (LATW, PW, HEADS, LONREL, PAIRS)
    base = jnp.clip(jax.random.normal(first, shape, jnp.float32), -6.0, 6.0)
    return base


def steps_of(rng, shape, pieces, smallest, top_value):
    def one(position, blocks):
        draws = jax.random.uniform(jax.random.fold_in(jax.random.fold_in(rng, 6), position), (blocks,), jnp.float32, smallest / len(pieces), top_value / len(pieces))
        return jnp.repeat(jnp.exp(draws), shape[position] // blocks).reshape((-1,) + (1,) * (len(shape) - position - 1))

    level = one(*pieces[0])
    for cut in pieces[1:]:
        level = level * one(*cut)
    return level


def scatter_about(rng, dims, spread, most, cuts=(), held_as=jnp.bfloat16):
    entries = spread * jax.random.normal(rng, dims, jnp.float32)
    if cuts:
        entries = entries * steps_of(rng, dims, cuts, -0.22, 0.18)
    return jnp.clip(entries, -most, most).astype(held_as)


def setup_inputs(seed: int = 0) -> dict:
    keys = jax.random.split(jax.random.key(seed), 8)
    features = draw_features(jax.random.fold_in(keys[7], 71), 0)
    cotangent = scatter_about(keys[1], (ZP, NLAT, NLON, D), 1.0, 6.0, ((1, 4), (2, 8)), jnp.float32)
    norm_gain = jnp.clip(1.0 + 0.18 * jax.random.normal(keys[2], (D,), jnp.float32), 0.1, 1.9)
    norm_shift = scatter_about(keys[3], (D,), 0.5, 3.0, (), jnp.float32)
    qkv_weight = scatter_about(keys[4], (D, 3 * D), D ** -0.5, 0.4375, (), jnp.float32)
    out_weight = scatter_about(keys[5], (D, D), D ** -0.5, 0.4375, (), jnp.float32)
    bias_table = draw_bias_table(jax.random.fold_in(keys[7], 71), 0)
    return dict(features=features, cotangent=cotangent, norm_gain=norm_gain, norm_shift=norm_shift, qkv_weight=qkv_weight, out_weight=out_weight, bias_table=bias_table)


EPSILON = 1e-05
HIGH = lax.Precision.HIGHEST

def offset_table():
    columns = jnp.arange(WLON, dtype=jnp.int32)
    offset = columns[None, :] - columns[:, None] + (WLON - 1)
    return (offset[:, :, None] == jnp.arange(LONREL, dtype=jnp.int32)[None, None, :]).astype(jnp.float32)

def level_valid():
    level = jnp.arange(WIN, dtype=jnp.int32) // (WLAT * WLON)
    same_level = level[:, None] == level[None, :]
    window_index = jnp.arange(PW, dtype=jnp.int32)[:, None, None]
    return (window_index > 0) | same_level[None, :, :]

def expand_bias(table, onehot):
    leading = table.shape[:-3]
    split_table = table.reshape(leading + (HEADS, LONREL, WZ, WZ, WLAT, WLAT))
    full_bias = jnp.einsum('...hrijab,xyr->...hiaxjby', split_table, onehot, precision=HIGH)
    return full_bias.reshape(leading + (HEADS, WIN, WIN))

def band_forward(band, gain, shift, qkv_weight, out_weight, table_band):
    onehot = offset_table()
    average = lax.optimization_barrier(jnp.mean(band, -1, keepdims=True))
    centred = band - average
    standard = centred * lax.rsqrt(lax.optimization_barrier(jnp.mean(centred * centred, -1, keepdims=True)) + EPSILON)
    normed = standard * gain + shift
    shifted = jnp.roll(jnp.roll(normed, 1, 0), WLON // 2, 2)
    col_count = shifted.shape[2] // WLON
    windows = shifted.reshape(PW, WZ, WLAT, col_count, WLON, D).transpose(0, 3, 1, 2, 4, 5).reshape(PW, col_count, WIN, D)
    projected = jnp.einsum('pnwd,de->pnwe', windows, qkv_weight, precision=HIGH)
    query_heads = projected[..., :D].reshape(PW, col_count, WIN, HEADS, HEAD)
    key_heads = projected[..., D:2 * D].reshape(PW, col_count, WIN, HEADS, HEAD)
    value_heads = projected[..., 2 * D:].reshape(PW, col_count, WIN, HEADS, HEAD)
    bias_full = expand_bias(table_band, onehot)
    scores = jnp.einsum('pnahe,pnbhe->pnhab', query_heads, key_heads, precision=HIGH) * HEAD ** (-0.5) + bias_full[:, None]
    scores = jnp.where(level_valid()[:, None, None], scores, -jnp.inf)
    attention = jax.nn.softmax(scores, axis=-1)
    mixture = jnp.einsum('pnhab,pnbhe->pnahe', attention, value_heads, precision=HIGH).reshape(PW, col_count, WIN, D)
    output = jnp.einsum('pnwd,de->pnwe', mixture, out_weight, precision=HIGH)
    back = output.reshape(PW, col_count, WZ, WLAT, WLON, D).transpose(0, 2, 3, 1, 4, 5).reshape(ZP, WLAT, col_count * WLON, D)
    return jnp.roll(jnp.roll(back, -(WLON // 2), 2), -1, 0)

def reference(features, cotangent, norm_gain, norm_shift, qkv_weight, out_weight, bias_table):

    def step(carry, index):
        start = (index * WLAT).astype(jnp.int32)
        band = lax.dynamic_slice_in_dim(features, start, WLAT, 1)
        band_grad = lax.dynamic_slice_in_dim(cotangent, start, WLAT, 1)
        table_band = lax.dynamic_index_in_dim(bias_table, index, 0, keepdims=False)
        _, pullback = jax.vjp(band_forward, band, norm_gain, norm_shift, qkv_weight, out_weight, table_band)
        grad_band, grad_gain, grad_shift, grad_qkv, grad_out, grad_table = pullback(band_grad)
        carry = (carry[0] + grad_gain, carry[1] + grad_shift, carry[2] + grad_qkv, carry[3] + grad_out)
        return (carry, (grad_band + band_grad, grad_table))
    start_carry = (jnp.zeros((D,), jnp.float32), jnp.zeros((D,), jnp.float32), jnp.zeros((D, 3 * D), jnp.float32), jnp.zeros((D, D), jnp.float32))
    carry, (grad_bands, grad_bias) = lax.scan(step, start_carry, jnp.arange(LATW, dtype=jnp.int32))
    grad_features = grad_bands.transpose(1, 0, 2, 3, 4).reshape(ZP, NLAT, NLON, D)
    factor = 1.0 / math.sqrt(TOKENS)
    grad_weights = jnp.concatenate([carry[2], carry[3]], axis=1) * factor
    grad_norm = jnp.stack([carry[0], carry[1]]) * factor
    return (grad_features, grad_weights, grad_bias, grad_norm)
```

```python
import functools
import math

import jax
import jax.numpy as jnp
from jax import lax
from jax.experimental import pallas as pl
from jax.experimental.pallas import tpu as pltpu
from jax.sharding import PartitionSpec as P

D = 192
HEADS = 6
HEAD = 32
ZP = 4
WZ = 2
WLAT = 6
WLON = 12
PW = 2
WIN = 144
LONREL = 23
PAIRS = 144
HALF = WLON // 2
LEVELS = WZ * WLAT
HALF_ROWS = HALF * LEVELS
GROUP = 4
GROUPS = WLON // GROUP
GROUP_ROWS = GROUP * LEVELS
BLOCK = HEADS * GROUP_ROWS
STRIP = LONREL * LEVELS

EPSILON = 1e-05
SCALE = HEAD ** (-0.5)
HIGH = lax.Precision.HIGH
FULL = lax.Precision.HIGHEST


def dot(left, right, precision=HIGH):
    return lax.dot_general(
        left, right, (((1,), (0,)), ((), ())), precision=precision, preferred_element_type=jnp.float32
    )


def dot_right_transposed(left, right, precision=HIGH):
    return lax.dot_general(
        left, right, (((1,), (1,)), ((), ())), precision=precision, preferred_element_type=jnp.float32
    )


def dot_left_transposed(left, right, precision=HIGH):
    return lax.dot_general(
        left, right, (((0,), (0,)), ((), ())), precision=precision, preferred_element_type=jnp.float32
    )


def whole(count):
    return [pl.BlockSpec(memory_space=pltpu.VMEM)] * count


def pack_kernel(features_ref, cotangent_ref, sent_ref, own_ref):
    for c in range(PW):
        for i in range(WZ):
            z = (WZ * c + i - 1) % ZP
            for a in range(WLAT):
                rows = pl.ds(i * WLAT + a, HALF, stride=LEVELS)
                both = jnp.concatenate([features_ref[z, a], cotangent_ref[z, a]], axis=-1)
                for tile in range(3):
                    own_ref[tile, c, rows, :] = both[:HALF, tile * 128 : (tile + 1) * 128]
                    sent_ref[tile, c, rows, :] = both[HALF:, tile * 128 : (tile + 1) * 128]


def unpack_kernel(own_ref, returned_ref, out_ref):
    for c in range(PW):
        for i in range(WZ):
            z = (WZ * c + i - 1) % ZP
            for a in range(WLAT):
                rows = pl.ds(i * WLAT + a, HALF, stride=LEVELS)
                for first, half_ref in ((0, own_ref), (HALF, returned_ref)):
                    out_ref[z, a, first : first + HALF, :128] = half_ref[c, rows, :]
                    out_ref[z, a, first : first + HALF, 128:] = half_ref[2, rows, :][:, c * 64 : (c + 1) * 64]


def block_kernel(
    factor, lat_count, lon_count,
    own_ref, borrowed_ref, gain_ref, shift_ref, qkv_ref, out_w_ref, strip_ref,
    grad_own_ref, grad_borrowed_ref, weights_ref, strip_grad_ref, norm_ref,
    table_ref, table_grad_ref, sums_ref,
):
    gain = gain_ref[...]
    shift = shift_ref[...]
    weight_q = qkv_ref[:, :D]
    weight_k = qkv_ref[:, D : 2 * D]
    weight_v = qkv_ref[:, 2 * D :]
    out_weight = out_w_ref[...]
    head_of_lane = lax.broadcasted_iota(jnp.int32, (GROUP_ROWS, D), 1) // HEAD

    def stacked(value):
        blocks = []
        for g in range(GROUPS):
            rows = value[g * GROUP_ROWS : (g + 1) * GROUP_ROWS]
            for h in range(HEADS):
                blocks.append(jnp.where(head_of_lane == h, rows, 0.0))
        return jnp.concatenate(blocks, axis=0)

    def unstacked(value):
        blocks = []
        for g in range(GROUPS):
            total = None
            for h in range(HEADS):
                first = g * BLOCK + h * GROUP_ROWS
                part = jnp.where(head_of_lane == h, value[first : first + GROUP_ROWS], 0.0)
                total = part if total is None else total + part
            blocks.append(total)
        return jnp.concatenate(blocks, axis=0)

    grad_q_w = grad_k_w = grad_v_w = grad_out_w = None
    gain_sum = shift_sum = None
    results = []
    for c in range(PW):
        for h in range(HEADS):
            strip = strip_ref[c, h * LEVELS : (h + 1) * LEVELS, :]
            if c == 0:
                level = lax.broadcasted_iota(jnp.int32, strip.shape, 0) // WLAT
                key_level = (lax.broadcasted_iota(jnp.int32, strip.shape, 1) % LEVELS) // WLAT
                strip = jnp.where(level == key_level, strip, -jnp.inf)
            for g in range(GROUP):
                first = h * GROUP_ROWS + g * LEVELS
                table_ref[first : first + LEVELS, g * LEVELS : g * LEVELS + STRIP] = strip

        both = jnp.concatenate(
            [jnp.concatenate([borrowed_ref[t, c], own_ref[t, c]], axis=0) for t in range(3)], axis=1
        )
        band = both[:, :D]
        window_grad = both[:, D:]
        average = jnp.mean(band, axis=-1, keepdims=True)
        centred = band - average
        inverse = lax.rsqrt(jnp.mean(centred * centred, axis=-1, keepdims=True) + EPSILON)
        unit = centred * inverse
        tokens = unit * gain + shift
        queries = dot(tokens, weight_q, FULL) * SCALE
        keys = dot(tokens, weight_k, FULL)
        values = dot(tokens, weight_v)
        grad_mixture = dot_right_transposed(window_grad, out_weight)
        query_stack = stacked(queries)
        grad_stack = stacked(grad_mixture)

        scores = dot_right_transposed(query_stack, keys, FULL)
        biased = []
        for g in range(GROUPS):
            start = (WLON - 1 - GROUP * g) * LEVELS
            biased.append(scores[g * BLOCK : (g + 1) * BLOCK] + table_ref[:, start : start + WIN])
        scores = jnp.concatenate(biased, axis=0)
        exponent = jnp.exp(scores - jnp.max(scores, axis=-1, keepdims=True))
        attention = exponent * (1.0 / jnp.sum(exponent, axis=-1, keepdims=True))
        mixture = unstacked(dot(attention, values))
        grad_attention = dot_right_transposed(grad_stack, values)
        weighted = jnp.sum(attention * grad_attention, axis=-1, keepdims=True)
        grad_scores = attention * (grad_attention - weighted)
        grad_values = dot_left_transposed(attention, grad_stack)
        grad_queries = unstacked(dot(grad_scores, keys)) * SCALE
        grad_keys = dot_left_transposed(grad_scores, query_stack)

        table_grad_ref[...] = jnp.zeros_like(table_grad_ref)
        for g in range(GROUPS):
            start = (WLON - 1 - GROUP * g) * LEVELS
            table_grad_ref[:, start : start + WIN] += grad_scores[g * BLOCK : (g + 1) * BLOCK]
        for h in range(HEADS):
            total = None
            for g in range(GROUP):
                first = h * GROUP_ROWS + g * LEVELS
                part = table_grad_ref[first : first + LEVELS, g * LEVELS : g * LEVELS + STRIP]
                total = part if total is None else total + part
            strip_grad_ref[c, h * LEVELS : (h + 1) * LEVELS, :] = total

        parts = (
            dot_left_transposed(tokens, grad_queries),
            dot_left_transposed(tokens, grad_keys),
            dot_left_transposed(tokens, grad_values),
            dot_left_transposed(mixture, window_grad),
        )
        for block, part in enumerate(parts):
            if c == 0:
                sums_ref[block] = part
            else:
                sums_ref[block] += part
        grad_tokens = (
            dot_right_transposed(grad_queries, weight_q)
            + dot_right_transposed(grad_keys, weight_k)
            + dot_right_transposed(grad_values, weight_v)
        )
        gain_part = jnp.sum(grad_tokens * unit, axis=0, keepdims=True)
        shift_part = jnp.sum(grad_tokens, axis=0, keepdims=True)
        gain_sum = gain_part if c == 0 else gain_sum + gain_part
        shift_sum = shift_part if c == 0 else shift_sum + shift_part
        grad_unit = grad_tokens * gain
        result = window_grad + inverse * (
            grad_unit
            - jnp.mean(grad_unit, axis=-1, keepdims=True)
            - unit * jnp.mean(grad_unit * unit, axis=-1, keepdims=True)
        )
        results.append(result)
    for ref, rows in ((grad_borrowed_ref, slice(0, HALF_ROWS)), (grad_own_ref, slice(HALF_ROWS, WIN))):
        for c in range(PW):
            ref[c] = results[c][rows, :128]
        ref[2] = jnp.concatenate([result[rows, 128:] for result in results], axis=1)
    norm_ref[...] = jnp.concatenate([gain_sum, shift_sum], axis=0) * factor
    for block in range(4):
        weights_ref[:, block * D : (block + 1) * D] = sums_ref[block] * factor


def exchanged(value, axis, bit):
    count = lax.axis_size(axis)
    return lax.ppermute(value, axis, [(source, source ^ bit) for source in range(count)])


def bits_of(count):
    return [1 << place for place in range(count.bit_length() - 1)]


def summed_part(value, axis, dimension):
    count = lax.axis_size(axis)
    index = lax.axis_index(axis)
    for bit in reversed(bits_of(count)):
        half = value.shape[dimension] // 2
        high = (index & bit) // bit
        kept = lax.dynamic_slice_in_dim(value, high * half, half, dimension)
        given = lax.dynamic_slice_in_dim(value, (1 - high) * half, half, dimension)
        value = kept + exchanged(given, axis, bit)
    return value


def summed(value, axis):
    for bit in bits_of(lax.axis_size(axis)):
        value = value + exchanged(value, axis, bit)
    return value


def shards(features, cotangent, norm_gain, norm_shift, qkv_weight, out_weight, bias_table):
    lat_count, lon_count = lax.axis_size("lat"), lax.axis_size("lon")
    token_count = ZP * features.shape[1] * features.shape[2] * lat_count * lon_count
    factor = 1.0 / math.sqrt(token_count)
    f32 = jnp.float32
    half_shape = jax.ShapeDtypeStruct((3, PW, HALF_ROWS, 128), f32)
    sent, own = pl.pallas_call(
        pack_kernel, out_shape=(half_shape, half_shape), in_specs=whole(2), out_specs=tuple(whole(2))
    )(features, cotangent)
    borrowed = lax.ppermute(sent, "lon", [(s, (s + 1) % lon_count) for s in range(lon_count)])
    strip = bias_table.reshape(PW, HEADS, LONREL, WZ, WZ, WLAT, WLAT).transpose(0, 1, 3, 5, 2, 4, 6)
    strip = strip.reshape(PW, HEADS * LEVELS, STRIP)
    grad_half = jax.ShapeDtypeStruct((3, HALF_ROWS, 128), f32)
    grad_own, grad_borrowed, weights, strip_grad, norm = pl.pallas_call(
        functools.partial(block_kernel, factor, lat_count, lon_count),
        out_shape=(
            grad_half,
            grad_half,
            jax.ShapeDtypeStruct((D, 4 * D), f32),
            jax.ShapeDtypeStruct((PW, HEADS * LEVELS, STRIP), f32),
            jax.ShapeDtypeStruct((2, D), f32),
        ),
        in_specs=whole(7),
        out_specs=tuple(whole(5)),
        scratch_shapes=[
            pltpu.VMEM((BLOCK, 384), f32),
            pltpu.VMEM((BLOCK, 384), f32),
            pltpu.VMEM((4, D, D), f32),
        ],
        compiler_params=pltpu.CompilerParams(vmem_limit_bytes=48 << 20),
    )(own, borrowed, norm_gain[None], norm_shift[None], qkv_weight, out_weight, strip)
    returned = lax.ppermute(grad_borrowed, "lon", [(s, (s - 1) % lon_count) for s in range(lon_count)])
    grad_features = pl.pallas_call(
        unpack_kernel,
        out_shape=jax.ShapeDtypeStruct(features.shape, f32),
        in_specs=whole(2),
        out_specs=whole(1)[0],
    )(grad_own, returned)
    grad_weights = summed_part(summed_part(weights, "lat", 0), "lon", 1)
    strip_grad = summed(strip_grad, "lon")
    grad_norm = summed(summed(norm, "lat"), "lon")
    grad_bias = strip_grad.reshape(PW, HEADS, WZ, WLAT, LONREL, WZ, WLAT).transpose(0, 1, 4, 2, 5, 3, 6)
    grad_bias = grad_bias.reshape(bias_table.shape)
    return (grad_features, grad_weights, grad_bias, grad_norm)


def solution(mesh):
    placed = (
        P(None, "lat", "lon", None),
        P(None, "lat", "lon", None),
        P(),
        P(),
        P(),
        P(),
        P("lat", None, None, None, None),
    )
    return jax.shard_map(
        shards,
        mesh=mesh,
        in_specs=placed,
        out_specs=(
            P(None, "lat", "lon", None),
            P("lat", "lon"),
            P("lat", None, None, None, None),
            P(),
        ),
        check_vma=False,
    )
```

```python
import functools
import math

import jax
import jax.numpy as jnp
from jax import lax
from jax.experimental import pallas as pl
from jax.experimental.pallas import tpu as pltpu
from jax.sharding import PartitionSpec as P

D = 192
HEADS = 6
HEAD = 32
ZP = 4
WZ = 2
WLAT = 6
WLON = 12
PW = 2
WIN = 144
LONREL = 23
PAIRS = 144
HALF = WLON // 2
LEVELS = WZ * WLAT
HALF_ROWS = HALF * LEVELS
GROUP = 4
GROUPS = WLON // GROUP
GROUP_ROWS = GROUP * LEVELS
BLOCK = HEADS * GROUP_ROWS
STRIP = LONREL * LEVELS
PADDED = 16
OFFSETS = 24

EPSILON = 1e-05
SCALE = HEAD ** (-0.5)
HIGH = lax.Precision.HIGH
FULL = lax.Precision.HIGHEST


def dot(left, right, precision=HIGH):
    return lax.dot_general(
        left, right, (((1,), (0,)), ((), ())), precision=precision, preferred_element_type=jnp.float32
    )


def dot_right_transposed(left, right, precision=HIGH):
    return lax.dot_general(
        left, right, (((1,), (1,)), ((), ())), precision=precision, preferred_element_type=jnp.float32
    )


def dot_left_transposed(left, right, precision=HIGH):
    return lax.dot_general(
        left, right, (((0,), (0,)), ((), ())), precision=precision, preferred_element_type=jnp.float32
    )


def whole(count):
    return [pl.BlockSpec(memory_space=pltpu.VMEM)] * count


def pack_kernel(features_ref, cotangent_ref, sent_ref, own_ref):
    for a in range(WLAT):
        for x in range(WLON):
            target_ref = own_ref if x < HALF else sent_ref
            band = features_ref[a, x]
            grad = cotangent_ref[a, x]
            tiles = (band[:, :128], jnp.concatenate([band[:, 128:], grad[:, 128:]], axis=1), grad[:, :128])
            for z in range(ZP):
                c, i = divmod((z + 1) % ZP, WZ)
                row = (x % HALF) * LEVELS + i * WLAT + a
                for tile in range(3):
                    target_ref[tile, c, row : row + 1, :] = tiles[tile][z : z + 1]


def unpack_kernel(own_ref, returned_ref, out_ref):
    for a in range(WLAT):
        for x in range(WLON):
            source_ref = own_ref if x < HALF else returned_ref
            for z in range(ZP):
                c, i = divmod((z + 1) % ZP, WZ)
                row = (x % HALF) * LEVELS + i * WLAT + a
                out_ref[a, x, z : z + 1, :128] = source_ref[c, row : row + 1, :]
                out_ref[a, x, z : z + 1, 128:] = source_ref[2, row : row + 1, c * 64 : (c + 1) * 64]


def pair_order():
    row = lax.broadcasted_iota(jnp.int32, (LEVELS * PADDED, 1), 0)
    key, query = row // PADDED, row % PADDED
    place = (query // WLAT) * 72 + (key // WLAT) * 36 + (query % WLAT) * WLAT + key % WLAT
    place = jnp.where(query < LEVELS, place, -1)
    return (place == lax.broadcasted_iota(jnp.int32, (LEVELS * PADDED, PAIRS), 1)).astype(jnp.float32)


def offset_order():
    row = lax.broadcasted_iota(jnp.int32, (LEVELS * OFFSETS, 1), 0)
    place = (row % OFFSETS) * LEVELS + row // OFFSETS
    columns = lax.broadcasted_iota(jnp.int32, (LEVELS * OFFSETS, LEVELS * OFFSETS), 1)
    return (place == columns).astype(jnp.float32)


def table_kernel(bias_ref, table_ref, turned_ref, strip_ref):
    pairs, offsets = pair_order(), offset_order()
    strip_ref[...] = jnp.zeros_like(strip_ref)
    for c in range(PW):
        rows = jnp.concatenate([bias_ref[h, :, c, :] for h in range(HEADS)], axis=0)
        turned_ref[...] = dot_right_transposed(pairs, rows, FULL)
        for h in range(HEADS):
            for key in range(LEVELS):
                strip_ref[h * PADDED : (h + 1) * PADDED, key * OFFSETS : key * OFFSETS + LONREL] = turned_ref[
                    key * PADDED : (key + 1) * PADDED, h * LONREL : (h + 1) * LONREL
                ]
        strips = dot(strip_ref[...], offsets, FULL)
        if c == 0:
            level = (lax.broadcasted_iota(jnp.int32, strips.shape, 0) % PADDED) // WLAT
            key_level = (lax.broadcasted_iota(jnp.int32, strips.shape, 1) % LEVELS) // WLAT
            strips = jnp.where(level == key_level, strips, -jnp.inf)
        for h in range(HEADS):
            strip = strips[h * PADDED : h * PADDED + LEVELS, :STRIP]
            for g in range(GROUP):
                first = h * GROUP_ROWS + g * LEVELS
                table_ref[c, first : first + LEVELS, g * LEVELS : g * LEVELS + STRIP] = strip


def finish_kernel(parity_ref, mine_ref, other_ref, weights_ref, norm_ref, bias_ref, weights_out_ref, norm_out_ref,
                  strip_ref, turned_ref):
    pairs, offsets = pair_order(), offset_order()
    low = parity_ref[0] == 0
    mine, other = mine_ref[...], other_ref[...]
    halves = (jnp.where(low, mine, other), jnp.where(low, other, mine))
    strip_ref[...] = jnp.zeros_like(strip_ref)
    strips = []
    for half in halves:
        tail = half[112:130]
        last = jnp.concatenate([tail[:, :20], tail[:, 20:40], tail[:, 40:60]], axis=0)
        strips.append(jnp.concatenate([half[:54], half[56:110], last], axis=1))
    for c in range(PW):
        for h in range(HEADS):
            strip = strips[h // 3]
            if c == 1:
                first = (h % 3) * LEVELS
                part = strip[first : first + LEVELS]
            else:
                first = 3 * LEVELS + (h % 3) * WLAT
                part = strip[first : first + WLAT]
                key_level = (lax.broadcasted_iota(jnp.int32, part.shape, 1) % LEVELS) // WLAT
                part = jnp.concatenate([jnp.where(key_level == i, part, 0.0) for i in range(WZ)], axis=0)
            strip_ref[h * PADDED : h * PADDED + LEVELS, :STRIP] = part
        by_level = dot_right_transposed(strip_ref[...], offsets, FULL)
        for h in range(HEADS):
            for key in range(LEVELS):
                turned_ref[key * PADDED : (key + 1) * PADDED, h * LONREL : (h + 1) * LONREL] = by_level[
                    h * PADDED : (h + 1) * PADDED, key * OFFSETS : key * OFFSETS + LONREL
                ]
        rows = dot_left_transposed(turned_ref[...], pairs, FULL)
        for h in range(HEADS):
            bias_ref[h, :, c, :] = rows[h * LONREL : (h + 1) * LONREL]
    weights_out_ref[...] = unpacked_chunk(weights_ref[...])
    norm_out_ref[:, :128] = norm_ref[:2]
    norm_out_ref[0:1, 128:] = norm_ref[2:3, :64]
    norm_out_ref[1:2, 128:] = norm_ref[2:3, 64:]


def packed_chunk(chunk):
    beside = jnp.concatenate([chunk[40:, 32 * piece : 32 * (piece + 1)] for piece in range(3)], axis=0)
    beside = jnp.concatenate([beside, jnp.zeros((16, 32), chunk.dtype)], axis=0)
    return jnp.concatenate([chunk[:40], beside], axis=1)


def unpacked_chunk(packed):
    last = jnp.concatenate([packed[8 * piece : 8 * (piece + 1), 96:] for piece in range(3)], axis=1)
    return jnp.concatenate([packed[:, :96], last], axis=0)


def block_kernel(
    factor, packed,
    own_ref, borrowed_ref, gain_ref, shift_ref, qkv_ref, out_w_ref, table_ref,
    grad_own_ref, grad_borrowed_ref, weights_ref, strip_grad_ref, norm_ref,
    table_grad_ref, sums_ref,
):
    gain = gain_ref[...]
    shift = shift_ref[...]
    weight_q = qkv_ref[:, :D]
    weight_k = qkv_ref[:, D : 2 * D]
    weight_v = qkv_ref[:, 2 * D :]
    out_weight = out_w_ref[...]
    head_of_lane = lax.broadcasted_iota(jnp.int32, (GROUP_ROWS, D), 1) // HEAD

    def stacked(value):
        blocks = []
        for g in range(GROUPS):
            rows = value[g * GROUP_ROWS : (g + 1) * GROUP_ROWS]
            for h in range(HEADS):
                blocks.append(jnp.where(head_of_lane == h, rows, 0.0))
        return jnp.concatenate(blocks, axis=0)

    def unstacked(value):
        blocks = []
        for g in range(GROUPS):
            total = None
            for h in range(HEADS):
                first = g * BLOCK + h * GROUP_ROWS
                part = jnp.where(head_of_lane == h, value[first : first + GROUP_ROWS], 0.0)
                total = part if total is None else total + part
            blocks.append(total)
        return jnp.concatenate(blocks, axis=0)

    grad_q_w = grad_k_w = grad_v_w = grad_out_w = None
    gain_sum = shift_sum = None
    results = []
    strip_parts = ([], [])
    for c in range(PW):
        both = jnp.concatenate(
            [jnp.concatenate([borrowed_ref[t, c], own_ref[t, c]], axis=0) for t in range(3)], axis=1
        )
        band = both[:, :D]
        window_grad = jnp.concatenate([both[:, 256:], both[:, D:256]], axis=1)
        average = jnp.mean(band, axis=-1, keepdims=True)
        centred = band - average
        inverse = lax.rsqrt(jnp.mean(centred * centred, axis=-1, keepdims=True) + EPSILON)
        unit = centred * inverse
        tokens = unit * gain + shift
        queries = dot(tokens, weight_q, FULL) * SCALE
        keys = dot(tokens, weight_k, FULL)
        values = dot(tokens, weight_v)
        grad_mixture = dot_right_transposed(window_grad, out_weight)
        query_stack = stacked(queries)
        grad_stack = stacked(grad_mixture)

        scores = dot_right_transposed(query_stack, keys, FULL)
        biased = []
        for g in range(GROUPS):
            start = (WLON - 1 - GROUP * g) * LEVELS
            biased.append(scores[g * BLOCK : (g + 1) * BLOCK] + table_ref[c, :, start : start + WIN])
        scores = jnp.concatenate(biased, axis=0)
        exponent = jnp.exp(scores - jnp.max(scores, axis=-1, keepdims=True))
        attention = exponent * (1.0 / jnp.sum(exponent, axis=-1, keepdims=True))
        mixture = unstacked(dot(attention, values))
        grad_attention = dot_right_transposed(grad_stack, values)
        weighted = jnp.sum(attention * grad_attention, axis=-1, keepdims=True)
        grad_scores = attention * (grad_attention - weighted)
        grad_values = dot_left_transposed(attention, grad_stack)
        grad_queries = unstacked(dot(grad_scores, keys)) * SCALE
        grad_keys = dot_left_transposed(grad_scores, query_stack)

        table_grad_ref[...] = jnp.zeros_like(table_grad_ref)
        for g in range(GROUPS):
            start = (WLON - 1 - GROUP * g) * LEVELS
            table_grad_ref[:, start : start + WIN] += grad_scores[g * BLOCK : (g + 1) * BLOCK]
        for half in range(2):
            strips = []
            for h in range(3 * half, 3 * half + 3):
                total = None
                for g in range(GROUP):
                    first = h * GROUP_ROWS + g * LEVELS
                    part = table_grad_ref[first : first + LEVELS, g * LEVELS : g * LEVELS + STRIP]
                    total = part if total is None else total + part
                strips.append(total if c == 1 else total[:WLAT] + total[WLAT:])
            strip_parts[half].insert(0, jnp.concatenate(strips, axis=0))

        parts = (
            dot_left_transposed(tokens, grad_queries),
            dot_left_transposed(tokens, grad_keys),
            dot_left_transposed(tokens, grad_values),
            dot_left_transposed(mixture, window_grad),
        )
        for block, part in enumerate(parts):
            if c == 0:
                sums_ref[block] = part
            else:
                sums_ref[block] += part
        grad_tokens = (
            dot_right_transposed(grad_queries, weight_q)
            + dot_right_transposed(grad_keys, weight_k)
            + dot_right_transposed(grad_values, weight_v)
        )
        gain_part = jnp.sum(grad_tokens * unit, axis=0, keepdims=True)
        shift_part = jnp.sum(grad_tokens, axis=0, keepdims=True)
        gain_sum = gain_part if c == 0 else gain_sum + gain_part
        shift_sum = shift_part if c == 0 else shift_sum + shift_part
        grad_unit = grad_tokens * gain
        result = window_grad + inverse * (
            grad_unit
            - jnp.mean(grad_unit, axis=-1, keepdims=True)
            - unit * jnp.mean(grad_unit * unit, axis=-1, keepdims=True)
        )
        results.append(result)
    for ref, rows in ((grad_borrowed_ref, slice(0, HALF_ROWS)), (grad_own_ref, slice(HALF_ROWS, WIN))):
        for c in range(PW):
            ref[c] = results[c][rows, :128]
        ref[2] = jnp.concatenate([result[rows, 128:] for result in results], axis=1)
    for half in range(2):
        strip = jnp.concatenate(strip_parts[half], axis=0)
        strip_grad_ref[half] = jnp.zeros_like(strip_grad_ref[half])
        strip_grad_ref[half, :54, :] = strip[:, :128]
        strip_grad_ref[half, 56:110, :] = strip[:, 128:256]
        for piece in range(3):
            strip_grad_ref[half, 112:130, 20 * piece : 20 * (piece + 1)] = strip[18 * piece : 18 * (piece + 1), 256:]
    gain_sum, shift_sum = gain_sum * factor, shift_sum * factor
    norm_ref[...] = jnp.zeros_like(norm_ref)
    norm_ref[:3] = jnp.concatenate(
        [gain_sum[:, :128], shift_sum[:, :128], jnp.concatenate([gain_sum[:, 128:], shift_sum[:, 128:]], axis=1)], axis=0
    )
    for block in range(4):
        part = sums_ref[block] * factor
        if not packed:
            weights_ref[:, block * D : (block + 1) * D] = part
            continue
        for y in range(2):
            for lat in range(4):
                chunk = part[48 * lat : 48 * (lat + 1), 96 * y : 96 * (y + 1)]
                weights_ref[lat % 2, y, block % 2, block // 2, lat // 2] = packed_chunk(chunk)


def exchanged(value, axis, bit):
    count = lax.axis_size(axis)
    return lax.ppermute(value, axis, [(source, source ^ bit) for source in range(count)])


def bits_of(count):
    return [1 << place for place in range(count.bit_length() - 1)]


def kept_and_given(value, axis, bit):
    high = (lax.axis_index(axis) // bit) % 2
    return (
        lax.dynamic_index_in_dim(value, high, 0, keepdims=False),
        lax.dynamic_index_in_dim(value, 1 - high, 0, keepdims=False),
    )


def exchange_all(values, axis, bit):
    flat = [value.reshape(-1, 128) for value in values]
    arrived = exchanged(jnp.concatenate(flat, axis=0), axis, bit)
    results, first = [], 0
    for value, rows in zip(values, flat):
        results.append(arrived[first : first + rows.shape[0]].reshape(value.shape))
        first += rows.shape[0]
    return results


def chunk_order(lat_count, lon_count):
    lat_bits, lon_bits = bits_of(lat_count), bits_of(lon_count)
    return [("lat", lat_bits[0])] + [("lon", bit) for bit in lon_bits] + [("lat", bit) for bit in lat_bits[1:]]


def chunks_by_bit(weights, lat_count, lon_count):
    rows, columns = weights.shape[0] // lat_count, weights.shape[1] // lon_count
    lat_places, lon_places = len(bits_of(lat_count)), len(bits_of(lon_count))
    split = weights.reshape((2,) * lat_places + (rows,) + (2,) * lon_places + (columns,))
    lat_dims = list(range(lat_places))[::-1]
    lon_dims = list(range(lat_places + 1, lat_places + 1 + lon_places))[::-1]
    order = lat_dims[:1] + lon_dims + lat_dims[1:] + [lat_places, lat_places + 1 + lon_places]
    places = lat_places + lon_places
    split = split.transpose(order).reshape((2,) * places + (rows * columns,))
    words = -(-rows * columns // 1024) * 1024
    split = jnp.pad(split, [(0, 0)] * places + [(0, words - rows * columns)])
    return split.reshape((2,) * places + (words // 128, 128))


def shards(features, cotangent, norm_gain, norm_shift, qkv_weight, out_weight, bias_table):
    lat_count, lon_count = lax.axis_size("lat"), lax.axis_size("lon")
    token_count = ZP * features.shape[1] * features.shape[2] * lat_count * lon_count
    factor = 1.0 / math.sqrt(token_count)
    packed = (lat_count, lon_count) == (4, 8)
    f32 = jnp.float32
    shape = jax.ShapeDtypeStruct
    params = pltpu.CompilerParams(vmem_limit_bytes=48 << 20)
    half_shape = shape((3, PW, HALF_ROWS, 128), f32)
    sent, own = pl.pallas_call(
        pack_kernel, out_shape=(half_shape, half_shape), in_specs=whole(2), out_specs=tuple(whole(2)),
        compiler_params=params,
    )(features.transpose(1, 2, 0, 3), cotangent.transpose(1, 2, 0, 3))
    borrowed = lax.ppermute(sent, "lon", [(s, (s + 1) % lon_count) for s in range(lon_count)])
    table = pl.pallas_call(
        table_kernel,
        out_shape=shape((PW, GROUP_ROWS * HEADS, 384), f32),
        in_specs=whole(1),
        out_specs=whole(1)[0],
        scratch_shapes=[
            pltpu.VMEM((LEVELS * PADDED, HEADS * LONREL), f32),
            pltpu.VMEM((HEADS * PADDED, LEVELS * OFFSETS), f32),
        ],
        compiler_params=params,
    )(bias_table[0].transpose(1, 2, 0, 3))
    grad_half = shape((3, HALF_ROWS, 128), f32)
    grad_own, grad_borrowed, weights, strip_grad, norm = pl.pallas_call(
        functools.partial(block_kernel, factor, packed),
        out_shape=(
            grad_half,
            grad_half,
            shape((2, 2, 2, 2, 2, 40, 128) if packed else (D, 4 * D), f32),
            shape((2, 136, 128), f32),
            shape((8, 128), f32),
        ),
        in_specs=whole(7),
        out_specs=tuple(whole(5)),
        scratch_shapes=[pltpu.VMEM((BLOCK, 384), f32), pltpu.VMEM((4, D, D), f32)],
        compiler_params=params,
    )(own, borrowed, norm_gain[None], norm_shift[None], qkv_weight, out_weight, table)
    if not packed:
        weights = chunks_by_bit(weights, lat_count, lon_count)
    returned = lax.ppermute(grad_borrowed, "lon", [(s, (s - 1) % lon_count) for s in range(lon_count)])
    grad_features = pl.pallas_call(
        unpack_kernel,
        out_shape=shape((WLAT, WLON, ZP, D), f32),
        in_specs=whole(2),
        out_specs=whole(1)[0],
        compiler_params=params,
    )(grad_own, returned).transpose(2, 0, 1, 3)
    other_strip = None
    for axis, bit in chunk_order(lat_count, lon_count):
        kept, given = kept_and_given(weights, axis, bit)
        if axis == "lon" and bit == 1:
            kept_strip, given_strip = kept_and_given(strip_grad, axis, bit)
            more, more_strip, more_norm = exchange_all([given, given_strip, norm], axis, bit)
            strip_grad = kept_strip + more_strip
        elif axis == "lon":
            more, more_strip, more_norm = exchange_all([given, strip_grad, norm], axis, bit)
            strip_grad = strip_grad + more_strip
        else:
            if bit > 1 and other_strip is None:
                other_strip = exchanged(strip_grad, "lon", 1)
            more, more_norm = exchange_all([given, norm], axis, bit)
        weights, norm = kept + more, norm + more_norm
    if packed:
        chunk = weights
    else:
        chunk = jnp.zeros((40, 128), f32)
    parity = (lax.axis_index("lon") % 2).astype(jnp.int32)[None]
    grad_bias, grad_weights, grad_norm = pl.pallas_call(
        finish_kernel,
        out_shape=(shape((HEADS, LONREL, PW, PAIRS), f32), shape((48, 96), f32), shape((2, D), f32)),
        in_specs=[pl.BlockSpec(memory_space=pltpu.SMEM)] + whole(4),
        out_specs=tuple(whole(3)),
        scratch_shapes=[
            pltpu.VMEM((HEADS * PADDED, LEVELS * OFFSETS), f32),
            pltpu.VMEM((LEVELS * PADDED, HEADS * LONREL), f32),
        ],
        compiler_params=params,
    )(parity, strip_grad, other_strip, chunk, norm)
    grad_bias = grad_bias.transpose(2, 0, 1, 3)[None]
    if not packed:
        rows, columns = D // lat_count, 4 * D // lon_count
        grad_weights = weights.reshape(-1)[: rows * columns].reshape(rows, columns)
    return (grad_features, grad_weights, grad_bias, grad_norm)


def solution(mesh):
    placed = (
        P(None, "lat", "lon", None),
        P(None, "lat", "lon", None),
        P(),
        P(),
        P(),
        P(),
        P("lat", None, None, None, None),
    )
    return jax.shard_map(
        shards,
        mesh=mesh,
        in_specs=placed,
        out_specs=(
            P(None, "lat", "lon", None),
            P("lat", "lon"),
            P("lat", None, None, None, None),
            P(),
        ),
        check_vma=False,
    )
```

```python
import functools
import math

import jax
import jax.numpy as jnp
from jax import lax
from jax.experimental import pallas as pl
from jax.experimental.pallas import tpu as pltpu
from jax.sharding import PartitionSpec as P

D = 192
HEADS = 6
HEAD = 32
ZP = 4
WZ = 2
WLAT = 6
WLON = 12
PW = 2
WIN = 144
LONREL = 23
PAIRS = 144
HALF = WLON // 2
LEVELS = WZ * WLAT
HALF_ROWS = HALF * LEVELS
GROUP = 4
GROUPS = WLON // GROUP
GROUP_ROWS = GROUP * LEVELS
BLOCK = HEADS * GROUP_ROWS
STRIP = LONREL * LEVELS
PADDED = 16
OFFSETS = 24

EPSILON = 1e-05
SCALE = HEAD ** (-0.5)
HIGH = lax.Precision.HIGH
FULL = lax.Precision.HIGHEST


def dot(left, right, precision=HIGH):
    return lax.dot_general(
        left, right, (((1,), (0,)), ((), ())), precision=precision, preferred_element_type=jnp.float32
    )


def dot_right_transposed(left, right, precision=HIGH):
    return lax.dot_general(
        left, right, (((1,), (1,)), ((), ())), precision=precision, preferred_element_type=jnp.float32
    )


def dot_left_transposed(left, right, precision=HIGH):
    return lax.dot_general(
        left, right, (((0,), (0,)), ((), ())), precision=precision, preferred_element_type=jnp.float32
    )


def whole(count):
    return [pl.BlockSpec(memory_space=pltpu.VMEM)] * count


def hbm(*values):
    return [pltpu.with_memory_space_constraint(value, pltpu.HBM) for value in values]


def fetched(pairs, semaphores):
    copies = [pltpu.make_async_copy(*pair, semaphores.at[place]) for place, pair in enumerate(pairs)]
    for copy in copies:
        copy.start()
    return copies


def pack_kernel(features_ref, cotangent_ref, sent_ref, own_ref, band_ref, grad_ref, semaphores):
    for copy in fetched([(features_ref, band_ref), (cotangent_ref, grad_ref)], semaphores):
        copy.wait()
    for a in range(WLAT):
        for x in range(WLON):
            target_ref = own_ref if x < HALF else sent_ref
            band = band_ref[a, x]
            grad = grad_ref[a, x]
            tiles = (band[:, :128], jnp.concatenate([band[:, 128:], grad[:, 128:]], axis=1), grad[:, :128])
            for z in range(ZP):
                c, i = divmod((z + 1) % ZP, WZ)
                row = (x % HALF) * LEVELS + i * WLAT + a
                for tile in range(3):
                    target_ref[tile, c, row : row + 1, :] = tiles[tile][z : z + 1]


def unpack_kernel(own_ref, returned_ref, out_ref):
    for a in range(WLAT):
        for x in range(WLON):
            source_ref = own_ref if x < HALF else returned_ref
            for z in range(ZP):
                c, i = divmod((z + 1) % ZP, WZ)
                row = (x % HALF) * LEVELS + i * WLAT + a
                out_ref[a, x, z : z + 1, :128] = source_ref[c, row : row + 1, :]
                out_ref[a, x, z : z + 1, 128:] = source_ref[2, row : row + 1, c * 64 : (c + 1) * 64]


def pair_order():
    row = lax.broadcasted_iota(jnp.int32, (LEVELS * PADDED, 1), 0)
    key, query = row // PADDED, row % PADDED
    place = (query // WLAT) * 72 + (key // WLAT) * 36 + (query % WLAT) * WLAT + key % WLAT
    place = jnp.where(query < LEVELS, place, -1)
    return (place == lax.broadcasted_iota(jnp.int32, (LEVELS * PADDED, PAIRS), 1)).astype(jnp.bfloat16)


def offset_order():
    row = lax.broadcasted_iota(jnp.int32, (LEVELS * OFFSETS, 1), 0)
    place = (row % OFFSETS) * LEVELS + row // OFFSETS
    columns = lax.broadcasted_iota(jnp.int32, (LEVELS * OFFSETS, LEVELS * OFFSETS), 1)
    return (place == columns).astype(jnp.bfloat16)


def parts_of(value, count):
    parts = []
    for _ in range(count):
        parts.append(value.astype(jnp.bfloat16))
        value = value - parts[-1].astype(jnp.float32)
    return parts


def moved(value, order, dims, count):
    total = None
    for part in parts_of(value, count):
        product = lax.dot_general(part, order, (dims, ((), ())), preferred_element_type=jnp.float32)
        total = product if total is None else total + product
    return total


def normalized(band):
    average = jnp.mean(band, axis=-1, keepdims=True)
    centred = band - average
    inverse = lax.rsqrt(jnp.mean(centred * centred, axis=-1, keepdims=True) + EPSILON)
    return centred * inverse, inverse


def split_tiles(half_ref):
    tiles = [half_ref[tile].reshape(WIN, 128) for tile in range(3)]
    band = jnp.concatenate([tiles[0], tiles[1][:, : D - 128]], axis=1)
    grad = jnp.concatenate([tiles[2], tiles[1][:, D - 128 :]], axis=1)
    return band, grad


def projections(half_ref, out_ref, gain, shift, weight_q, weight_k, weight_v, out_weight):
    band, grad = split_tiles(half_ref)
    unit, inverse = normalized(band)
    tokens = unit * gain + shift
    out_ref[0] = unit
    out_ref[1] = jnp.broadcast_to(inverse, unit.shape)
    out_ref[2] = tokens
    out_ref[3] = grad
    out_ref[4] = dot(tokens, weight_q, FULL) * SCALE
    out_ref[5] = dot(tokens, weight_k, FULL)
    out_ref[6] = dot(tokens, weight_v)
    out_ref[7] = dot_right_transposed(grad, out_weight)


def prepare_kernel(
    bias_hbm, own_ref, gain_hbm, shift_hbm, qkv_hbm, out_w_hbm,
    table_ref, projected_ref, affine_ref, parts_ref,
    turned_ref, strip_ref, bias_ref, qkv_ref, semaphores,
):
    copies = fetched(
        [
            (bias_hbm, bias_ref),
            (gain_hbm, affine_ref.at[0:1]),
            (shift_hbm, affine_ref.at[1:2]),
            (qkv_hbm, qkv_ref),
            (out_w_hbm, parts_ref.at[3]),
        ],
        semaphores,
    )
    pairs, offsets = pair_order(), offset_order()
    for copy in copies:
        copy.wait()
    for part in range(3):
        parts_ref[part] = qkv_ref[:, part * D : (part + 1) * D]
    projections(own_ref, projected_ref, affine_ref[0:1], affine_ref[1:2], *(parts_ref[part] for part in range(4)))
    strip_ref[...] = jnp.zeros_like(strip_ref)
    rows = jnp.concatenate([bias_ref[h, :, c, :] for c in range(PW) for h in range(HEADS)], axis=0)
    turned = None
    for part in parts_of(rows, 3):
        product = lax.dot_general(pairs, part, (((1,), (1,)), ((), ())), preferred_element_type=jnp.float32)
        turned = product if turned is None else turned + product
    turned_ref[...] = turned
    for block in range(PW * HEADS):
        for key in range(LEVELS):
            strip_ref[block * PADDED : (block + 1) * PADDED, key * OFFSETS : key * OFFSETS + LONREL] = turned_ref[
                key * PADDED : (key + 1) * PADDED, block * LONREL : (block + 1) * LONREL
            ]
    strips = moved(strip_ref[...], offsets, ((1,), (0,)), 3)
    row = lax.broadcasted_iota(jnp.int32, strips.shape, 0)
    level = (row % PADDED) // WLAT
    key_level = (lax.broadcasted_iota(jnp.int32, strips.shape, 1) % LEVELS) // WLAT
    strips = jnp.where((row >= HEADS * PADDED) | (level == key_level), strips, -jnp.inf)
    for c in range(PW):
        for h in range(HEADS):
            first = (c * HEADS + h) * PADDED
            strip = strips[first : first + LEVELS, :STRIP]
            for g in range(GROUP):
                first = h * GROUP_ROWS + g * LEVELS
                table_ref[c, first : first + LEVELS, g * LEVELS : g * LEVELS + STRIP] = strip


def turn_kernel(strip_ref, rows_ref, turned_ref):
    pairs, offsets = pair_order(), offset_order()
    by_level = moved(strip_ref[...], offsets, ((1,), (1,)), 2)
    for block in range(PW * HEADS):
        for key in range(LEVELS):
            turned_ref[key * PADDED : (key + 1) * PADDED, block * OFFSETS : (block + 1) * OFFSETS] = by_level[
                block * PADDED : (block + 1) * PADDED, key * OFFSETS : (key + 1) * OFFSETS
            ]
    rows = moved(turned_ref[...], pairs, ((0,), (0,)), 2)
    half = HEADS * OFFSETS // 2
    for y in range(2):
        first, second = rows[y * half : (y + 1) * half], rows[(y + 2) * half : (y + 3) * half]
        rows_ref[y, :half] = second[:, :128]
        rows_ref[y, half:] = jnp.concatenate(
            [second[:, 128:], first[:, :36], first[:, 108:], jnp.zeros((half, 40), jnp.float32)], axis=1
        )


def finish_kernel(parity_ref, mine_ref, other_ref, weights_ref, norm_ref, bias_ref, weights_out_ref, norm_out_ref):
    low = parity_ref[0] == 0
    mine, other = mine_ref[...], other_ref[...]
    halves = (jnp.where(low, mine, other), jnp.where(low, other, mine))
    half = HEADS * OFFSETS // 2
    for h in range(HEADS):
        first = (h % 3) * OFFSETS
        left = halves[h // 3][first : first + LONREL]
        right = halves[h // 3][half + first : half + first + LONREL]
        bias_ref[h, :, 1, :] = jnp.concatenate([left, right[:, :16]], axis=1)
        bias_ref[h, :, 0, :] = jnp.concatenate(
            [right[:, 16:52], jnp.zeros((LONREL, 72), jnp.float32), right[:, 52:88]], axis=1
        )
    weights_out_ref[...] = unpacked_chunk(weights_ref[...])
    norm = norm_ref[:4] + norm_ref[4:]
    norm_out_ref[:, :128] = norm[:2]
    norm_out_ref[0:1, 128:] = norm[2:3, :64]
    norm_out_ref[1:2, 128:] = norm[2:3, 64:]


def packed_chunk(chunk):
    beside = jnp.concatenate([chunk[40:, 32 * piece : 32 * (piece + 1)] for piece in range(3)], axis=0)
    beside = jnp.concatenate([beside, jnp.zeros((16, 32), chunk.dtype)], axis=0)
    return jnp.concatenate([chunk[:40], beside], axis=1)


def unpacked_chunk(packed):
    last = jnp.concatenate([packed[8 * piece : 8 * (piece + 1), 96:] for piece in range(3)], axis=1)
    return jnp.concatenate([packed[:, :96], last], axis=0)


def block_kernel(
    factor, packed,
    borrowed_ref, projected_ref, affine_ref, parts_ref, table_ref,
    grad_own_ref, grad_borrowed_ref, weights_ref, strip_grad_ref, norm_ref,
    table_grad_ref, arrived_ref,
):
    gain, shift = affine_ref[0:1], affine_ref[1:2]
    projections(borrowed_ref, arrived_ref, gain, shift, *(parts_ref[part] for part in range(4)))

    def whole_window(index, c):
        rows = slice(c * HALF_ROWS, (c + 1) * HALF_ROWS)
        return jnp.concatenate([arrived_ref[index, rows], projected_ref[index, rows]], axis=0)

    head_of_lane = lax.broadcasted_iota(jnp.int32, (WIN, D), 1) // HEAD

    def stacked(value):
        return jnp.concatenate([jnp.where(head_of_lane == h, value, 0.0) for h in range(HEADS)], axis=0)

    def unstacked(value):
        total = None
        for h in range(HEADS):
            part = jnp.where(head_of_lane == h, value[h * WIN : (h + 1) * WIN], 0.0)
            total = part if total is None else total + part
        return total

    strip_grad_ref[...] = jnp.zeros_like(strip_grad_ref)
    mixtures, grads_q, grads_k, grads_v = [], [], [], []
    for c in range(PW):
        keys, values = whole_window(5, c), whole_window(6, c)
        query_stack = stacked(whole_window(4, c))
        grad_stack = stacked(whole_window(7, c))
        scores = dot_right_transposed(query_stack, keys, FULL)
        biased = []
        for h in range(HEADS):
            for g in range(GROUPS):
                first = h * WIN + g * GROUP_ROWS
                start = (WLON - 1 - GROUP * g) * LEVELS
                bias = table_ref[c, h * GROUP_ROWS : (h + 1) * GROUP_ROWS, start : start + WIN]
                biased.append(scores[first : first + GROUP_ROWS] + bias)
        scores = jnp.concatenate(biased, axis=0)
        exponent = jnp.exp(scores - jnp.max(scores, axis=-1, keepdims=True))
        attention = exponent * (1.0 / jnp.sum(exponent, axis=-1, keepdims=True))
        mixtures.append(unstacked(dot(attention, values)))
        grad_attention = dot_right_transposed(grad_stack, values)
        weighted = jnp.sum(attention * grad_attention, axis=-1, keepdims=True)
        grad_scores = attention * (grad_attention - weighted)
        grads_v.append(dot_left_transposed(attention, grad_stack))
        grads_q.append(unstacked(dot(grad_scores, keys)) * SCALE)
        grads_k.append(dot_left_transposed(grad_scores, query_stack))

        table_grad_ref[...] = jnp.zeros_like(table_grad_ref)
        for h in range(HEADS):
            for g in range(GROUPS):
                first = h * WIN + g * GROUP_ROWS
                start = (WLON - 1 - GROUP * g) * LEVELS
                table_grad_ref[h * GROUP_ROWS : (h + 1) * GROUP_ROWS, start : start + WIN] += grad_scores[
                    first : first + GROUP_ROWS
                ]
        for h in range(HEADS):
            total = None
            for g in range(GROUP):
                first = h * GROUP_ROWS + g * LEVELS
                part = table_grad_ref[first : first + LEVELS, g * LEVELS : g * LEVELS + STRIP]
                total = part if total is None else total + part
            first = (c * HEADS + h) * PADDED
            strip_grad_ref[first : first + LEVELS, :STRIP] = total

    grad_projected = jnp.concatenate(
        [jnp.concatenate(grads, axis=0) for grads in (grads_q, grads_k, grads_v)], axis=1
    )
    tokens, window_grad, unit, inverse = (
        jnp.concatenate([whole_window(index, c) for c in range(PW)], axis=0) for index in (2, 3, 0, 1)
    )
    grad_tokens = sum(
        dot_right_transposed(jnp.concatenate(grads, axis=0), parts_ref[part])
        for part, grads in enumerate((grads_q, grads_k, grads_v))
    )
    grad_unit = grad_tokens * gain
    result = window_grad + inverse * (
        grad_unit
        - jnp.mean(grad_unit, axis=-1, keepdims=True)
        - unit * jnp.mean(grad_unit * unit, axis=-1, keepdims=True)
    )
    for ref, offset in ((grad_borrowed_ref, 0), (grad_own_ref, HALF_ROWS)):
        halves = [result[c * WIN + offset : c * WIN + offset + HALF_ROWS] for c in range(PW)]
        for c in range(PW):
            ref[c] = halves[c][:, :128]
        ref[2] = jnp.concatenate([half[:, 128:] for half in halves], axis=1)
    gain_sum = jnp.sum(grad_tokens * unit, axis=0, keepdims=True) * factor
    shift_sum = jnp.sum(grad_tokens, axis=0, keepdims=True) * factor
    norm_ref[...] = jnp.zeros_like(norm_ref)
    norm_ref[:3] = jnp.concatenate(
        [gain_sum[:, :128], shift_sum[:, :128], jnp.concatenate([gain_sum[:, 128:], shift_sum[:, 128:]], axis=1)], axis=0
    )
    grad_qkv = dot_left_transposed(tokens, grad_projected) * factor
    grad_out = dot_left_transposed(jnp.concatenate(mixtures, axis=0), window_grad) * factor
    if not packed:
        weights_ref[:, : 3 * D] = grad_qkv
        weights_ref[:, 3 * D :] = grad_out
        return
    for block in range(4):
        for y in range(2):
            first = block * D + 96 * y
            column = grad_qkv[:, first : first + 96] if block < 3 else grad_out[:, 96 * y : 96 * (y + 1)]
            for lat in range(4):
                chunk = column[48 * lat : 48 * (lat + 1)]
                place = (y, block % 2, block // 2) if lat % 2 == 0 else (block % 2, block // 2, y)
                weights_ref[(lat % 2,) + place + (lat // 2,)] = packed_chunk(chunk)


def bits_of(count):
    return [1 << place for place in range(count.bit_length() - 1)]


def partners(first_bits, second_bits):
    lat_count, lon_count = lax.axis_size("lat"), lax.axis_size("lon")
    pairs = []
    for lat in range(lat_count):
        for lon in range(lon_count):
            lat_bit, lon_bit = first_bits if lat % 2 == 0 else second_bits
            pairs.append((lat * lon_count + lon, (lat ^ lat_bit) * lon_count + (lon ^ lon_bit)))
    return pairs


def side(first_bits, second_bits):
    lat, lon = lax.axis_index("lat"), lax.axis_index("lon")
    first, second = ((lat & lat_bit | lon & lon_bit) != 0 for lat_bit, lon_bit in (first_bits, second_bits))
    return jnp.where(lat & 1 == 0, first, second).astype(jnp.int32)


def exchanged(value, step):
    return lax.ppermute(value, ("lat", "lon"), partners(*step))


def kept_and_given(value, step):
    high = side(*step)
    return (
        lax.dynamic_index_in_dim(value, high, 0, keepdims=False),
        lax.dynamic_index_in_dim(value, 1 - high, 0, keepdims=False),
    )


def exchange_all(values, step):
    flat = [value.reshape(-1, 128) for value in values]
    arrived = exchanged(jnp.concatenate(flat, axis=0), step)
    results, first = [], 0
    for value, rows in zip(values, flat):
        results.append(arrived[first : first + rows.shape[0]].reshape(value.shape))
        first += rows.shape[0]
    return results


def halving_steps(lat_count, lon_count):
    lat_bits, lon_bits = bits_of(lat_count), bits_of(lon_count)
    lon_steps = [((0, first), (0, second)) for first, second in zip(lon_bits, lon_bits[1:] + lon_bits[:1])]
    lat_steps = [((bit, 0), (bit, 0)) for bit in lat_bits]
    return lat_steps[:1], lon_steps, lat_steps[1:]


def chunks_by_step(weights, lat_count, lon_count):
    rows, columns = weights.shape[0] // lat_count, weights.shape[1] // lon_count
    lat_places, lon_places = len(bits_of(lat_count)), len(bits_of(lon_count))
    split = weights.reshape((2,) * lat_places + (rows,) + (2,) * lon_places + (columns,))
    lat_dims = list(range(lat_places))[::-1]
    lon_dims = list(range(lat_places + 1, lat_places + 1 + lon_places))[::-1]
    halves = []
    for core, dims in enumerate((lon_dims, lon_dims[1:] + lon_dims[:1])):
        order = lat_dims[:1] + dims + lat_dims[1:] + [lat_places, lat_places + 1 + lon_places]
        halves.append(split.transpose(order)[core])
    places = lat_places + lon_places
    split = jnp.stack(halves).reshape((2,) * places + (rows * columns,))
    words = -(-rows * columns // 1024) * 1024
    split = jnp.pad(split, [(0, 0)] * places + [(0, words - rows * columns)])
    return split.reshape((2,) * places + (words // 128, 128))


def shards(features, cotangent, norm_gain, norm_shift, qkv_weight, out_weight, bias_table):
    lat_count, lon_count = lax.axis_size("lat"), lax.axis_size("lon")
    token_count = ZP * features.shape[1] * features.shape[2] * lat_count * lon_count
    factor = 1.0 / math.sqrt(token_count)
    packed = (lat_count, lon_count) == (4, 8)
    f32 = jnp.float32
    shape = jax.ShapeDtypeStruct
    params = pltpu.CompilerParams(vmem_limit_bytes=48 << 20)
    half_shape = shape((3, PW, HALF_ROWS, 128), f32)
    block_shape = (WLAT, WLON, ZP, D)
    sent, own = pl.pallas_call(
        pack_kernel,
        out_shape=(pltpu.VMEM(half_shape.shape, f32),) * 2,
        in_specs=[pl.BlockSpec(memory_space=pltpu.HBM)] * 2,
        out_specs=tuple(whole(2)),
        scratch_shapes=[pltpu.VMEM(block_shape, f32), pltpu.VMEM(block_shape, f32), pltpu.SemaphoreType.DMA((2,))],
        compiler_params=params,
    )(*hbm(features.transpose(1, 2, 0, 3), cotangent.transpose(1, 2, 0, 3)))
    borrowed = lax.ppermute(sent, "lon", [(s, (s + 1) % lon_count) for s in range(lon_count)])
    projected_shape = (8, WIN, D)
    in_hbm = pl.BlockSpec(memory_space=pltpu.HBM)
    bias, gain_row, shift_row, qkv_rows, out_rows = hbm(
        bias_table[0].transpose(1, 2, 0, 3), norm_gain[None], norm_shift[None], qkv_weight, out_weight
    )
    table, projected, affine, parts = pl.pallas_call(
        prepare_kernel,
        out_shape=(
            pltpu.VMEM((PW, GROUP_ROWS * HEADS, 384), f32),
            pltpu.VMEM(projected_shape, f32),
            pltpu.VMEM((2, D), f32),
            pltpu.VMEM((4, D, D), f32),
        ),
        in_specs=[in_hbm] + whole(1) + [in_hbm] * 4,
        out_specs=tuple(whole(4)),
        scratch_shapes=[
            pltpu.VMEM((LEVELS * PADDED, PW * HEADS * LONREL), f32),
            pltpu.VMEM((PW * HEADS * PADDED, LEVELS * OFFSETS), f32),
            pltpu.VMEM((HEADS, LONREL, PW, PAIRS), f32),
            pltpu.VMEM((D, 3 * D), f32),
            pltpu.SemaphoreType.DMA((5,)),
        ],
        compiler_params=params,
    )(bias, own, gain_row, shift_row, qkv_rows, out_rows)
    grad_half = shape((3, HALF_ROWS, 128), f32)
    grad_own, grad_borrowed, weights, strips, norm = pl.pallas_call(
        functools.partial(block_kernel, factor, packed),
        out_shape=(
            grad_half,
            grad_half,
            shape((2, 2, 2, 2, 2, 40, 128) if packed else (D, 4 * D), f32),
            shape((PW * HEADS * PADDED, LEVELS * OFFSETS), f32),
            shape((8, 128), f32),
        ),
        in_specs=whole(5),
        out_specs=tuple(whole(5)),
        scratch_shapes=[pltpu.VMEM((BLOCK, 384), f32), pltpu.VMEM(projected_shape, f32)],
        compiler_params=params,
    )(borrowed, projected, affine, parts, table)
    if not packed:
        weights = chunks_by_step(weights, lat_count, lon_count)
    rows_shape = shape((2, HEADS * OFFSETS, 128), f32)
    strip_grad = pl.pallas_call(
        turn_kernel,
        out_shape=rows_shape,
        in_specs=whole(1),
        out_specs=whole(1)[0],
        scratch_shapes=[pltpu.VMEM((LEVELS * PADDED, PW * HEADS * OFFSETS), f32)],
        compiler_params=params,
    )(strips)
    first_steps, lon_steps, last_steps = halving_steps(lat_count, lon_count)
    norm = jnp.where(lax.axis_index("lon") % 2 == 0, norm, jnp.roll(norm, 4, 0))
    returned = other_strip = None
    for step in first_steps + lon_steps + last_steps:
        kept, given = kept_and_given(weights, step)
        if step in lon_steps:
            given_strip = strip_grad
            if step == lon_steps[0]:
                strip_grad, given_strip = kept_and_given(strip_grad, step)
                given, grad_borrowed = lax.optimization_barrier((given, grad_borrowed))
                returned = lax.ppermute(grad_borrowed, "lon", [(s, (s - 1) % lon_count) for s in range(lon_count)])
            more, more_strip, more_norm = exchange_all([given, given_strip, norm], step)
            strip_grad = strip_grad + more_strip
        else:
            if step == last_steps[0]:
                other_strip = exchanged(strip_grad, lon_steps[0])
            more, more_norm = exchange_all([given, norm], step)
            if step == last_steps[-1]:
                more, returned = lax.optimization_barrier((more, returned))
        weights, norm = kept + more, norm + more_norm
    grad_features = pl.pallas_call(
        unpack_kernel,
        out_shape=shape(block_shape, f32),
        in_specs=whole(2),
        out_specs=whole(1)[0],
        compiler_params=params,
    )(grad_own, returned).transpose(2, 0, 1, 3)
    chunk = weights if packed else jnp.zeros((40, 128), f32)
    parity = side(*lon_steps[0])[None]
    grad_bias, grad_weights, grad_norm = pl.pallas_call(
        finish_kernel,
        out_shape=(shape((HEADS, LONREL, PW, PAIRS), f32), shape((48, 96), f32), shape((2, D), f32)),
        in_specs=[pl.BlockSpec(memory_space=pltpu.SMEM)] + whole(4),
        out_specs=tuple(whole(3)),
        compiler_params=params,
    )(parity, strip_grad, other_strip, chunk, norm)
    grad_bias = grad_bias.transpose(2, 0, 1, 3)[None]
    if not packed:
        rows, columns = D // lat_count, 4 * D // lon_count
        grad_weights = weights.reshape(-1)[: rows * columns].reshape(rows, columns)
    return (grad_features, grad_weights, grad_bias, grad_norm)


def solution(mesh):
    placed = (
        P(None, "lat", "lon", None),
        P(None, "lat", "lon", None),
        P(),
        P(),
        P(),
        P(),
        P("lat", None, None, None, None),
    )
    return jax.shard_map(
        shards,
        mesh=mesh,
        in_specs=placed,
        out_specs=(
            P(None, "lat", "lon", None),
            P("lat", "lon"),
            P("lat", None, None, None, None),
            P(),
        ),
        check_vma=False,
    )
```

```python
import functools
import math

import jax
import jax.numpy as jnp
from jax import lax
from jax.experimental import pallas as pl
from jax.experimental.pallas import tpu as pltpu
from jax.sharding import PartitionSpec as P

D = 192
HEADS = 6
HEAD = 32
ZP = 4
WZ = 2
WLAT = 6
WLON = 12
PW = 2
WIN = 144
LONREL = 23
PAIRS = 144
HALF = WLON // 2
LEVELS = WZ * WLAT
HALF_ROWS = HALF * LEVELS
GROUP = 4
GROUPS = WLON // GROUP
GROUP_ROWS = GROUP * LEVELS
BLOCK = HEADS * GROUP_ROWS
STRIP = LONREL * LEVELS
PADDED = 16
OFFSETS = 24

EPSILON = 1e-05
SCALE = HEAD ** (-0.5)
HIGH = lax.Precision.HIGH
FULL = lax.Precision.HIGHEST


def dot(left, right, precision=HIGH):
    return lax.dot_general(
        left, right, (((1,), (0,)), ((), ())), precision=precision, preferred_element_type=jnp.float32
    )


def dot_right_transposed(left, right, precision=HIGH):
    return lax.dot_general(
        left, right, (((1,), (1,)), ((), ())), precision=precision, preferred_element_type=jnp.float32
    )


def dot_left_transposed(left, right, precision=HIGH):
    return lax.dot_general(
        left, right, (((0,), (0,)), ((), ())), precision=precision, preferred_element_type=jnp.float32
    )


def whole(count):
    return [pl.BlockSpec(memory_space=pltpu.VMEM)] * count


def hbm(*values):
    return [pltpu.with_memory_space_constraint(value, pltpu.HBM) for value in values]


def fetched(pairs, semaphores):
    copies = [pltpu.make_async_copy(*pair, semaphores.at[place]) for place, pair in enumerate(pairs)]
    for copy in copies:
        copy.start()
    return copies


def pack_kernel(features_ref, cotangent_ref, sent_ref, own_ref, band_ref, grad_ref, semaphores):
    for copy in fetched([(features_ref, band_ref), (cotangent_ref, grad_ref)], semaphores):
        copy.wait()
    for a in range(WLAT):
        for x in range(WLON):
            target_ref = own_ref if x < HALF else sent_ref
            band = band_ref[a, x]
            grad = grad_ref[a, x]
            tiles = (band[:, :128], jnp.concatenate([band[:, 128:], grad[:, 128:]], axis=1), grad[:, :128])
            for z in range(ZP):
                c, i = divmod((z + 1) % ZP, WZ)
                row = (x % HALF) * LEVELS + i * WLAT + a
                for tile in range(3):
                    target_ref[tile, c, row : row + 1, :] = tiles[tile][z : z + 1]


def unpack_kernel(own_ref, returned_ref, out_ref):
    for a in range(WLAT):
        for x in range(WLON):
            source_ref = own_ref if x < HALF else returned_ref
            for z in range(ZP):
                c, i = divmod((z + 1) % ZP, WZ)
                row = (x % HALF) * LEVELS + i * WLAT + a
                out_ref[a, x, z : z + 1, :128] = source_ref[c, row : row + 1, :]
                out_ref[a, x, z : z + 1, 128:] = source_ref[2, row : row + 1, c * 64 : (c + 1) * 64]


def pair_order():
    row = lax.broadcasted_iota(jnp.int32, (LEVELS * PADDED, 1), 0)
    key, query = row // PADDED, row % PADDED
    place = (query // WLAT) * 72 + (key // WLAT) * 36 + (query % WLAT) * WLAT + key % WLAT
    place = jnp.where(query < LEVELS, place, -1)
    return (place == lax.broadcasted_iota(jnp.int32, (LEVELS * PADDED, PAIRS), 1)).astype(jnp.bfloat16)


def offset_order():
    row = lax.broadcasted_iota(jnp.int32, (LEVELS * OFFSETS, 1), 0)
    place = (row % OFFSETS) * LEVELS + row // OFFSETS
    columns = lax.broadcasted_iota(jnp.int32, (LEVELS * OFFSETS, LEVELS * OFFSETS), 1)
    return (place == columns).astype(jnp.bfloat16)


def parts_of(value, count):
    parts = []
    for _ in range(count):
        parts.append(value.astype(jnp.bfloat16))
        value = value - parts[-1].astype(jnp.float32)
    return parts


def moved(value, order, dims, count):
    total = None
    for part in parts_of(value, count):
        product = lax.dot_general(part, order, (dims, ((), ())), preferred_element_type=jnp.float32)
        total = product if total is None else total + product
    return total


def normalized(band):
    average = jnp.mean(band, axis=-1, keepdims=True)
    centred = band - average
    inverse = lax.rsqrt(jnp.mean(centred * centred, axis=-1, keepdims=True) + EPSILON)
    return centred * inverse, inverse


def split_tiles(half_ref):
    tiles = [half_ref[tile].reshape(WIN, 128) for tile in range(3)]
    band = jnp.concatenate([tiles[0], tiles[1][:, : D - 128]], axis=1)
    grad = jnp.concatenate([tiles[2], tiles[1][:, D - 128 :]], axis=1)
    return band, grad


def projections(half_ref, out_ref, gain, shift, weight_q, weight_k, weight_v, out_weight):
    band, grad = split_tiles(half_ref)
    unit, inverse = normalized(band)
    tokens = unit * gain + shift
    out_ref[0] = unit
    out_ref[1] = jnp.broadcast_to(inverse, unit.shape)
    out_ref[2] = tokens
    out_ref[3] = grad
    out_ref[4] = dot(tokens, weight_q, FULL) * SCALE
    out_ref[5] = dot(tokens, weight_k, FULL)
    out_ref[6] = dot(tokens, weight_v)
    out_ref[7] = dot_right_transposed(grad, out_weight)


def prepare_kernel(
    bias_hbm, own_ref, gain_hbm, shift_hbm, qkv_hbm, out_w_hbm,
    table_ref, projected_ref, affine_ref, parts_ref,
    turned_ref, strip_ref, bias_ref, qkv_ref, semaphores,
):
    copies = fetched(
        [
            (bias_hbm, bias_ref),
            (gain_hbm, affine_ref.at[0:1]),
            (shift_hbm, affine_ref.at[1:2]),
            (qkv_hbm, qkv_ref),
            (out_w_hbm, parts_ref.at[3]),
        ],
        semaphores,
    )
    pairs, offsets = pair_order(), offset_order()
    for copy in copies:
        copy.wait()
    for part in range(3):
        parts_ref[part] = qkv_ref[:, part * D : (part + 1) * D]
    projections(own_ref, projected_ref, affine_ref[0:1], affine_ref[1:2], *(parts_ref[part] for part in range(4)))
    strip_ref[...] = jnp.zeros_like(strip_ref)
    rows = jnp.concatenate([bias_ref[h, :, c, :] for c in range(PW) for h in range(HEADS)], axis=0)
    turned = None
    for part in parts_of(rows, 3):
        product = lax.dot_general(pairs, part, (((1,), (1,)), ((), ())), preferred_element_type=jnp.float32)
        turned = product if turned is None else turned + product
    turned_ref[...] = turned
    for block in range(PW * HEADS):
        for key in range(LEVELS):
            strip_ref[block * PADDED : (block + 1) * PADDED, key * OFFSETS : key * OFFSETS + LONREL] = turned_ref[
                key * PADDED : (key + 1) * PADDED, block * LONREL : (block + 1) * LONREL
            ]
    strips = moved(strip_ref[...], offsets, ((1,), (0,)), 3)
    row = lax.broadcasted_iota(jnp.int32, strips.shape, 0)
    level = (row % PADDED) // WLAT
    key_level = (lax.broadcasted_iota(jnp.int32, strips.shape, 1) % LEVELS) // WLAT
    strips = jnp.where((row >= HEADS * PADDED) | (level == key_level), strips, -jnp.inf)
    for c in range(PW):
        for h in range(HEADS):
            first = (c * HEADS + h) * PADDED
            strip = strips[first : first + LEVELS, :STRIP]
            for g in range(GROUP):
                first = h * GROUP_ROWS + g * LEVELS
                table_ref[c, first : first + LEVELS, g * LEVELS : g * LEVELS + STRIP] = strip


def turn_kernel(strip_ref, rows_ref, turned_ref):
    pairs, offsets = pair_order(), offset_order()
    by_level = moved(strip_ref[...], offsets, ((1,), (1,)), 2)
    for block in range(PW * HEADS):
        for key in range(LEVELS):
            turned_ref[key * PADDED : (key + 1) * PADDED, block * OFFSETS : (block + 1) * OFFSETS] = by_level[
                block * PADDED : (block + 1) * PADDED, key * OFFSETS : (key + 1) * OFFSETS
            ]
    rows = moved(turned_ref[...], pairs, ((0,), (0,)), 2)
    half = HEADS * OFFSETS // 2
    for y in range(2):
        first, second = rows[y * half : (y + 1) * half], rows[(y + 2) * half : (y + 3) * half]
        rows_ref[y, :half] = second[:, :128]
        rows_ref[y, half:] = jnp.concatenate(
            [second[:, 128:], first[:, :36], first[:, 108:], jnp.zeros((half, 40), jnp.float32)], axis=1
        )


def finish_kernel(parity_ref, mine_ref, other_ref, weights_ref, norm_ref, bias_ref, weights_out_ref, norm_out_ref):
    low = parity_ref[0] == 0
    mine, other = mine_ref[...], other_ref[...]
    halves = (jnp.where(low, mine, other), jnp.where(low, other, mine))
    half = HEADS * OFFSETS // 2
    for h in range(HEADS):
        first = (h % 3) * OFFSETS
        left = halves[h // 3][first : first + LONREL]
        right = halves[h // 3][half + first : half + first + LONREL]
        bias_ref[h, :, 1, :] = jnp.concatenate([left, right[:, :16]], axis=1)
        bias_ref[h, :, 0, :] = jnp.concatenate(
            [right[:, 16:52], jnp.zeros((LONREL, 72), jnp.float32), right[:, 52:88]], axis=1
        )
    weights_out_ref[...] = unpacked_chunk(weights_ref[...])
    norm = norm_ref[:4] + norm_ref[4:]
    norm_out_ref[:, :128] = norm[:2]
    norm_out_ref[0:1, 128:] = norm[2:3, :64]
    norm_out_ref[1:2, 128:] = norm[2:3, 64:]


def packed_chunk(chunk):
    beside = jnp.concatenate([chunk[40:, 32 * piece : 32 * (piece + 1)] for piece in range(3)], axis=0)
    beside = jnp.concatenate([beside, jnp.zeros((16, 32), chunk.dtype)], axis=0)
    return jnp.concatenate([chunk[:40], beside], axis=1)


def unpacked_chunk(packed):
    last = jnp.concatenate([packed[8 * piece : 8 * (piece + 1), 96:] for piece in range(3)], axis=1)
    return jnp.concatenate([packed[:, :96], last], axis=0)


HEADS_AT_ONCE = 6
DEPTH = 1


def halves_of(value):
    high = value.astype(jnp.bfloat16)
    return high, (value - high.astype(jnp.float32)).astype(jnp.bfloat16)


def product(left, right, dims):
    dims = (dims, ((), ()))

    def one(a, b):
        return lax.dot_general(a, b, dims, preferred_element_type=jnp.float32)

    return one(left[0], right[0]) + one(left[0], right[1]) + one(left[1], right[0])


def full_product(left, right, dims):
    dims = (dims, ((), ()))

    def one(a, b):
        return lax.dot_general(a, b, dims, preferred_element_type=jnp.float32)

    low = one(left[0], right[2]) + one(left[2], right[0]) + one(left[1], right[1])
    return low + one(left[0], right[1]) + one(left[1], right[0]) + one(left[0], right[0])


NORMAL = ((1,), (0,))
RIGHT = ((1,), (1,))
LEFT = ((0,), (0,))


def block_kernel(
    factor, packed,
    borrowed_ref, projected_ref, affine_ref, parts_ref, table_ref,
    grad_own_ref, grad_borrowed_ref, weights_ref, strip_grad_ref, norm_ref,
    table_grad_ref, arrived_ref,
):
    gain, shift = affine_ref[0:1], affine_ref[1:2]
    projections(borrowed_ref, arrived_ref, gain, shift, *(parts_ref[part] for part in range(4)))

    def whole_window(index, c):
        rows = slice(c * HALF_ROWS, (c + 1) * HALF_ROWS)
        return jnp.concatenate([arrived_ref[index, rows], projected_ref[index, rows]], axis=0)

    head_of_lane = lax.broadcasted_iota(jnp.int32, (WIN, D), 1) // HEAD
    strip_grad_ref[...] = jnp.zeros_like(strip_grad_ref)
    table_grad_ref[...] = jnp.zeros_like(table_grad_ref)
    windows = []
    for c in range(PW):
        windows.append(
            dict(
                queries=whole_window(4, c),
                grad=whole_window(7, c),
                keys=parts_of(whole_window(5, c), 3),
                values=halves_of(whole_window(6, c)),
                mixture=None, grad_q=None, grad_k=None, grad_v=None,
            )
        )

    def add(window, name, value):
        window[name] = value if window[name] is None else window[name] + value

    def masked(value, heads):
        return jnp.concatenate([jnp.where(head_of_lane == h, value, 0.0) for h in heads], axis=0)

    def joined(value, heads):
        return sum(jnp.where(head_of_lane == h, value[n * WIN : (n + 1) * WIN], 0.0) for n, h in enumerate(heads))

    def first_stage(c, heads):
        window = windows[c]
        stack = parts_of(masked(window["queries"], heads), 3)
        scores = full_product(stack, window["keys"], RIGHT)
        biased = []
        for n, h in enumerate(heads):
            for g in range(GROUPS):
                first = n * WIN + g * GROUP_ROWS
                start = (WLON - 1 - GROUP * g) * LEVELS
                bias = table_ref[c, h * GROUP_ROWS : (h + 1) * GROUP_ROWS, start : start + WIN]
                biased.append(scores[first : first + GROUP_ROWS] + bias)
        scores = jnp.concatenate(biased, axis=0)
        exponent = jnp.exp(scores - jnp.max(scores, axis=-1, keepdims=True))
        attention = exponent * (1.0 / jnp.sum(exponent, axis=-1, keepdims=True))
        return stack[:2], attention

    def second_stage(c, heads, stack, attention):
        window = windows[c]
        halves = halves_of(attention)
        add(window, "mixture", joined(product(halves, window["values"], NORMAL), heads))
        grad_stack = halves_of(masked(window["grad"], heads))
        grad_attention = product(grad_stack, window["values"], RIGHT)
        weighted = jnp.sum(attention * grad_attention, axis=-1, keepdims=True)
        grad_scores = attention * (grad_attention - weighted)
        add(window, "grad_v", product(halves, grad_stack, LEFT))
        return stack, grad_scores

    def third_stage(c, heads, stack, grad_scores):
        window = windows[c]
        halves = halves_of(grad_scores)
        add(window, "grad_q", joined(product(halves, window["keys"][:2], NORMAL), heads))
        add(window, "grad_k", product(halves, stack, LEFT))
        for n, h in enumerate(heads):
            table_rows = slice((c * HEADS + h) * GROUP_ROWS, (c * HEADS + h + 1) * GROUP_ROWS)
            for g in range(GROUPS):
                first = n * WIN + g * GROUP_ROWS
                start = (WLON - 1 - GROUP * g) * LEVELS
                table_grad_ref[table_rows, start : start + WIN] += grad_scores[first : first + GROUP_ROWS]
            total = None
            for g in range(GROUP):
                first = (c * HEADS + h) * GROUP_ROWS + g * LEVELS
                part = table_grad_ref[first : first + LEVELS, g * LEVELS : g * LEVELS + STRIP]
                total = part if total is None else total + part
            first = (c * HEADS + h) * PADDED
            strip_grad_ref[first : first + LEVELS, :STRIP] = total

    chunks = [
        (c, tuple(range(h, h + HEADS_AT_ONCE))) for h in range(0, HEADS, HEADS_AT_ONCE) for c in range(PW)
    ]
    stages = (first_stage, second_stage, third_stage)
    state = {}
    for tick in range(len(chunks) + DEPTH * (len(stages) - 1)):
        for place in reversed(range(len(stages))):
            index = tick - DEPTH * place
            if 0 <= index < len(chunks):
                state[index] = stages[place](*chunks[index], *(state[index] if place else ()))

    def rows_of(name):
        return jnp.concatenate([window[name] for window in windows], axis=0)

    grads = [halves_of(value) for value in (rows_of("grad_q") * SCALE, rows_of("grad_k"), rows_of("grad_v"))]
    tokens, window_grad, unit, inverse = (
        jnp.concatenate([whole_window(index, c) for c in range(PW)], axis=0) for index in (2, 3, 0, 1)
    )
    grad_tokens = sum(product(grads[part], halves_of(parts_ref[part]), RIGHT) for part in range(3))
    grad_unit = grad_tokens * gain
    result = window_grad + inverse * (
        grad_unit
        - jnp.mean(grad_unit, axis=-1, keepdims=True)
        - unit * jnp.mean(grad_unit * unit, axis=-1, keepdims=True)
    )
    for ref, offset in ((grad_borrowed_ref, 0), (grad_own_ref, HALF_ROWS)):
        halves = [result[c * WIN + offset : c * WIN + offset + HALF_ROWS] for c in range(PW)]
        for c in range(PW):
            ref[c] = halves[c][:, :128]
        ref[2] = jnp.concatenate([half[:, 128:] for half in halves], axis=1)
    gain_sum = jnp.sum(grad_tokens * unit, axis=0, keepdims=True) * factor
    shift_sum = jnp.sum(grad_tokens, axis=0, keepdims=True) * factor
    norm_ref[...] = jnp.zeros_like(norm_ref)
    norm_ref[:3] = jnp.concatenate(
        [gain_sum[:, :128], shift_sum[:, :128], jnp.concatenate([gain_sum[:, 128:], shift_sum[:, 128:]], axis=1)], axis=0
    )
    token_halves = halves_of(tokens * factor)
    sums = [product(token_halves, grad, LEFT) for grad in grads]
    sums.append(product(halves_of(rows_of("mixture") * factor), halves_of(window_grad), LEFT))
    for block, total in enumerate(sums):
        if not packed:
            weights_ref[:, block * D : (block + 1) * D] = total
            continue
        for y in range(2):
            for lat in range(4):
                chunk = total[48 * lat : 48 * (lat + 1), 96 * y : 96 * (y + 1)]
                place = (block % 2, block // 2, y) if lat % 2 == 0 else (block // 2, y, block % 2)
                weights_ref[(lat % 2, lat // 2) + place] = packed_chunk(chunk)


def bits_of(count):
    return [1 << place for place in range(count.bit_length() - 1)]


def partners(first_bits, second_bits):
    lat_count, lon_count = lax.axis_size("lat"), lax.axis_size("lon")
    pairs = []
    for lat in range(lat_count):
        for lon in range(lon_count):
            lat_bit, lon_bit = first_bits if lat % 2 == 0 else second_bits
            pairs.append((lat * lon_count + lon, (lat ^ lat_bit) * lon_count + (lon ^ lon_bit)))
    return pairs


def side(first_bits, second_bits):
    lat, lon = lax.axis_index("lat"), lax.axis_index("lon")
    first, second = ((lat & lat_bit | lon & lon_bit) != 0 for lat_bit, lon_bit in (first_bits, second_bits))
    return jnp.where(lat & 1 == 0, first, second).astype(jnp.int32)


def exchanged(value, step):
    return lax.ppermute(value, ("lat", "lon"), partners(*step))


def kept_and_given(value, step):
    high = side(*step)
    return (
        lax.dynamic_index_in_dim(value, high, 0, keepdims=False),
        lax.dynamic_index_in_dim(value, 1 - high, 0, keepdims=False),
    )


def exchange_all(values, step):
    flat = [value.reshape(-1, 128) for value in values]
    arrived = exchanged(jnp.concatenate(flat, axis=0), step)
    results, first = [], 0
    for value, rows in zip(values, flat):
        results.append(arrived[first : first + rows.shape[0]].reshape(value.shape))
        first += rows.shape[0]
    return results


def turned_by(items, count):
    return items[count:] + items[:count]


def summing_steps(lat_count, lon_count):
    lat_bits, lon_bits = bits_of(lat_count), bits_of(lon_count)
    lat_steps = [((bit, 0), (bit, 0)) for bit in lat_bits]
    lon_steps = [((0, first), (0, second)) for first, second in zip(turned_by(lon_bits, 1), turned_by(lon_bits, 2))]
    return lat_steps, lon_steps, lon_steps[-1]


def chunks_by_step(weights, lat_count, lon_count):
    rows, columns = weights.shape[0] // lat_count, weights.shape[1] // lon_count
    lat_places, lon_places = len(bits_of(lat_count)), len(bits_of(lon_count))
    split = weights.reshape((2,) * lat_places + (rows,) + (2,) * lon_places + (columns,))
    lat_dims = list(range(lat_places))[::-1]
    lon_dims = list(range(lat_places + 1, lat_places + 1 + lon_places))[::-1]
    halves = []
    for core, dims in enumerate((turned_by(lon_dims, 1), turned_by(lon_dims, 2))):
        order = lat_dims + dims + [lat_places, lat_places + 1 + lon_places]
        halves.append(split.transpose(order)[core])
    places = lat_places + lon_places
    split = jnp.stack(halves).reshape((2,) * places + (rows * columns,))
    words = -(-rows * columns // 1024) * 1024
    split = jnp.pad(split, [(0, 0)] * places + [(0, words - rows * columns)])
    return split.reshape((2,) * places + (words // 128, 128))


def shards(features, cotangent, norm_gain, norm_shift, qkv_weight, out_weight, bias_table):
    lat_count, lon_count = lax.axis_size("lat"), lax.axis_size("lon")
    token_count = ZP * features.shape[1] * features.shape[2] * lat_count * lon_count
    factor = 1.0 / math.sqrt(token_count)
    packed = (lat_count, lon_count) == (4, 8)
    f32 = jnp.float32
    shape = jax.ShapeDtypeStruct
    params = pltpu.CompilerParams(vmem_limit_bytes=48 << 20)
    half_shape = shape((3, PW, HALF_ROWS, 128), f32)
    block_shape = (WLAT, WLON, ZP, D)
    sent, own = pl.pallas_call(
        pack_kernel,
        out_shape=(pltpu.VMEM(half_shape.shape, f32),) * 2,
        in_specs=[pl.BlockSpec(memory_space=pltpu.HBM)] * 2,
        out_specs=tuple(whole(2)),
        scratch_shapes=[pltpu.VMEM(block_shape, f32), pltpu.VMEM(block_shape, f32), pltpu.SemaphoreType.DMA((2,))],
        compiler_params=params,
    )(*hbm(features.transpose(1, 2, 0, 3), cotangent.transpose(1, 2, 0, 3)))
    borrowed = lax.ppermute(sent, "lon", [(s, (s + 1) % lon_count) for s in range(lon_count)])
    projected_shape = (8, WIN, D)
    in_hbm = pl.BlockSpec(memory_space=pltpu.HBM)
    bias, gain_row, shift_row, qkv_rows, out_rows = hbm(
        bias_table[0].transpose(1, 2, 0, 3), norm_gain[None], norm_shift[None], qkv_weight, out_weight
    )
    table, projected, affine, parts = pl.pallas_call(
        prepare_kernel,
        out_shape=(
            pltpu.VMEM((PW, GROUP_ROWS * HEADS, 384), f32),
            pltpu.VMEM(projected_shape, f32),
            pltpu.VMEM((2, D), f32),
            pltpu.VMEM((4, D, D), f32),
        ),
        in_specs=[in_hbm] + whole(1) + [in_hbm] * 4,
        out_specs=tuple(whole(4)),
        scratch_shapes=[
            pltpu.VMEM((LEVELS * PADDED, PW * HEADS * LONREL), f32),
            pltpu.VMEM((PW * HEADS * PADDED, LEVELS * OFFSETS), f32),
            pltpu.VMEM((HEADS, LONREL, PW, PAIRS), f32),
            pltpu.VMEM((D, 3 * D), f32),
            pltpu.SemaphoreType.DMA((5,)),
        ],
        compiler_params=params,
    )(bias, own, gain_row, shift_row, qkv_rows, out_rows)
    grad_half = shape((3, HALF_ROWS, 128), f32)
    grad_own, grad_borrowed, weights, strips, norm = pl.pallas_call(
        functools.partial(block_kernel, factor, packed),
        out_shape=(
            grad_half,
            grad_half,
            shape((2, 2, 2, 2, 2, 40, 128) if packed else (D, 4 * D), f32),
            shape((PW * HEADS * PADDED, LEVELS * OFFSETS), f32),
            shape((8, 128), f32),
        ),
        in_specs=whole(5),
        out_specs=tuple(whole(5)),
        scratch_shapes=[pltpu.VMEM((PW * BLOCK, 384), f32), pltpu.VMEM(projected_shape, f32)],
        compiler_params=params,
    )(borrowed, projected, affine, parts, table)
    if not packed:
        weights = chunks_by_step(weights, lat_count, lon_count)
    rows_shape = shape((2, HEADS * OFFSETS, 128), f32)
    strip_grad = pl.pallas_call(
        turn_kernel,
        out_shape=rows_shape,
        in_specs=whole(1),
        out_specs=whole(1)[0],
        scratch_shapes=[pltpu.VMEM((LEVELS * PADDED, PW * HEADS * OFFSETS), f32)],
        compiler_params=params,
    )(strips)
    lat_steps, lon_steps, strip_step = summing_steps(lat_count, lon_count)
    apart = lon_steps[0][0][1]
    norm = jnp.where(lax.axis_index("lon") & apart == 0, norm, jnp.roll(norm, 4, 0))
    strip_grad, given_strip = kept_and_given(strip_grad, strip_step)
    strip_grad = strip_grad + exchanged(given_strip, strip_step)
    other_strip = None
    for step in lat_steps + lon_steps:
        kept, given = kept_and_given(weights, step)
        if step in lat_steps:
            more, more_norm = exchange_all([given, norm], step)
        else:
            if step == lon_steps[0]:
                given, grad_borrowed = lax.optimization_barrier((given, grad_borrowed))
                returned = lax.ppermute(grad_borrowed, "lon", [(s, (s - 1) % lon_count) for s in range(lon_count)])
            more, more_strip, more_norm = exchange_all([given, strip_grad, norm], step)
            if step == lon_steps[-1]:
                other_strip = more_strip
            else:
                strip_grad = strip_grad + more_strip
        weights, norm = kept + more, norm + more_norm
    grad_features = pl.pallas_call(
        unpack_kernel,
        out_shape=shape(block_shape, f32),
        in_specs=whole(2),
        out_specs=whole(1)[0],
        compiler_params=params,
    )(grad_own, returned).transpose(2, 0, 1, 3)
    chunk = weights if packed else jnp.zeros((40, 128), f32)
    parity = side(*strip_step)[None]
    grad_bias, grad_weights, grad_norm = pl.pallas_call(
        finish_kernel,
        out_shape=(shape((HEADS, LONREL, PW, PAIRS), f32), shape((48, 96), f32), shape((2, D), f32)),
        in_specs=[pl.BlockSpec(memory_space=pltpu.SMEM)] + whole(4),
        out_specs=tuple(whole(3)),
        compiler_params=params,
    )(parity, strip_grad, other_strip, chunk, norm)
    grad_bias = grad_bias.transpose(2, 0, 1, 3)[None]
    if not packed:
        rows, columns = D // lat_count, 4 * D // lon_count
        grad_weights = weights.reshape(-1)[: rows * columns].reshape(rows, columns)
    return (grad_features, grad_weights, grad_bias, grad_norm)


def solution(mesh):
    placed = (
        P(None, "lat", "lon", None),
        P(None, "lat", "lon", None),
        P(),
        P(),
        P(),
        P(),
        P("lat", None, None, None, None),
    )
    return jax.shard_map(
        shards,
        mesh=mesh,
        in_specs=placed,
        out_specs=(
            P(None, "lat", "lon", None),
            P("lat", "lon"),
            P("lat", None, None, None, None),
            P(),
        ),
        check_vma=False,
    )
```

```python
import functools
import math

import jax
import jax.numpy as jnp
from jax import lax
from jax.experimental import pallas as pl
from jax.experimental.pallas import tpu as pltpu
from jax.sharding import PartitionSpec as P

D = 192
HEADS = 6
HEAD = 32
ZP = 4
WZ = 2
WLAT = 6
WLON = 12
PW = 2
WIN = 144
LONREL = 23
PAIRS = 144
HALF = WLON // 2
LEVELS = WZ * WLAT
HALF_ROWS = HALF * LEVELS
GROUP = 4
GROUPS = WLON // GROUP
GROUP_ROWS = GROUP * LEVELS
BLOCK = HEADS * GROUP_ROWS
STRIP = LONREL * LEVELS
PADDED = 16
TURNS = (0, 1)
OFFSETS = 24

EPSILON = 1e-05
SCALE = HEAD ** (-0.5)
HIGH = lax.Precision.HIGH
FULL = lax.Precision.HIGHEST


def dot(left, right, precision=HIGH):
    return lax.dot_general(
        left, right, (((1,), (0,)), ((), ())), precision=precision, preferred_element_type=jnp.float32
    )


def dot_right_transposed(left, right, precision=HIGH):
    return lax.dot_general(
        left, right, (((1,), (1,)), ((), ())), precision=precision, preferred_element_type=jnp.float32
    )


def dot_left_transposed(left, right, precision=HIGH):
    return lax.dot_general(
        left, right, (((0,), (0,)), ((), ())), precision=precision, preferred_element_type=jnp.float32
    )


def whole(count):
    return [pl.BlockSpec(memory_space=pltpu.VMEM)] * count


def hbm(*values):
    return [pltpu.with_memory_space_constraint(value, pltpu.HBM) for value in values]


def fetched(pairs, semaphores):
    copies = [pltpu.make_async_copy(*pair, semaphores.at[place]) for place, pair in enumerate(pairs)]
    for copy in copies:
        copy.start()
    return copies


def pack_kernel(features_ref, cotangent_ref, sent_ref, own_ref, band_ref, grad_ref, semaphores):
    for copy in fetched([(features_ref, band_ref), (cotangent_ref, grad_ref)], semaphores):
        copy.wait()
    for a in range(WLAT):
        for x in range(WLON):
            target_ref = own_ref if x < HALF else sent_ref
            band = band_ref[a, x]
            grad = grad_ref[a, x]
            tiles = (band[:, :128], jnp.concatenate([band[:, 128:], grad[:, 128:]], axis=1), grad[:, :128])
            for z in range(ZP):
                c, i = divmod((z + 1) % ZP, WZ)
                row = (x % HALF) * LEVELS + i * WLAT + a
                for tile in range(3):
                    target_ref[tile, c, row : row + 1, :] = tiles[tile][z : z + 1]


def unpack_kernel(own_ref, returned_ref, out_ref):
    for a in range(WLAT):
        for x in range(WLON):
            source_ref = own_ref if x < HALF else returned_ref
            for z in range(ZP):
                c, i = divmod((z + 1) % ZP, WZ)
                row = (x % HALF) * LEVELS + i * WLAT + a
                out_ref[a, x, z : z + 1, :128] = source_ref[c, row : row + 1, :]
                out_ref[a, x, z : z + 1, 128:] = source_ref[2, row : row + 1, c * 64 : (c + 1) * 64]


def pair_order():
    row = lax.broadcasted_iota(jnp.int32, (LEVELS * PADDED, 1), 0)
    key, query = row // PADDED, row % PADDED
    place = (query // WLAT) * 72 + (key // WLAT) * 36 + (query % WLAT) * WLAT + key % WLAT
    place = jnp.where(query < LEVELS, place, -1)
    return (place == lax.broadcasted_iota(jnp.int32, (LEVELS * PADDED, PAIRS), 1)).astype(jnp.bfloat16)


def offset_order():
    row = lax.broadcasted_iota(jnp.int32, (LEVELS * OFFSETS, 1), 0)
    place = (row % OFFSETS) * LEVELS + row // OFFSETS
    columns = lax.broadcasted_iota(jnp.int32, (LEVELS * OFFSETS, LEVELS * OFFSETS), 1)
    return (place == columns).astype(jnp.bfloat16)


def parts_of(value, count):
    parts = []
    for _ in range(count):
        parts.append(value.astype(jnp.bfloat16))
        value = value - parts[-1].astype(jnp.float32)
    return parts


def moved(value, order, dims, count):
    total = None
    for part in parts_of(value, count):
        product = lax.dot_general(part, order, (dims, ((), ())), preferred_element_type=jnp.float32)
        total = product if total is None else total + product
    return total


def normalized(band):
    average = jnp.mean(band, axis=-1, keepdims=True)
    centred = band - average
    inverse = lax.rsqrt(jnp.mean(centred * centred, axis=-1, keepdims=True) + EPSILON)
    return centred * inverse, inverse


def split_tiles(half_ref):
    tiles = [half_ref[tile].reshape(WIN, 128) for tile in range(3)]
    band = jnp.concatenate([tiles[0], tiles[1][:, : D - 128]], axis=1)
    grad = jnp.concatenate([tiles[2], tiles[1][:, D - 128 :]], axis=1)
    return band, grad


def projections(half_ref, out_ref, gain, shift, weight_q, weight_k, weight_v, out_weight):
    band, grad = split_tiles(half_ref)
    unit, inverse = normalized(band)
    tokens = unit * gain + shift
    out_ref[0] = unit
    out_ref[1] = jnp.broadcast_to(inverse, unit.shape)
    out_ref[2] = tokens
    out_ref[3] = grad
    out_ref[4] = dot(tokens, weight_q, FULL) * SCALE
    out_ref[5] = dot(tokens, weight_k, FULL)
    out_ref[6] = dot(tokens, weight_v)
    out_ref[7] = dot_right_transposed(grad, out_weight)


def prepare_kernel(
    bias_hbm, own_ref, gain_hbm, shift_hbm, qkv_hbm, out_w_hbm,
    table_ref, projected_ref, affine_ref, parts_ref,
    turned_ref, strip_ref, bias_ref, qkv_ref, semaphores,
):
    copies = fetched(
        [
            (bias_hbm, bias_ref),
            (gain_hbm, affine_ref.at[0:1]),
            (shift_hbm, affine_ref.at[1:2]),
            (qkv_hbm, qkv_ref),
            (out_w_hbm, parts_ref.at[3]),
        ],
        semaphores,
    )
    pairs, offsets = pair_order(), offset_order()
    for copy in copies:
        copy.wait()
    for part in range(3):
        parts_ref[part] = qkv_ref[:, part * D : (part + 1) * D]
    projections(own_ref, projected_ref, affine_ref[0:1], affine_ref[1:2], *(parts_ref[part] for part in range(4)))
    strip_ref[...] = jnp.zeros_like(strip_ref)
    rows = jnp.concatenate([bias_ref[h, :, c, :] for c in range(PW) for h in range(HEADS)], axis=0)
    turned = None
    for part in parts_of(rows, 3):
        product = lax.dot_general(pairs, part, (((1,), (1,)), ((), ())), preferred_element_type=jnp.float32)
        turned = product if turned is None else turned + product
    turned_ref[...] = turned
    for block in range(PW * HEADS):
        for key in range(LEVELS):
            strip_ref[block * PADDED : (block + 1) * PADDED, key * OFFSETS : key * OFFSETS + LONREL] = turned_ref[
                key * PADDED : (key + 1) * PADDED, block * LONREL : (block + 1) * LONREL
            ]
    strips = moved(strip_ref[...], offsets, ((1,), (0,)), 3)
    row = lax.broadcasted_iota(jnp.int32, strips.shape, 0)
    level = (row % PADDED) // WLAT
    key_level = (lax.broadcasted_iota(jnp.int32, strips.shape, 1) % LEVELS) // WLAT
    strips = jnp.where((row >= HEADS * PADDED) | (level == key_level), strips, -jnp.inf)
    for c in range(PW):
        for h in range(HEADS):
            first = (c * HEADS + h) * PADDED
            strip = strips[first : first + LEVELS, :STRIP]
            for g in range(GROUP):
                first = h * GROUP_ROWS + g * LEVELS
                table_ref[c, first : first + LEVELS, g * LEVELS : g * LEVELS + STRIP] = strip


def turn_kernel(strip_ref, rows_ref, turned_ref):
    pairs, offsets = pair_order(), offset_order()
    by_level = moved(strip_ref[...], offsets, ((1,), (1,)), 2)
    for block in range(PW * HEADS):
        for key in range(LEVELS):
            turned_ref[key * PADDED : (key + 1) * PADDED, block * OFFSETS : (block + 1) * OFFSETS] = by_level[
                block * PADDED : (block + 1) * PADDED, key * OFFSETS : (key + 1) * OFFSETS
            ]
    rows = moved(turned_ref[...], pairs, ((0,), (0,)), 2)
    half = HEADS * OFFSETS // 2
    for y in range(2):
        first, second = rows[y * half : (y + 1) * half], rows[(y + 2) * half : (y + 3) * half]
        rows_ref[y, :half] = second[:, :128]
        rows_ref[y, half:] = jnp.concatenate(
            [second[:, 128:], first[:, :36], first[:, 108:], jnp.zeros((half, 40), jnp.float32)], axis=1
        )


def finish_kernel(parity_ref, mine_ref, other_ref, weights_ref, norm_ref, bias_ref, weights_out_ref, norm_out_ref):
    low = parity_ref[0] == 0
    mine, other = mine_ref[...], other_ref[...]
    halves = (jnp.where(low, mine, other), jnp.where(low, other, mine))
    half = HEADS * OFFSETS // 2
    for h in range(HEADS):
        first = (h % 3) * OFFSETS
        left = halves[h // 3][first : first + LONREL]
        right = halves[h // 3][half + first : half + first + LONREL]
        bias_ref[h, :, 1, :] = jnp.concatenate([left, right[:, :16]], axis=1)
        bias_ref[h, :, 0, :] = jnp.concatenate(
            [right[:, 16:52], jnp.zeros((LONREL, 72), jnp.float32), right[:, 52:88]], axis=1
        )
    weights_out_ref[...] = unpacked_chunk(weights_ref[...])
    norm = norm_ref[:4] + norm_ref[4:]
    norm_out_ref[:, :128] = norm[:2]
    norm_out_ref[0:1, 128:] = norm[2:3, :64]
    norm_out_ref[1:2, 128:] = norm[2:3, 64:]


def packed_chunk(chunk):
    beside = jnp.concatenate([chunk[40:, 32 * piece : 32 * (piece + 1)] for piece in range(3)], axis=0)
    beside = jnp.concatenate([beside, jnp.zeros((16, 32), chunk.dtype)], axis=0)
    return jnp.concatenate([chunk[:40], beside], axis=1)


def unpacked_chunk(packed):
    last = jnp.concatenate([packed[8 * piece : 8 * (piece + 1), 96:] for piece in range(3)], axis=1)
    return jnp.concatenate([packed[:, :96], last], axis=0)


ORDER = "S0 D0 S1 P0 D1 M0 V0 P1 G0 M1 V1 G1 Q0 K0 T0 Q1 K1 T1".split()


def halves_of(value):
    high = value.astype(jnp.bfloat16)
    return high, (value - high.astype(jnp.float32)).astype(jnp.bfloat16)


def product(left, right, dims):
    dims = (dims, ((), ()))

    def one(a, b):
        return lax.dot_general(a, b, dims, preferred_element_type=jnp.float32)

    return one(left[0], right[0]) + one(left[0], right[1]) + one(left[1], right[0])


def full_product(left, right, dims):
    dims = (dims, ((), ()))

    def one(a, b):
        return lax.dot_general(a, b, dims, preferred_element_type=jnp.float32)

    low = one(left[0], right[2]) + one(left[2], right[0]) + one(left[1], right[1])
    return low + one(left[0], right[1]) + one(left[1], right[0]) + one(left[0], right[0])


NORMAL = ((1,), (0,))
RIGHT = ((1,), (1,))
LEFT = ((0,), (0,))


def block_kernel(
    factor, packed,
    borrowed_ref, projected_ref, affine_ref, parts_ref, table_ref,
    grad_own_ref, grad_borrowed_ref, weights_ref, strip_grad_ref, norm_ref,
    table_grad_ref, arrived_ref,
):
    gain, shift = affine_ref[0:1], affine_ref[1:2]
    projections(borrowed_ref, arrived_ref, gain, shift, *(parts_ref[part] for part in range(4)))

    def whole_window(index, c):
        rows = slice(c * HALF_ROWS, (c + 1) * HALF_ROWS)
        return jnp.concatenate([arrived_ref[index, rows], projected_ref[index, rows]], axis=0)

    lane = lax.broadcasted_iota(jnp.int32, (1, D), 1) // HEAD
    head_masks = [(lane == h).astype(jnp.float32).astype(jnp.bfloat16) for h in range(HEADS)]
    head_of_lane = lax.broadcasted_iota(jnp.int32, (WIN, D), 1) // HEAD
    strip_grad_ref[...] = jnp.zeros_like(strip_grad_ref)
    table_grad_ref[...] = jnp.zeros_like(table_grad_ref)

    def masked(parts):
        return tuple(jnp.concatenate([part * mask for mask in head_masks], axis=0) for part in parts)

    def joined(value):
        total = value[:WIN]
        for h in range(1, HEADS):
            total = jnp.where(head_of_lane == h, value[h * WIN : (h + 1) * WIN], total)
        return total

    def score(window, c):
        window["keys"] = parts_of(whole_window(5, c), 3)
        window["queries"] = masked(parts_of(whole_window(4, c), 3))
        window["scores"] = full_product(window["queries"], window["keys"], RIGHT)

    def grad_attend(window, c):
        window["values"] = halves_of(whole_window(6, c))
        window["grads"] = masked(halves_of(whole_window(7, c)))
        window["grad_attention"] = product(window["grads"], window["values"], RIGHT)

    def softmax(window, c):
        biased = []
        for h in range(HEADS):
            for g in range(GROUPS):
                first = h * WIN + g * GROUP_ROWS
                start = (WLON - 1 - GROUP * g) * LEVELS
                bias = table_ref[c, h * GROUP_ROWS : (h + 1) * GROUP_ROWS, start : start + WIN]
                biased.append(window["scores"][first : first + GROUP_ROWS] + bias)
        scores = jnp.concatenate(biased, axis=0)
        exponent = jnp.exp(scores - jnp.max(scores, axis=-1, keepdims=True))
        window["attention"] = exponent * (1.0 / jnp.sum(exponent, axis=-1, keepdims=True))
        window["halves"] = halves_of(window["attention"])

    def mix(window, c):
        window["mixture"] = joined(product(window["halves"], window["values"], NORMAL))

    def value_grad(window, c):
        window["grad_v"] = product(window["halves"], window["grads"], LEFT)

    def score_grad(window, c):
        attention, grad_attention = window["attention"], window["grad_attention"]
        weighted = jnp.sum(attention * grad_attention, axis=-1, keepdims=True)
        window["grad_scores"] = attention * (grad_attention - weighted)
        window["score_halves"] = halves_of(window["grad_scores"])

    def query_grad(window, c):
        window["grad_q"] = joined(product(window["score_halves"], window["keys"][:2], NORMAL))

    def key_grad(window, c):
        window["grad_k"] = product(window["score_halves"], window["queries"][:2], LEFT)

    def strip_grad(window, c):
        for h in range(HEADS):
            table_rows = slice((c * HEADS + h) * GROUP_ROWS, (c * HEADS + h + 1) * GROUP_ROWS)
            for g in range(GROUPS):
                first = h * WIN + g * GROUP_ROWS
                start = (WLON - 1 - GROUP * g) * LEVELS
                table_grad_ref[table_rows, start : start + WIN] += window["grad_scores"][first : first + GROUP_ROWS]
            total = None
            for g in range(GROUP):
                first = (c * HEADS + h) * GROUP_ROWS + g * LEVELS
                part = table_grad_ref[first : first + LEVELS, g * LEVELS : g * LEVELS + STRIP]
                total = part if total is None else total + part
            first = (c * HEADS + h) * PADDED
            strip_grad_ref[first : first + LEVELS, :STRIP] = total

    windows = [{}, {}]
    stages = dict(
        S=score, P=softmax, D=grad_attend, M=mix, V=value_grad, G=score_grad, Q=query_grad, K=key_grad, T=strip_grad
    )
    for name, c in ORDER:
        stages[name](windows[int(c)], int(c))

    def rows_of(name):
        return jnp.concatenate([window[name] for window in windows], axis=0)

    grads = [halves_of(value) for value in (rows_of("grad_q") * SCALE, rows_of("grad_k"), rows_of("grad_v"))]
    tokens, window_grad, unit, inverse = (
        jnp.concatenate([whole_window(index, c) for c in range(PW)], axis=0) for index in (2, 3, 0, 1)
    )
    grad_tokens = sum(product(grads[part], halves_of(parts_ref[part]), RIGHT) for part in range(3))
    grad_unit = grad_tokens * gain
    result = window_grad + inverse * (
        grad_unit
        - jnp.mean(grad_unit, axis=-1, keepdims=True)
        - unit * jnp.mean(grad_unit * unit, axis=-1, keepdims=True)
    )
    for ref, offset in ((grad_borrowed_ref, 0), (grad_own_ref, HALF_ROWS)):
        halves = [result[c * WIN + offset : c * WIN + offset + HALF_ROWS] for c in range(PW)]
        for c in range(PW):
            ref[c] = halves[c][:, :128]
        ref[2] = jnp.concatenate([half[:, 128:] for half in halves], axis=1)
    gain_sum = jnp.sum(grad_tokens * unit, axis=0, keepdims=True) * factor
    shift_sum = jnp.sum(grad_tokens, axis=0, keepdims=True) * factor
    norm_ref[...] = jnp.zeros_like(norm_ref)
    norm_ref[:3] = jnp.concatenate(
        [gain_sum[:, :128], shift_sum[:, :128], jnp.concatenate([gain_sum[:, 128:], shift_sum[:, 128:]], axis=1)], axis=0
    )
    token_halves = halves_of(tokens * factor)
    sums = [product(token_halves, grad, LEFT) for grad in grads]
    sums.append(product(halves_of(rows_of("mixture") * factor), halves_of(window_grad), LEFT))
    for block, total in enumerate(sums):
        if not packed:
            weights_ref[:, block * D : (block + 1) * D] = total
            continue
        for y in range(2):
            for lat in range(4):
                chunk = total[48 * lat : 48 * (lat + 1), 96 * y : 96 * (y + 1)]
                place = turned_by((y, block % 2, block // 2), TURNS[lat % 2])
                weights_ref[(lat % 2, lat // 2) + place] = packed_chunk(chunk)


def bits_of(count):
    return [1 << place for place in range(count.bit_length() - 1)]


def partners(first_bits, second_bits):
    lat_count, lon_count = lax.axis_size("lat"), lax.axis_size("lon")
    pairs = []
    for lat in range(lat_count):
        for lon in range(lon_count):
            lat_bit, lon_bit = first_bits if lat % 2 == 0 else second_bits
            pairs.append((lat * lon_count + lon, (lat ^ lat_bit) * lon_count + (lon ^ lon_bit)))
    return pairs


def side(first_bits, second_bits):
    lat, lon = lax.axis_index("lat"), lax.axis_index("lon")
    first, second = ((lat & lat_bit | lon & lon_bit) != 0 for lat_bit, lon_bit in (first_bits, second_bits))
    return jnp.where(lat & 1 == 0, first, second).astype(jnp.int32)


def exchanged(value, step):
    return lax.ppermute(value, ("lat", "lon"), partners(*step))


def kept_and_given(value, step):
    high = side(*step)
    return (
        lax.dynamic_index_in_dim(value, high, 0, keepdims=False),
        lax.dynamic_index_in_dim(value, 1 - high, 0, keepdims=False),
    )


def exchange_all(values, step):
    flat = [value.reshape(-1, 128) for value in values]
    arrived = exchanged(jnp.concatenate(flat, axis=0), step)
    results, first = [], 0
    for value, rows in zip(values, flat):
        results.append(arrived[first : first + rows.shape[0]].reshape(value.shape))
        first += rows.shape[0]
    return results


def turned_by(items, count):
    return items[count:] + items[:count]


def summing_steps(lat_count, lon_count):
    lat_bits, lon_bits = bits_of(lat_count), bits_of(lon_count)
    lat_steps = [((bit, 0), (bit, 0)) for bit in lat_bits]
    lon_steps = [((0, first), (0, second)) for first, second in zip(*(turned_by(lon_bits, turn) for turn in TURNS))]
    return lat_steps, lon_steps, lon_steps[-1]


def chunks_by_step(weights, lat_count, lon_count):
    rows, columns = weights.shape[0] // lat_count, weights.shape[1] // lon_count
    lat_places, lon_places = len(bits_of(lat_count)), len(bits_of(lon_count))
    split = weights.reshape((2,) * lat_places + (rows,) + (2,) * lon_places + (columns,))
    lat_dims = list(range(lat_places))[::-1]
    lon_dims = list(range(lat_places + 1, lat_places + 1 + lon_places))[::-1]
    halves = []
    for core, dims in enumerate(turned_by(lon_dims, turn) for turn in TURNS):
        order = lat_dims + dims + [lat_places, lat_places + 1 + lon_places]
        halves.append(split.transpose(order)[core])
    places = lat_places + lon_places
    split = jnp.stack(halves).reshape((2,) * places + (rows * columns,))
    words = -(-rows * columns // 1024) * 1024
    split = jnp.pad(split, [(0, 0)] * places + [(0, words - rows * columns)])
    return split.reshape((2,) * places + (words // 128, 128))


def shards(features, cotangent, norm_gain, norm_shift, qkv_weight, out_weight, bias_table):
    lat_count, lon_count = lax.axis_size("lat"), lax.axis_size("lon")
    token_count = ZP * features.shape[1] * features.shape[2] * lat_count * lon_count
    factor = 1.0 / math.sqrt(token_count)
    packed = (lat_count, lon_count) == (4, 8)
    f32 = jnp.float32
    shape = jax.ShapeDtypeStruct
    params = pltpu.CompilerParams(vmem_limit_bytes=48 << 20)
    half_shape = shape((3, PW, HALF_ROWS, 128), f32)
    block_shape = (WLAT, WLON, ZP, D)
    sent, own = pl.pallas_call(
        pack_kernel,
        out_shape=(pltpu.VMEM(half_shape.shape, f32),) * 2,
        in_specs=[pl.BlockSpec(memory_space=pltpu.HBM)] * 2,
        out_specs=tuple(whole(2)),
        scratch_shapes=[pltpu.VMEM(block_shape, f32), pltpu.VMEM(block_shape, f32), pltpu.SemaphoreType.DMA((2,))],
        compiler_params=params,
    )(*hbm(features.transpose(1, 2, 0, 3), cotangent.transpose(1, 2, 0, 3)))
    borrowed = lax.ppermute(sent, "lon", [(s, (s + 1) % lon_count) for s in range(lon_count)])
    projected_shape = (8, WIN, D)
    in_hbm = pl.BlockSpec(memory_space=pltpu.HBM)
    bias, gain_row, shift_row, qkv_rows, out_rows = hbm(
        bias_table[0].transpose(1, 2, 0, 3), norm_gain[None], norm_shift[None], qkv_weight, out_weight
    )
    table, projected, affine, parts = pl.pallas_call(
        prepare_kernel,
        out_shape=(
            pltpu.VMEM((PW, GROUP_ROWS * HEADS, 384), f32),
            pltpu.VMEM(projected_shape, f32),
            pltpu.VMEM((2, D), f32),
            pltpu.VMEM((4, D, D), f32),
        ),
        in_specs=[in_hbm] + whole(1) + [in_hbm] * 4,
        out_specs=tuple(whole(4)),
        scratch_shapes=[
            pltpu.VMEM((LEVELS * PADDED, PW * HEADS * LONREL), f32),
            pltpu.VMEM((PW * HEADS * PADDED, LEVELS * OFFSETS), f32),
            pltpu.VMEM((HEADS, LONREL, PW, PAIRS), f32),
            pltpu.VMEM((D, 3 * D), f32),
            pltpu.SemaphoreType.DMA((5,)),
        ],
        compiler_params=params,
    )(bias, own, gain_row, shift_row, qkv_rows, out_rows)
    grad_half = shape((3, HALF_ROWS, 128), f32)
    grad_own, grad_borrowed, weights, strips, norm = pl.pallas_call(
        functools.partial(block_kernel, factor, packed),
        out_shape=(
            grad_half,
            grad_half,
            shape((2, 2, 2, 2, 2, 40, 128) if packed else (D, 4 * D), f32),
            shape((PW * HEADS * PADDED, LEVELS * OFFSETS), f32),
            shape((8, 128), f32),
        ),
        in_specs=whole(5),
        out_specs=tuple(whole(5)),
        scratch_shapes=[pltpu.VMEM((PW * BLOCK, 384), f32), pltpu.VMEM(projected_shape, f32)],
        compiler_params=params,
    )(borrowed, projected, affine, parts, table)
    if not packed:
        weights = chunks_by_step(weights, lat_count, lon_count)
    rows_shape = shape((2, HEADS * OFFSETS, 128), f32)
    strip_grad = pl.pallas_call(
        turn_kernel,
        out_shape=rows_shape,
        in_specs=whole(1),
        out_specs=whole(1)[0],
        scratch_shapes=[pltpu.VMEM((LEVELS * PADDED, PW * HEADS * OFFSETS), f32)],
        compiler_params=params,
    )(strips)
    lat_steps, lon_steps, strip_step = summing_steps(lat_count, lon_count)
    apart = lon_steps[0][0][1] if (TURNS[1] - TURNS[0]) % len(lon_steps) == 1 else lon_steps[0][1][1]
    norm = jnp.where(lax.axis_index("lon") & apart == 0, norm, jnp.roll(norm, 4, 0))
    strip_grad, given_strip = kept_and_given(strip_grad, strip_step)
    strip_grad = strip_grad + exchanged(given_strip, strip_step)
    other_strip = None
    for step in lat_steps + lon_steps:
        kept, given = kept_and_given(weights, step)
        if step in lat_steps:
            more, more_norm = exchange_all([given, norm], step)
        else:
            if step == lon_steps[0]:
                given, grad_borrowed = lax.optimization_barrier((given, grad_borrowed))
                returned = lax.ppermute(grad_borrowed, "lon", [(s, (s - 1) % lon_count) for s in range(lon_count)])
            more, more_strip, more_norm = exchange_all([given, strip_grad, norm], step)
            if step == lon_steps[-1]:
                other_strip = more_strip
            else:
                strip_grad = strip_grad + more_strip
        weights, norm = kept + more, norm + more_norm
    grad_features = pl.pallas_call(
        unpack_kernel,
        out_shape=shape(block_shape, f32),
        in_specs=whole(2),
        out_specs=whole(1)[0],
        compiler_params=params,
    )(grad_own, returned).transpose(2, 0, 1, 3)
    chunk = weights if packed else jnp.zeros((40, 128), f32)
    parity = side(*strip_step)[None]
    grad_bias, grad_weights, grad_norm = pl.pallas_call(
        finish_kernel,
        out_shape=(shape((HEADS, LONREL, PW, PAIRS), f32), shape((48, 96), f32), shape((2, D), f32)),
        in_specs=[pl.BlockSpec(memory_space=pltpu.SMEM)] + whole(4),
        out_specs=tuple(whole(3)),
        compiler_params=params,
    )(parity, strip_grad, other_strip, chunk, norm)
    grad_bias = grad_bias.transpose(2, 0, 1, 3)[None]
    if not packed:
        rows, columns = D // lat_count, 4 * D // lon_count
        grad_weights = weights.reshape(-1)[: rows * columns].reshape(rows, columns)
    return (grad_features, grad_weights, grad_bias, grad_norm)


def solution(mesh):
    placed = (
        P(None, "lat", "lon", None),
        P(None, "lat", "lon", None),
        P(),
        P(),
        P(),
        P(),
        P("lat", None, None, None, None),
    )
    return jax.shard_map(
        shards,
        mesh=mesh,
        in_specs=placed,
        out_specs=(
            P(None, "lat", "lon", None),
            P("lat", "lon"),
            P("lat", None, None, None, None),
            P(),
        ),
        check_vma=False,
    )
```

```python
import functools
import math

import jax
import jax.numpy as jnp
from jax import lax
from jax.experimental import pallas as pl
from jax.experimental.pallas import tpu as pltpu
from jax.sharding import PartitionSpec as P

D = 192
HEADS = 6
HEAD = 32
ZP = 4
WZ = 2
WLAT = 6
WLON = 12
PW = 2
WIN = 144
LONREL = 23
PAIRS = 144
HALF = WLON // 2
LEVELS = WZ * WLAT
HALF_ROWS = HALF * LEVELS
GROUP = 4
GROUPS = WLON // GROUP
GROUP_ROWS = GROUP * LEVELS
BLOCK = HEADS * GROUP_ROWS
STRIP = LONREL * LEVELS
PADDED = 16
TURN = 0
OFFSETS = 24

EPSILON = 1e-05
SCALE = HEAD ** (-0.5)
HIGH = lax.Precision.HIGH
FULL = lax.Precision.HIGHEST


def dot(left, right, precision=HIGH):
    return lax.dot_general(
        left, right, (((1,), (0,)), ((), ())), precision=precision, preferred_element_type=jnp.float32
    )


def dot_right_transposed(left, right, precision=HIGH):
    return lax.dot_general(
        left, right, (((1,), (1,)), ((), ())), precision=precision, preferred_element_type=jnp.float32
    )


def dot_left_transposed(left, right, precision=HIGH):
    return lax.dot_general(
        left, right, (((0,), (0,)), ((), ())), precision=precision, preferred_element_type=jnp.float32
    )


def whole(count):
    return [pl.BlockSpec(memory_space=pltpu.VMEM)] * count


def hbm(*values):
    return [pltpu.with_memory_space_constraint(value, pltpu.HBM) for value in values]


def fetched(pairs, semaphores):
    copies = [pltpu.make_async_copy(*pair, semaphores.at[place]) for place, pair in enumerate(pairs)]
    for copy in copies:
        copy.start()
    return copies


def pack_half(band_ref, grad_ref, target_ref):
    for a in range(WLAT):
        for x in range(HALF):
            band = band_ref[a, x]
            grad = grad_ref[a, x]
            tiles = (band[:, :128], jnp.concatenate([band[:, 128:], grad[:, 128:]], axis=1), grad[:, :128])
            for z in range(ZP):
                c, i = divmod((z + 1) % ZP, WZ)
                row = x * LEVELS + i * WLAT + a
                for tile in range(3):
                    target_ref[tile, c, row : row + 1, :] = tiles[tile][z : z + 1]


def pack_kernel(features_ref, cotangent_ref, sent_ref, band_ref, grad_ref, semaphores):
    pairs = [(features_ref.at[:, HALF:], band_ref), (cotangent_ref.at[:, HALF:], grad_ref)]
    for copy in fetched(pairs, semaphores):
        copy.wait()
    pack_half(band_ref, grad_ref, sent_ref)


def unpack_kernel(own_ref, returned_ref, out_ref):
    for a in range(WLAT):
        for x in range(WLON):
            source_ref = own_ref if x < HALF else returned_ref
            for z in range(ZP):
                c, i = divmod((z + 1) % ZP, WZ)
                row = (x % HALF) * LEVELS + i * WLAT + a
                out_ref[a, x, z : z + 1, :128] = source_ref[c, row : row + 1, :]
                out_ref[a, x, z : z + 1, 128:] = source_ref[2, row : row + 1, c * 64 : (c + 1) * 64]


def pair_order():
    row = lax.broadcasted_iota(jnp.int32, (LEVELS * PADDED, 1), 0)
    key, query = row // PADDED, row % PADDED
    place = (query // WLAT) * 72 + (key // WLAT) * 36 + (query % WLAT) * WLAT + key % WLAT
    place = jnp.where(query < LEVELS, place, -1)
    return (place == lax.broadcasted_iota(jnp.int32, (LEVELS * PADDED, PAIRS), 1)).astype(jnp.bfloat16)


def offset_order():
    row = lax.broadcasted_iota(jnp.int32, (LEVELS * OFFSETS, 1), 0)
    place = (row % OFFSETS) * LEVELS + row // OFFSETS
    columns = lax.broadcasted_iota(jnp.int32, (LEVELS * OFFSETS, LEVELS * OFFSETS), 1)
    return (place == columns).astype(jnp.bfloat16)


def parts_of(value, count):
    parts = []
    for _ in range(count):
        parts.append(value.astype(jnp.bfloat16))
        value = value - parts[-1].astype(jnp.float32)
    return parts


def moved(value, order, dims, count):
    total = None
    for part in parts_of(value, count):
        product = lax.dot_general(part, order, (dims, ((), ())), preferred_element_type=jnp.float32)
        total = product if total is None else total + product
    return total


def normalized(band):
    average = jnp.mean(band, axis=-1, keepdims=True)
    centred = band - average
    inverse = lax.rsqrt(jnp.mean(centred * centred, axis=-1, keepdims=True) + EPSILON)
    return centred * inverse, inverse


def split_tiles(half_ref):
    tiles = [half_ref[tile].reshape(WIN, 128) for tile in range(3)]
    band = jnp.concatenate([tiles[0], tiles[1][:, : D - 128]], axis=1)
    grad = jnp.concatenate([tiles[2], tiles[1][:, D - 128 :]], axis=1)
    return band, grad


def projections(half_ref, out_ref, gain, shift, weight_q, weight_k, weight_v, out_weight):
    band, grad = split_tiles(half_ref)
    unit, inverse = normalized(band)
    tokens = unit * gain + shift
    out_ref[0] = unit
    out_ref[1] = jnp.broadcast_to(inverse, unit.shape)
    out_ref[2] = tokens
    out_ref[3] = grad
    out_ref[4] = dot(tokens, weight_q, FULL) * SCALE
    out_ref[5] = dot(tokens, weight_k, FULL)
    out_ref[6] = dot(tokens, weight_v)
    out_ref[7] = dot_right_transposed(grad, out_weight)


def prepare_kernel(
    bias_hbm, features_hbm, cotangent_hbm, gain_hbm, shift_hbm, qkv_hbm, out_w_hbm,
    table_ref, projected_ref, affine_ref, parts_ref,
    turned_ref, strip_ref, bias_ref, qkv_ref, band_ref, grad_ref, own_ref, semaphores,
):
    copies = fetched(
        [
            (bias_hbm, bias_ref),
            (features_hbm.at[:, :HALF], band_ref),
            (cotangent_hbm.at[:, :HALF], grad_ref),
            (gain_hbm, affine_ref.at[0:1]),
            (shift_hbm, affine_ref.at[1:2]),
            (qkv_hbm, qkv_ref),
            (out_w_hbm, parts_ref.at[3]),
        ],
        semaphores,
    )
    pairs, offsets = pair_order(), offset_order()
    for copy in copies:
        copy.wait()
    pack_half(band_ref, grad_ref, own_ref)
    for part in range(3):
        parts_ref[part] = qkv_ref[:, part * D : (part + 1) * D]
    projections(own_ref, projected_ref, affine_ref[0:1], affine_ref[1:2], *(parts_ref[part] for part in range(4)))
    spare = jnp.zeros((OFFSETS - LONREL, PAIRS), jnp.float32)
    rows = jnp.concatenate(
        [part for c in range(PW) for h in range(HEADS) for part in (bias_ref[h, :, c, :], spare)], axis=0
    )
    turned = None
    for part in parts_of(rows, 3):
        product = lax.dot_general(pairs, part, (((1,), (1,)), ((), ())), preferred_element_type=jnp.float32)
        turned = product if turned is None else turned + product
    turned_ref[...] = turned
    for block in range(PW * HEADS):
        for key in range(LEVELS):
            strip_ref[block * PADDED : (block + 1) * PADDED, key * OFFSETS : (key + 1) * OFFSETS] = turned_ref[
                key * PADDED : (key + 1) * PADDED, block * OFFSETS : (block + 1) * OFFSETS
            ]
    strips = moved(strip_ref[...], offsets, ((1,), (0,)), 3)
    row = lax.broadcasted_iota(jnp.int32, strips.shape, 0)
    level = (row % PADDED) // WLAT
    key_level = (lax.broadcasted_iota(jnp.int32, strips.shape, 1) % LEVELS) // WLAT
    strips = jnp.where((row >= HEADS * PADDED) | (level == key_level), strips, -jnp.inf)
    for c in range(PW):
        for h in range(HEADS):
            first = (c * HEADS + h) * PADDED
            strip = strips[first : first + LEVELS, :STRIP]
            for g in range(GROUP):
                first = h * GROUP_ROWS + g * LEVELS
                table_ref[c, first : first + LEVELS, g * LEVELS : g * LEVELS + STRIP] = strip


def turn_kernel(strip_ref, rows_ref, turned_ref):
    pairs, offsets = pair_order(), offset_order()
    by_level = moved(strip_ref[...], offsets, ((1,), (1,)), 2)
    for block in range(PW * HEADS):
        for key in range(LEVELS):
            turned_ref[key * PADDED : (key + 1) * PADDED, block * OFFSETS : (block + 1) * OFFSETS] = by_level[
                block * PADDED : (block + 1) * PADDED, key * OFFSETS : (key + 1) * OFFSETS
            ]
    rows = moved(turned_ref[...], pairs, ((0,), (0,)), 2)
    half = HEADS * OFFSETS // 2
    for y in range(2):
        first, second = rows[y * half : (y + 1) * half], rows[(y + 2) * half : (y + 3) * half]
        rows_ref[y, :half] = second[:, :128]
        rows_ref[y, half:] = jnp.concatenate(
            [second[:, 128:], first[:, :36], first[:, 108:], jnp.zeros((half, 40), jnp.float32)], axis=1
        )


def finish_kernel(parity_ref, mine_ref, other_ref, weights_ref, norm_ref, bias_ref, weights_out_ref, norm_out_ref):
    low = parity_ref[0] == 0
    mine, other = mine_ref[...], other_ref[...]
    halves = (jnp.where(low, mine, other), jnp.where(low, other, mine))
    half = HEADS * OFFSETS // 2
    for h in range(HEADS):
        first = (h % 3) * OFFSETS
        left = halves[h // 3][first : first + LONREL]
        right = halves[h // 3][half + first : half + first + LONREL]
        bias_ref[h, :, 1, :] = jnp.concatenate([left, right[:, :16]], axis=1)
        bias_ref[h, :, 0, :] = jnp.concatenate(
            [right[:, 16:52], jnp.zeros((LONREL, 72), jnp.float32), right[:, 52:88]], axis=1
        )
    weights_out_ref[...] = unpacked_chunk(weights_ref[...])
    norm = norm_ref[:4] + norm_ref[4:]
    norm_out_ref[:, :128] = norm[:2]
    norm_out_ref[0:1, 128:] = norm[2:3, :64]
    norm_out_ref[1:2, 128:] = norm[2:3, 64:]


def packed_chunk(chunk):
    beside = jnp.concatenate([chunk[40:, 32 * piece : 32 * (piece + 1)] for piece in range(3)], axis=0)
    beside = jnp.concatenate([beside, jnp.zeros((16, 32), chunk.dtype)], axis=0)
    return jnp.concatenate([chunk[:40], beside], axis=1)


def unpacked_chunk(packed):
    last = jnp.concatenate([packed[8 * piece : 8 * (piece + 1), 96:] for piece in range(3)], axis=1)
    return jnp.concatenate([packed[:, :96], last], axis=0)


ORDER = "S0 D0 S1 P0 D1 M0 V0 P1 G0 M1 V1 G1 Q0 K0 T0 Q1 K1 T1".split()


def halves_of(value):
    high = value.astype(jnp.bfloat16)
    return high, (value - high.astype(jnp.float32)).astype(jnp.bfloat16)


def product(left, right, dims):
    dims = (dims, ((), ()))

    def one(a, b):
        return lax.dot_general(a, b, dims, preferred_element_type=jnp.float32)

    return one(left[0], right[0]) + one(left[0], right[1]) + one(left[1], right[0])


def full_product(left, right, dims):
    dims = (dims, ((), ()))

    def one(a, b):
        return lax.dot_general(a, b, dims, preferred_element_type=jnp.float32)

    low = one(left[0], right[2]) + one(left[2], right[0]) + one(left[1], right[1])
    return low + one(left[0], right[1]) + one(left[1], right[0]) + one(left[0], right[0])


NORMAL = ((1,), (0,))
RIGHT = ((1,), (1,))
LEFT = ((0,), (0,))


def block_kernel(
    factor, packed,
    borrowed_ref, projected_ref, affine_ref, parts_ref, table_ref,
    grad_own_ref, grad_borrowed_ref, weights_ref, strip_grad_ref, norm_ref,
    table_grad_ref, arrived_ref,
):
    gain, shift = affine_ref[0:1], affine_ref[1:2]
    projections(borrowed_ref, arrived_ref, gain, shift, *(parts_ref[part] for part in range(4)))

    def whole_window(index, c):
        rows = slice(c * HALF_ROWS, (c + 1) * HALF_ROWS)
        return jnp.concatenate([arrived_ref[index, rows], projected_ref[index, rows]], axis=0)

    lane = lax.broadcasted_iota(jnp.int32, (1, D), 1) // HEAD
    head_masks = [(lane == h).astype(jnp.float32).astype(jnp.bfloat16) for h in range(HEADS)]
    head_of_lane = lax.broadcasted_iota(jnp.int32, (WIN, D), 1) // HEAD
    strip_grad_ref[...] = jnp.zeros_like(strip_grad_ref)
    table_grad_ref[...] = jnp.zeros_like(table_grad_ref)

    def masked(parts):
        return tuple(jnp.concatenate([part * mask for mask in head_masks], axis=0) for part in parts)

    def joined(value):
        total = value[:WIN]
        for h in range(1, HEADS):
            total = jnp.where(head_of_lane == h, value[h * WIN : (h + 1) * WIN], total)
        return total

    def score(window, c):
        window["keys"] = parts_of(whole_window(5, c), 3)
        window["queries"] = masked(parts_of(whole_window(4, c), 3))
        window["scores"] = full_product(window["queries"], window["keys"], RIGHT)

    def grad_attend(window, c):
        window["values"] = halves_of(whole_window(6, c))
        window["grads"] = masked(halves_of(whole_window(7, c)))
        window["grad_attention"] = product(window["grads"], window["values"], RIGHT)

    def softmax(window, c):
        biased = []
        for h in range(HEADS):
            for g in range(GROUPS):
                first = h * WIN + g * GROUP_ROWS
                start = (WLON - 1 - GROUP * g) * LEVELS
                bias = table_ref[c, h * GROUP_ROWS : (h + 1) * GROUP_ROWS, start : start + WIN]
                biased.append(window["scores"][first : first + GROUP_ROWS] + bias)
        scores = jnp.concatenate(biased, axis=0)
        exponent = jnp.exp(scores - jnp.max(scores, axis=-1, keepdims=True))
        window["attention"] = exponent * (1.0 / jnp.sum(exponent, axis=-1, keepdims=True))
        window["halves"] = halves_of(window["attention"])

    def mix(window, c):
        window["mixture"] = joined(product(window["halves"], window["values"], NORMAL))

    def value_grad(window, c):
        window["grad_v"] = product(window["halves"], window["grads"], LEFT)

    def score_grad(window, c):
        attention, grad_attention = window["attention"], window["grad_attention"]
        weighted = jnp.sum(attention * grad_attention, axis=-1, keepdims=True)
        window["grad_scores"] = attention * (grad_attention - weighted)
        window["score_halves"] = halves_of(window["grad_scores"])

    def query_grad(window, c):
        window["grad_q"] = joined(product(window["score_halves"], window["keys"][:2], NORMAL))

    def key_grad(window, c):
        window["grad_k"] = product(window["score_halves"], window["queries"][:2], LEFT)

    def strip_grad(window, c):
        for h in range(HEADS):
            table_rows = slice((c * HEADS + h) * GROUP_ROWS, (c * HEADS + h + 1) * GROUP_ROWS)
            for g in range(GROUPS):
                first = h * WIN + g * GROUP_ROWS
                start = (WLON - 1 - GROUP * g) * LEVELS
                table_grad_ref[table_rows, start : start + WIN] += window["grad_scores"][first : first + GROUP_ROWS]
            total = None
            for g in range(GROUP):
                first = (c * HEADS + h) * GROUP_ROWS + g * LEVELS
                part = table_grad_ref[first : first + LEVELS, g * LEVELS : g * LEVELS + STRIP]
                total = part if total is None else total + part
            first = (c * HEADS + h) * PADDED
            strip_grad_ref[first : first + LEVELS, :STRIP] = total

    windows = [{}, {}]
    stages = dict(
        S=score, P=softmax, D=grad_attend, M=mix, V=value_grad, G=score_grad, Q=query_grad, K=key_grad, T=strip_grad
    )
    for name, c in ORDER:
        stages[name](windows[int(c)], int(c))

    def rows_of(name):
        return jnp.concatenate([window[name] for window in windows], axis=0)

    grads = [halves_of(value) for value in (rows_of("grad_q") * SCALE, rows_of("grad_k"), rows_of("grad_v"))]
    tokens, window_grad, unit, inverse = (
        jnp.concatenate([whole_window(index, c) for c in range(PW)], axis=0) for index in (2, 3, 0, 1)
    )
    grad_tokens = sum(product(grads[part], halves_of(parts_ref[part]), RIGHT) for part in range(3))
    grad_unit = grad_tokens * gain
    result = window_grad + inverse * (
        grad_unit
        - jnp.mean(grad_unit, axis=-1, keepdims=True)
        - unit * jnp.mean(grad_unit * unit, axis=-1, keepdims=True)
    )
    for ref, offset in ((grad_borrowed_ref, 0), (grad_own_ref, HALF_ROWS)):
        halves = [result[c * WIN + offset : c * WIN + offset + HALF_ROWS] for c in range(PW)]
        for c in range(PW):
            ref[c] = halves[c][:, :128]
        ref[2] = jnp.concatenate([half[:, 128:] for half in halves], axis=1)
    gain_sum = jnp.sum(grad_tokens * unit, axis=0, keepdims=True) * factor
    shift_sum = jnp.sum(grad_tokens, axis=0, keepdims=True) * factor
    norm_ref[...] = jnp.zeros_like(norm_ref)
    norm_ref[:3] = jnp.concatenate(
        [gain_sum[:, :128], shift_sum[:, :128], jnp.concatenate([gain_sum[:, 128:], shift_sum[:, 128:]], axis=1)], axis=0
    )
    token_halves = halves_of(tokens * factor)
    sums = [product(token_halves, grad, LEFT) for grad in grads]
    sums.append(product(halves_of(rows_of("mixture") * factor), halves_of(window_grad), LEFT))
    for block, total in enumerate(sums):
        if not packed:
            weights_ref[:, block * D : (block + 1) * D] = total
            continue
        for y in range(2):
            for lat in range(4):
                chunk = total[48 * lat : 48 * (lat + 1), 96 * y : 96 * (y + 1)]
                place = turned_by((y, block % 2, block // 2), TURN)
                place = (lat // 2,) + place if lat % 2 == 0 else place + (lat // 2,)
                weights_ref[(lat % 2,) + place] = packed_chunk(chunk)


def bits_of(count):
    return [1 << place for place in range(count.bit_length() - 1)]


def partners(first_bits, second_bits):
    lat_count, lon_count = lax.axis_size("lat"), lax.axis_size("lon")
    pairs = []
    for lat in range(lat_count):
        for lon in range(lon_count):
            lat_bit, lon_bit = first_bits if lat % 2 == 0 else second_bits
            pairs.append((lat * lon_count + lon, (lat ^ lat_bit) * lon_count + (lon ^ lon_bit)))
    return pairs


def side(first_bits, second_bits):
    lat, lon = lax.axis_index("lat"), lax.axis_index("lon")
    first, second = ((lat & lat_bit | lon & lon_bit) != 0 for lat_bit, lon_bit in (first_bits, second_bits))
    return jnp.where(lat & 1 == 0, first, second).astype(jnp.int32)


def exchanged(value, step):
    return lax.ppermute(value, ("lat", "lon"), partners(*step))


def kept_and_given(value, step):
    high = side(*step)
    return (
        lax.dynamic_index_in_dim(value, high, 0, keepdims=False),
        lax.dynamic_index_in_dim(value, 1 - high, 0, keepdims=False),
    )


def exchange_all(values, step):
    flat = [value.reshape(-1, 128) for value in values]
    arrived = exchanged(jnp.concatenate(flat, axis=0), step)
    results, first = [], 0
    for value, rows in zip(values, flat):
        results.append(arrived[first : first + rows.shape[0]].reshape(value.shape))
        first += rows.shape[0]
    return results


def turned_by(items, count):
    return items[count:] + items[:count]


def summing_steps(lat_count, lon_count):
    lat_bits, lon_bits = bits_of(lat_count), turned_by(bits_of(lon_count), TURN)
    core, second, *others = [(bit, 0) for bit in lat_bits]
    lons = [(0, bit) for bit in lon_bits]
    first_order = [second] + others + lons
    second_order = lons[:1] + others + lons[1:] + [second]
    return (core, core), list(zip(first_order, second_order)), (lons[-1], lons[0])


def chunks_by_step(weights, lat_count, lon_count):
    rows, columns = weights.shape[0] // lat_count, weights.shape[1] // lon_count
    lat_places, lon_places = len(bits_of(lat_count)), len(bits_of(lon_count))
    split = weights.reshape((2,) * lat_places + (rows,) + (2,) * lon_places + (columns,))
    core, second, *others = list(range(lat_places))[::-1]
    lons = turned_by(list(range(lat_places + 1, lat_places + 1 + lon_places))[::-1], TURN)
    halves = []
    for place, dims in enumerate(([second] + others + lons, lons[:1] + others + lons[1:] + [second])):
        order = [core] + dims + [lat_places, lat_places + 1 + lon_places]
        halves.append(split.transpose(order)[place])
    places = lat_places + lon_places
    split = jnp.stack(halves).reshape((2,) * places + (rows * columns,))
    words = -(-rows * columns // 1024) * 1024
    split = jnp.pad(split, [(0, 0)] * places + [(0, words - rows * columns)])
    return split.reshape((2,) * places + (words // 128, 128))


def shards(features, cotangent, norm_gain, norm_shift, qkv_weight, out_weight, bias_table):
    lat_count, lon_count = lax.axis_size("lat"), lax.axis_size("lon")
    token_count = ZP * features.shape[1] * features.shape[2] * lat_count * lon_count
    factor = 1.0 / math.sqrt(token_count)
    packed = (lat_count, lon_count) == (4, 8)
    f32 = jnp.float32
    shape = jax.ShapeDtypeStruct
    params = pltpu.CompilerParams(vmem_limit_bytes=48 << 20)
    half_shape = shape((3, PW, HALF_ROWS, 128), f32)
    block_shape = (WLAT, WLON, ZP, D)
    features, cotangent = hbm(features.transpose(1, 2, 0, 3), cotangent.transpose(1, 2, 0, 3))
    half_block = pltpu.VMEM((WLAT, HALF, ZP, D), f32)
    sent = pl.pallas_call(
        pack_kernel,
        out_shape=pltpu.VMEM(half_shape.shape, f32),
        in_specs=[pl.BlockSpec(memory_space=pltpu.HBM)] * 2,
        out_specs=whole(1)[0],
        scratch_shapes=[half_block, half_block, pltpu.SemaphoreType.DMA((2,))],
        compiler_params=params,
    )(features, cotangent)
    borrowed = lax.ppermute(sent, "lon", [(s, (s + 1) % lon_count) for s in range(lon_count)])
    projected_shape = (8, WIN, D)
    in_hbm = pl.BlockSpec(memory_space=pltpu.HBM)
    bias, gain_row, shift_row, qkv_rows, out_rows = hbm(
        bias_table[0].transpose(1, 2, 0, 3), norm_gain[None], norm_shift[None], qkv_weight, out_weight
    )
    table, projected, affine, parts = pl.pallas_call(
        prepare_kernel,
        out_shape=(
            pltpu.VMEM((PW, GROUP_ROWS * HEADS, 384), f32),
            pltpu.VMEM(projected_shape, f32),
            pltpu.VMEM((2, D), f32),
            pltpu.VMEM((4, D, D), f32),
        ),
        in_specs=[in_hbm] * 7,
        out_specs=tuple(whole(4)),
        scratch_shapes=[
            pltpu.VMEM((LEVELS * PADDED, PW * HEADS * OFFSETS), f32),
            pltpu.VMEM((PW * HEADS * PADDED, LEVELS * OFFSETS), f32),
            pltpu.VMEM((HEADS, LONREL, PW, PAIRS), f32),
            pltpu.VMEM((D, 3 * D), f32),
            half_block,
            half_block,
            pltpu.VMEM(half_shape.shape, f32),
            pltpu.SemaphoreType.DMA((7,)),
        ],
        compiler_params=params,
    )(bias, features, cotangent, gain_row, shift_row, qkv_rows, out_rows)
    grad_half = shape((3, HALF_ROWS, 128), f32)
    grad_own, grad_borrowed, weights, strips, norm = pl.pallas_call(
        functools.partial(block_kernel, factor, packed),
        out_shape=(
            grad_half,
            grad_half,
            shape((2, 2, 2, 2, 2, 40, 128) if packed else (D, 4 * D), f32),
            shape((PW * HEADS * PADDED, LEVELS * OFFSETS), f32),
            shape((8, 128), f32),
        ),
        in_specs=whole(5),
        out_specs=tuple(whole(5)),
        scratch_shapes=[pltpu.VMEM((PW * BLOCK, 384), f32), pltpu.VMEM(projected_shape, f32)],
        compiler_params=params,
    )(borrowed, projected, affine, parts, table)
    if not packed:
        weights = chunks_by_step(weights, lat_count, lon_count)
    rows_shape = shape((2, HEADS * OFFSETS, 128), f32)
    strip_grad = pl.pallas_call(
        turn_kernel,
        out_shape=rows_shape,
        in_specs=whole(1),
        out_specs=whole(1)[0],
        scratch_shapes=[pltpu.VMEM((LEVELS * PADDED, PW * HEADS * OFFSETS), f32)],
        compiler_params=params,
    )(strips)
    core_step, steps, strip_step = summing_steps(lat_count, lon_count)
    norm = jnp.where(lax.axis_index("lat") & 2 == 0, norm, jnp.roll(norm, 4, 0))
    strip_grad, given_strip = kept_and_given(strip_grad, strip_step)
    strip_grad = strip_grad + exchanged(given_strip, strip_step)
    shared = steps[-(len(bits_of(lon_count)) - 1) - 1 : -1]
    for step in [core_step] + steps[:-1]:
        kept, given = kept_and_given(weights, step)
        if step in shared:
            if step == shared[0]:
                returned = lax.ppermute(grad_borrowed, "lon", [(s, (s - 1) % lon_count) for s in range(lon_count)])
            more, more_strip, more_norm = exchange_all([given, strip_grad, norm], step)
            strip_grad = strip_grad + more_strip
        else:
            more, more_norm = exchange_all([given, norm], step)
        weights, norm = kept + more, norm + more_norm
    other_strip = exchanged(strip_grad, strip_step)
    kept, given = kept_and_given(weights, steps[-1])
    more, more_norm = exchange_all([given, norm], steps[-1])
    more, returned = lax.optimization_barrier((more, returned))
    weights, norm = kept + more, norm + more_norm
    grad_features = pl.pallas_call(
        unpack_kernel,
        out_shape=shape(block_shape, f32),
        in_specs=whole(2),
        out_specs=whole(1)[0],
        compiler_params=params,
    )(grad_own, returned).transpose(2, 0, 1, 3)
    chunk = weights if packed else jnp.zeros((40, 128), f32)
    parity = side(*strip_step)[None]
    grad_bias, grad_weights, grad_norm = pl.pallas_call(
        finish_kernel,
        out_shape=(shape((HEADS, LONREL, PW, PAIRS), f32), shape((48, 96), f32), shape((2, D), f32)),
        in_specs=[pl.BlockSpec(memory_space=pltpu.SMEM)] + whole(4),
        out_specs=tuple(whole(3)),
        compiler_params=params,
    )(parity, strip_grad, other_strip, chunk, norm)
    grad_bias = grad_bias.transpose(2, 0, 1, 3)[None]
    if not packed:
        rows, columns = D // lat_count, 4 * D // lon_count
        grad_weights = weights.reshape(-1)[: rows * columns].reshape(rows, columns)
    return (grad_features, grad_weights, grad_bias, grad_norm)


def solution(mesh):
    placed = (
        P(None, "lat", "lon", None),
        P(None, "lat", "lon", None),
        P(),
        P(),
        P(),
        P(),
        P("lat", None, None, None, None),
    )
    return jax.shard_map(
        shards,
        mesh=mesh,
        in_specs=placed,
        out_specs=(
            P(None, "lat", "lon", None),
            P("lat", "lon"),
            P("lat", None, None, None, None),
            P(),
        ),
        check_vma=False,
    )
```

```python
import functools
import math

import jax
import jax.numpy as jnp
from jax import lax
from jax.experimental import pallas as pl
from jax.experimental.pallas import tpu as pltpu
from jax.sharding import PartitionSpec as P

D = 192
HEADS = 6
HEAD = 32
ZP = 4
WZ = 2
WLAT = 6
WLON = 12
PW = 2
WIN = 144
LONREL = 23
PAIRS = 144
HALF = WLON // 2
LEVELS = WZ * WLAT
HALF_ROWS = HALF * LEVELS
GROUP = 4
GROUPS = WLON // GROUP
GROUP_ROWS = GROUP * LEVELS
BLOCK = HEADS * GROUP_ROWS
STRIP = LONREL * LEVELS
PADDED = 16
TURN = 0
OFFSETS = 24

EPSILON = 1e-05
SCALE = HEAD ** (-0.5)
HIGH = lax.Precision.HIGH
FULL = lax.Precision.HIGHEST


def dot(left, right, precision=HIGH):
    return lax.dot_general(
        left, right, (((1,), (0,)), ((), ())), precision=precision, preferred_element_type=jnp.float32
    )


def dot_right_transposed(left, right, precision=HIGH):
    return lax.dot_general(
        left, right, (((1,), (1,)), ((), ())), precision=precision, preferred_element_type=jnp.float32
    )


def dot_left_transposed(left, right, precision=HIGH):
    return lax.dot_general(
        left, right, (((0,), (0,)), ((), ())), precision=precision, preferred_element_type=jnp.float32
    )


def whole(count):
    return [pl.BlockSpec(memory_space=pltpu.VMEM)] * count


def hbm(*values):
    return [pltpu.with_memory_space_constraint(value, pltpu.HBM) for value in values]


def fetched(pairs, semaphores):
    copies = [pltpu.make_async_copy(*pair, semaphores.at[place]) for place, pair in enumerate(pairs)]
    for copy in copies:
        copy.start()
    return copies


def pack_half(band_ref, grad_ref, target_ref):
    for a in range(WLAT):
        for x in range(HALF):
            band = band_ref[a, x]
            grad = grad_ref[a, x]
            tiles = (band[:, :128], jnp.concatenate([band[:, 128:], grad[:, 128:]], axis=1), grad[:, :128])
            for z in range(ZP):
                c, i = divmod((z + 1) % ZP, WZ)
                row = x * LEVELS + i * WLAT + a
                for tile in range(3):
                    target_ref[tile, c, row : row + 1, :] = tiles[tile][z : z + 1]


def pack_kernel(features_ref, cotangent_ref, sent_ref, band_ref, grad_ref, semaphores):
    pairs = [(features_ref.at[:, HALF:], band_ref), (cotangent_ref.at[:, HALF:], grad_ref)]
    for copy in fetched(pairs, semaphores):
        copy.wait()
    pack_half(band_ref, grad_ref, sent_ref)


def unpack_kernel(own_ref, returned_ref, out_ref):
    for a in range(WLAT):
        for x in range(WLON):
            source_ref = own_ref if x < HALF else returned_ref
            for z in range(ZP):
                c, i = divmod((z + 1) % ZP, WZ)
                row = (x % HALF) * LEVELS + i * WLAT + a
                out_ref[a, x, z : z + 1, :128] = source_ref[c, row : row + 1, :]
                out_ref[a, x, z : z + 1, 128:] = source_ref[2, row : row + 1, c * 64 : (c + 1) * 64]


def pair_order():
    row = lax.broadcasted_iota(jnp.int32, (LEVELS * PADDED, 1), 0)
    key, query = row // PADDED, row % PADDED
    place = (query // WLAT) * 72 + (key // WLAT) * 36 + (query % WLAT) * WLAT + key % WLAT
    place = jnp.where(query < LEVELS, place, -1)
    return (place == lax.broadcasted_iota(jnp.int32, (LEVELS * PADDED, PAIRS), 1)).astype(jnp.bfloat16)


def offset_order():
    row = lax.broadcasted_iota(jnp.int32, (LEVELS * OFFSETS, 1), 0)
    place = (row % OFFSETS) * LEVELS + row // OFFSETS
    columns = lax.broadcasted_iota(jnp.int32, (LEVELS * OFFSETS, LEVELS * OFFSETS), 1)
    return (place == columns).astype(jnp.bfloat16)


def parts_of(value, count):
    parts = []
    for _ in range(count):
        parts.append(value.astype(jnp.bfloat16))
        value = value - parts[-1].astype(jnp.float32)
    return parts


def moved(value, order, dims, count):
    total = None
    for part in parts_of(value, count):
        product = lax.dot_general(part, order, (dims, ((), ())), preferred_element_type=jnp.float32)
        total = product if total is None else total + product
    return total


def normalized(band):
    average = jnp.mean(band, axis=-1, keepdims=True)
    centred = band - average
    inverse = lax.rsqrt(jnp.mean(centred * centred, axis=-1, keepdims=True) + EPSILON)
    return centred * inverse, inverse


def split_tiles(half_ref):
    tiles = [half_ref[tile].reshape(WIN, 128) for tile in range(3)]
    band = jnp.concatenate([tiles[0], tiles[1][:, : D - 128]], axis=1)
    grad = jnp.concatenate([tiles[2], tiles[1][:, D - 128 :]], axis=1)
    return band, grad


def projections(half_ref, out_ref, gain, shift, weight_q, weight_k, weight_v, out_weight):
    band, grad = split_tiles(half_ref)
    unit, inverse = normalized(band)
    tokens = unit * gain + shift
    out_ref[0] = unit
    out_ref[1] = jnp.broadcast_to(inverse, unit.shape)
    out_ref[2] = tokens
    out_ref[3] = grad
    out_ref[4] = dot(tokens, weight_q, FULL) * SCALE
    out_ref[5] = dot(tokens, weight_k, FULL)
    out_ref[6] = dot(tokens, weight_v)
    out_ref[7] = dot_right_transposed(grad, out_weight)


def prepare_kernel(
    bias_hbm, features_hbm, cotangent_hbm, gain_hbm, shift_hbm, qkv_hbm, out_w_hbm,
    table_ref, projected_ref, affine_ref, parts_ref, pairs_ref, offsets_ref,
    turned_ref, strip_ref, bias_ref, qkv_ref, band_ref, grad_ref, own_ref, semaphores,
):
    copies = fetched(
        [
            (bias_hbm, bias_ref),
            (features_hbm.at[:, :HALF], band_ref),
            (cotangent_hbm.at[:, :HALF], grad_ref),
            (gain_hbm, affine_ref.at[0:1]),
            (shift_hbm, affine_ref.at[1:2]),
            (qkv_hbm, qkv_ref),
            (out_w_hbm, parts_ref.at[3]),
        ],
        semaphores,
    )
    pairs, offsets = pair_order(), offset_order()
    pairs_ref[...], offsets_ref[...] = pairs, offsets
    for copy in copies:
        copy.wait()
    pack_half(band_ref, grad_ref, own_ref)
    for part in range(3):
        parts_ref[part] = qkv_ref[:, part * D : (part + 1) * D]
    projections(own_ref, projected_ref, affine_ref[0:1], affine_ref[1:2], *(parts_ref[part] for part in range(4)))
    spare = jnp.zeros((OFFSETS - LONREL, PAIRS), jnp.float32)
    rows = jnp.concatenate(
        [part for c in range(PW) for h in range(HEADS) for part in (bias_ref[h, :, c, :], spare)], axis=0
    )
    turned = None
    for part in parts_of(rows, 3):
        product = lax.dot_general(pairs, part, (((1,), (1,)), ((), ())), preferred_element_type=jnp.float32)
        turned = product if turned is None else turned + product
    turned_ref[...] = turned
    for block in range(PW * HEADS):
        for key in range(LEVELS):
            strip_ref[block * PADDED : (block + 1) * PADDED, key * OFFSETS : (key + 1) * OFFSETS] = turned_ref[
                key * PADDED : (key + 1) * PADDED, block * OFFSETS : (block + 1) * OFFSETS
            ]
    strips = moved(strip_ref[...], offsets, ((1,), (0,)), 3)
    row = lax.broadcasted_iota(jnp.int32, strips.shape, 0)
    level = (row % PADDED) // WLAT
    key_level = (lax.broadcasted_iota(jnp.int32, strips.shape, 1) % LEVELS) // WLAT
    strips = jnp.where((row >= HEADS * PADDED) | (level == key_level), strips, -jnp.inf)
    for c in range(PW):
        for h in range(HEADS):
            first = (c * HEADS + h) * PADDED
            strip = strips[first : first + LEVELS, :STRIP]
            for g in range(GROUP):
                first = h * GROUP_ROWS + g * LEVELS
                table_ref[c, first : first + LEVELS, g * LEVELS : g * LEVELS + STRIP] = strip


def turn_kernel(strip_ref, pairs_ref, offsets_ref, rows_ref, turned_ref):
    pairs, offsets = pairs_ref[...], offsets_ref[...]
    by_level = moved(strip_ref[...], offsets, ((1,), (1,)), 2)
    for block in range(PW * HEADS):
        for key in range(LEVELS):
            turned_ref[key * PADDED : (key + 1) * PADDED, block * OFFSETS : (block + 1) * OFFSETS] = by_level[
                block * PADDED : (block + 1) * PADDED, key * OFFSETS : (key + 1) * OFFSETS
            ]
    rows = moved(turned_ref[...], pairs, ((0,), (0,)), 2)
    half = HEADS * OFFSETS // 2
    for y in range(2):
        first, second = rows[y * half : (y + 1) * half], rows[(y + 2) * half : (y + 3) * half]
        rows_ref[y, :half] = second[:, :128]
        rows_ref[y, half:] = jnp.concatenate(
            [second[:, 128:], first[:, :36], first[:, 108:], jnp.zeros((half, 40), jnp.float32)], axis=1
        )


def finish_kernel(parity_ref, mine_ref, other_ref, weights_ref, norm_ref, bias_ref, weights_out_ref, norm_out_ref):
    low = parity_ref[0] == 0
    mine, other = mine_ref[...], other_ref[...]
    halves = (jnp.where(low, mine, other), jnp.where(low, other, mine))
    half = HEADS * OFFSETS // 2
    for h in range(HEADS):
        first = (h % 3) * OFFSETS
        left = halves[h // 3][first : first + LONREL]
        right = halves[h // 3][half + first : half + first + LONREL]
        bias_ref[h, :, 1, :] = jnp.concatenate([left, right[:, :16]], axis=1)
        bias_ref[h, :, 0, :] = jnp.concatenate(
            [right[:, 16:52], jnp.zeros((LONREL, 72), jnp.float32), right[:, 52:88]], axis=1
        )
    weights_out_ref[...] = unpacked_chunk(weights_ref[...])
    norm = norm_ref[:4] + norm_ref[4:]
    norm_out_ref[:, :128] = norm[:2]
    norm_out_ref[0:1, 128:] = norm[2:3, :64]
    norm_out_ref[1:2, 128:] = norm[2:3, 64:]


def packed_chunk(chunk):
    beside = jnp.concatenate([chunk[40:, 32 * piece : 32 * (piece + 1)] for piece in range(3)], axis=0)
    beside = jnp.concatenate([beside, jnp.zeros((16, 32), chunk.dtype)], axis=0)
    return jnp.concatenate([chunk[:40], beside], axis=1)


def unpacked_chunk(packed):
    last = jnp.concatenate([packed[8 * piece : 8 * (piece + 1), 96:] for piece in range(3)], axis=1)
    return jnp.concatenate([packed[:, :96], last], axis=0)


ORDER = (
    "S0", "D0", "S1", "P0", "D1", "M0", "V0", "P1", "G0",
    "M1", "V1", "G1", "Q0", "K0", "T0", "Q1", "K1", "T1",
)


def halves_of(value):
    high = value.astype(jnp.bfloat16)
    return high, (value - high.astype(jnp.float32)).astype(jnp.bfloat16)


def product(left, right, dims):
    dims = (dims, ((), ()))

    def one(a, b):
        return lax.dot_general(a, b, dims, preferred_element_type=jnp.float32)

    return one(left[0], right[0]) + one(left[0], right[1]) + one(left[1], right[0])


def full_product(left, right, dims):
    dims = (dims, ((), ()))

    def one(a, b):
        return lax.dot_general(a, b, dims, preferred_element_type=jnp.float32)

    low = one(left[0], right[2]) + one(left[2], right[0]) + one(left[1], right[1])
    return low + one(left[0], right[1]) + one(left[1], right[0]) + one(left[0], right[0])


NORMAL = ((1,), (0,))
RIGHT = ((1,), (1,))
LEFT = ((0,), (0,))


def block_kernel(
    factor, packed,
    borrowed_ref, projected_ref, affine_ref, parts_ref, table_ref,
    grad_own_ref, grad_borrowed_ref, weights_ref, strip_grad_ref, norm_ref,
    table_grad_ref, arrived_ref,
):
    gain, shift = affine_ref[0:1], affine_ref[1:2]
    projections(borrowed_ref, arrived_ref, gain, shift, *(parts_ref[part] for part in range(4)))

    def whole_window(index, c):
        rows = slice(c * HALF_ROWS, (c + 1) * HALF_ROWS)
        return jnp.concatenate([arrived_ref[index, rows], projected_ref[index, rows]], axis=0)

    lane = lax.broadcasted_iota(jnp.int32, (1, D), 1) // HEAD
    head_masks = [(lane == h).astype(jnp.float32).astype(jnp.bfloat16) for h in range(HEADS)]
    head_of_lane = lax.broadcasted_iota(jnp.int32, (WIN, D), 1) // HEAD
    strip_grad_ref[...] = jnp.zeros_like(strip_grad_ref)
    table_grad_ref[...] = jnp.zeros_like(table_grad_ref)

    def masked(parts):
        return tuple(jnp.concatenate([part * mask for mask in head_masks], axis=0) for part in parts)

    def joined(value):
        total = value[:WIN]
        for h in range(1, HEADS):
            total = jnp.where(head_of_lane == h, value[h * WIN : (h + 1) * WIN], total)
        return total

    def score(window, c):
        window["keys"] = parts_of(whole_window(5, c), 3)
        window["queries"] = masked(parts_of(whole_window(4, c), 3))
        window["scores"] = full_product(window["queries"], window["keys"], RIGHT)

    def grad_attend(window, c):
        window["values"] = halves_of(whole_window(6, c))
        window["grads"] = masked(halves_of(whole_window(7, c)))
        window["grad_attention"] = product(window["grads"], window["values"], RIGHT)

    def softmax(window, c):
        biased = []
        for h in range(HEADS):
            for g in range(GROUPS):
                first = h * WIN + g * GROUP_ROWS
                start = (WLON - 1 - GROUP * g) * LEVELS
                bias = table_ref[c, h * GROUP_ROWS : (h + 1) * GROUP_ROWS, start : start + WIN]
                biased.append(window["scores"][first : first + GROUP_ROWS] + bias)
        scores = jnp.concatenate(biased, axis=0)
        exponent = jnp.exp(scores - jnp.max(scores, axis=-1, keepdims=True))
        window["attention"] = exponent * (1.0 / jnp.sum(exponent, axis=-1, keepdims=True))
        window["halves"] = halves_of(window["attention"])

    def mix(window, c):
        window["mixture"] = joined(product(window["halves"], window["values"], NORMAL))

    def value_grad(window, c):
        window["grad_v"] = product(window["halves"], window["grads"], LEFT)

    def score_grad(window, c):
        attention, grad_attention = window["attention"], window["grad_attention"]
        weighted = jnp.sum(attention * grad_attention, axis=-1, keepdims=True)
        window["grad_scores"] = attention * (grad_attention - weighted)
        window["score_halves"] = halves_of(window["grad_scores"])

    def query_grad(window, c):
        window["grad_q"] = joined(product(window["score_halves"], window["keys"][:2], NORMAL))

    def key_grad(window, c):
        window["grad_k"] = product(window["score_halves"], window["queries"][:2], LEFT)

    def strip_grad(window, c):
        for h in range(HEADS):
            table_rows = slice((c * HEADS + h) * GROUP_ROWS, (c * HEADS + h + 1) * GROUP_ROWS)
            for g in range(GROUPS):
                first = h * WIN + g * GROUP_ROWS
                start = (WLON - 1 - GROUP * g) * LEVELS
                table_grad_ref[table_rows, start : start + WIN] += window["grad_scores"][first : first + GROUP_ROWS]
            total = None
            for g in range(GROUP):
                first = (c * HEADS + h) * GROUP_ROWS + g * LEVELS
                part = table_grad_ref[first : first + LEVELS, g * LEVELS : g * LEVELS + STRIP]
                total = part if total is None else total + part
            first = (c * HEADS + h) * PADDED
            strip_grad_ref[first : first + LEVELS, :STRIP] = total

    windows = [{}, {}]
    stages = dict(
        S=score, P=softmax, D=grad_attend, M=mix, V=value_grad, G=score_grad, Q=query_grad, K=key_grad, T=strip_grad
    )
    for name, c in ORDER:
        stages[name](windows[int(c)], int(c))

    def rows_of(name):
        return jnp.concatenate([window[name] for window in windows], axis=0)

    grads = [halves_of(value) for value in (rows_of("grad_q") * SCALE, rows_of("grad_k"), rows_of("grad_v"))]
    tokens, window_grad, unit, inverse = (
        jnp.concatenate([whole_window(index, c) for c in range(PW)], axis=0) for index in (2, 3, 0, 1)
    )
    grad_tokens = sum(product(grads[part], halves_of(parts_ref[part]), RIGHT) for part in range(3))
    grad_unit = grad_tokens * gain
    result = window_grad + inverse * (
        grad_unit
        - jnp.mean(grad_unit, axis=-1, keepdims=True)
        - unit * jnp.mean(grad_unit * unit, axis=-1, keepdims=True)
    )
    for ref, offset in ((grad_borrowed_ref, 0), (grad_own_ref, HALF_ROWS)):
        halves = [result[c * WIN + offset : c * WIN + offset + HALF_ROWS] for c in range(PW)]
        for c in range(PW):
            ref[c] = halves[c][:, :128]
        ref[2] = jnp.concatenate([half[:, 128:] for half in halves], axis=1)
    gain_sum = jnp.sum(grad_tokens * unit, axis=0, keepdims=True) * factor
    shift_sum = jnp.sum(grad_tokens, axis=0, keepdims=True) * factor
    norm_ref[...] = jnp.zeros_like(norm_ref)
    norm_ref[:3] = jnp.concatenate(
        [gain_sum[:, :128], shift_sum[:, :128], jnp.concatenate([gain_sum[:, 128:], shift_sum[:, 128:]], axis=1)], axis=0
    )
    token_halves = halves_of(tokens * factor)
    sums = [product(token_halves, grad, LEFT) for grad in grads]
    sums.append(product(halves_of(rows_of("mixture") * factor), halves_of(window_grad), LEFT))
    for block, total in enumerate(sums):
        if not packed:
            weights_ref[:, block * D : (block + 1) * D] = total
            continue
        for y in range(2):
            for lat in range(4):
                chunk = total[48 * lat : 48 * (lat + 1), 96 * y : 96 * (y + 1)]
                place = turned_by((y, block % 2, block // 2), TURN)
                place = (lat // 2,) + place if lat % 2 == 0 else place + (lat // 2,)
                weights_ref[(lat % 2,) + place] = packed_chunk(chunk)


def bits_of(count):
    return [1 << place for place in range(count.bit_length() - 1)]


def partners(first_bits, second_bits):
    lat_count, lon_count = lax.axis_size("lat"), lax.axis_size("lon")
    pairs = []
    for lat in range(lat_count):
        for lon in range(lon_count):
            lat_bit, lon_bit = first_bits if lat % 2 == 0 else second_bits
            pairs.append((lat * lon_count + lon, (lat ^ lat_bit) * lon_count + (lon ^ lon_bit)))
    return pairs


def side(first_bits, second_bits):
    lat, lon = lax.axis_index("lat"), lax.axis_index("lon")
    first, second = ((lat & lat_bit | lon & lon_bit) != 0 for lat_bit, lon_bit in (first_bits, second_bits))
    return jnp.where(lat & 1 == 0, first, second).astype(jnp.int32)


def exchanged(value, step):
    return lax.ppermute(value, ("lat", "lon"), partners(*step))


def kept_and_given(value, step):
    high = side(*step)
    return (
        lax.dynamic_index_in_dim(value, high, 0, keepdims=False),
        lax.dynamic_index_in_dim(value, 1 - high, 0, keepdims=False),
    )


def exchange_all(values, step):
    flat = [value.reshape(-1, 128) for value in values]
    arrived = exchanged(jnp.concatenate(flat, axis=0), step)
    results, first = [], 0
    for value, rows in zip(values, flat):
        results.append(arrived[first : first + rows.shape[0]].reshape(value.shape))
        first += rows.shape[0]
    return results


def turned_by(items, count):
    return items[count:] + items[:count]


def summing_steps(lat_count, lon_count):
    lat_bits, lon_bits = bits_of(lat_count), turned_by(bits_of(lon_count), TURN)
    core, second, *others = [(bit, 0) for bit in lat_bits]
    lons = [(0, bit) for bit in lon_bits]
    first_order = [second] + others + lons
    second_order = lons[:1] + others + lons[1:] + [second]
    return (core, core), list(zip(first_order, second_order)), (lons[-1], lons[0])


def chunks_by_step(weights, lat_count, lon_count):
    rows, columns = weights.shape[0] // lat_count, weights.shape[1] // lon_count
    lat_places, lon_places = len(bits_of(lat_count)), len(bits_of(lon_count))
    split = weights.reshape((2,) * lat_places + (rows,) + (2,) * lon_places + (columns,))
    core, second, *others = list(range(lat_places))[::-1]
    lons = turned_by(list(range(lat_places + 1, lat_places + 1 + lon_places))[::-1], TURN)
    halves = []
    for place, dims in enumerate(([second] + others + lons, lons[:1] + others + lons[1:] + [second])):
        order = [core] + dims + [lat_places, lat_places + 1 + lon_places]
        halves.append(split.transpose(order)[place])
    places = lat_places + lon_places
    split = jnp.stack(halves).reshape((2,) * places + (rows * columns,))
    words = -(-rows * columns // 1024) * 1024
    split = jnp.pad(split, [(0, 0)] * places + [(0, words - rows * columns)])
    return split.reshape((2,) * places + (words // 128, 128))


def shards(features, cotangent, norm_gain, norm_shift, qkv_weight, out_weight, bias_table):
    lat_count, lon_count = lax.axis_size("lat"), lax.axis_size("lon")
    token_count = ZP * features.shape[1] * features.shape[2] * lat_count * lon_count
    factor = 1.0 / math.sqrt(token_count)
    packed = (lat_count, lon_count) == (4, 8)
    f32 = jnp.float32
    shape = jax.ShapeDtypeStruct
    params = pltpu.CompilerParams(vmem_limit_bytes=48 << 20)
    half_shape = shape((3, PW, HALF_ROWS, 128), f32)
    block_shape = (WLAT, WLON, ZP, D)
    features, cotangent = hbm(features.transpose(1, 2, 0, 3), cotangent.transpose(1, 2, 0, 3))
    half_block = pltpu.VMEM((WLAT, HALF, ZP, D), f32)
    sent = pl.pallas_call(
        pack_kernel,
        out_shape=pltpu.VMEM(half_shape.shape, f32),
        in_specs=[pl.BlockSpec(memory_space=pltpu.HBM)] * 2,
        out_specs=whole(1)[0],
        scratch_shapes=[half_block, half_block, pltpu.SemaphoreType.DMA((2,))],
        compiler_params=params,
    )(features, cotangent)
    borrowed = lax.ppermute(sent, "lon", [(s, (s + 1) % lon_count) for s in range(lon_count)])
    projected_shape = (8, WIN, D)
    in_hbm = pl.BlockSpec(memory_space=pltpu.HBM)
    bias, gain_row, shift_row, qkv_rows, out_rows = hbm(
        bias_table[0].transpose(1, 2, 0, 3), norm_gain[None], norm_shift[None], qkv_weight, out_weight
    )
    table, projected, affine, parts, pairs, offsets = pl.pallas_call(
        prepare_kernel,
        out_shape=(
            pltpu.VMEM((PW, GROUP_ROWS * HEADS, 384), f32),
            pltpu.VMEM(projected_shape, f32),
            pltpu.VMEM((2, D), f32),
            pltpu.VMEM((4, D, D), f32),
            pltpu.VMEM((LEVELS * PADDED, PAIRS), jnp.bfloat16),
            pltpu.VMEM((LEVELS * OFFSETS, LEVELS * OFFSETS), jnp.bfloat16),
        ),
        in_specs=[in_hbm] * 7,
        out_specs=tuple(whole(6)),
        scratch_shapes=[
            pltpu.VMEM((LEVELS * PADDED, PW * HEADS * OFFSETS), f32),
            pltpu.VMEM((PW * HEADS * PADDED, LEVELS * OFFSETS), f32),
            pltpu.VMEM((HEADS, LONREL, PW, PAIRS), f32),
            pltpu.VMEM((D, 3 * D), f32),
            half_block,
            half_block,
            pltpu.VMEM(half_shape.shape, f32),
            pltpu.SemaphoreType.DMA((7,)),
        ],
        compiler_params=params,
    )(bias, features, cotangent, gain_row, shift_row, qkv_rows, out_rows)
    grad_half = shape((3, HALF_ROWS, 128), f32)
    grad_own, grad_borrowed, weights, strips, norm = pl.pallas_call(
        functools.partial(block_kernel, factor, packed),
        out_shape=(
            grad_half,
            grad_half,
            shape((2, 2, 2, 2, 2, 40, 128) if packed else (D, 4 * D), f32),
            shape((PW * HEADS * PADDED, LEVELS * OFFSETS), f32),
            shape((8, 128), f32),
        ),
        in_specs=whole(5),
        out_specs=tuple(whole(5)),
        scratch_shapes=[pltpu.VMEM((PW * BLOCK, 384), f32), pltpu.VMEM(projected_shape, f32)],
        compiler_params=params,
    )(borrowed, projected, affine, parts, table)
    if not packed:
        weights = chunks_by_step(weights, lat_count, lon_count)
    rows_shape = shape((2, HEADS * OFFSETS, 128), f32)
    strip_grad = pl.pallas_call(
        turn_kernel,
        out_shape=rows_shape,
        in_specs=whole(3),
        out_specs=whole(1)[0],
        scratch_shapes=[pltpu.VMEM((LEVELS * PADDED, PW * HEADS * OFFSETS), f32)],
        compiler_params=params,
    )(strips, pairs, offsets)
    core_step, steps, strip_step = summing_steps(lat_count, lon_count)
    norm = jnp.where(lax.axis_index("lat") & 2 == 0, norm, jnp.roll(norm, 4, 0))
    strip_grad, given_strip = kept_and_given(strip_grad, strip_step)
    strip_grad = strip_grad + exchanged(given_strip, strip_step)
    shared = steps[-(len(bits_of(lon_count)) - 1) - 1 : -1]
    for step in [core_step] + steps[:-1]:
        kept, given = kept_and_given(weights, step)
        if step in shared:
            if step == shared[0]:
                returned = lax.ppermute(grad_borrowed, "lon", [(s, (s - 1) % lon_count) for s in range(lon_count)])
            more, more_strip, more_norm = exchange_all([given, strip_grad, norm], step)
            strip_grad = strip_grad + more_strip
        else:
            more, more_norm = exchange_all([given, norm], step)
        weights, norm = kept + more, norm + more_norm
    other_strip = exchanged(strip_grad, strip_step)
    kept, given = kept_and_given(weights, steps[-1])
    more, more_norm = exchange_all([given, norm], steps[-1])
    more, returned = lax.optimization_barrier((more, returned))
    weights, norm = kept + more, norm + more_norm
    grad_features = pl.pallas_call(
        unpack_kernel,
        out_shape=shape(block_shape, f32),
        in_specs=whole(2),
        out_specs=whole(1)[0],
        compiler_params=params,
    )(grad_own, returned).transpose(2, 0, 1, 3)
    chunk = weights if packed else jnp.zeros((40, 128), f32)
    parity = side(*strip_step)[None]
    grad_bias, grad_weights, grad_norm = pl.pallas_call(
        finish_kernel,
        out_shape=(shape((HEADS, LONREL, PW, PAIRS), f32), shape((48, 96), f32), shape((2, D), f32)),
        in_specs=[pl.BlockSpec(memory_space=pltpu.SMEM)] + whole(4),
        out_specs=tuple(whole(3)),
        compiler_params=params,
    )(parity, strip_grad, other_strip, chunk, norm)
    grad_bias = grad_bias.transpose(2, 0, 1, 3)[None]
    if not packed:
        rows, columns = D // lat_count, 4 * D // lon_count
        grad_weights = weights.reshape(-1)[: rows * columns].reshape(rows, columns)
    return (grad_features, grad_weights, grad_bias, grad_norm)


def solution(mesh):
    placed = (
        P(None, "lat", "lon", None),
        P(None, "lat", "lon", None),
        P(),
        P(),
        P(),
        P(),
        P("lat", None, None, None, None),
    )
    return jax.shard_map(
        shards,
        mesh=mesh,
        in_specs=placed,
        out_specs=(
            P(None, "lat", "lon", None),
            P("lat", "lon"),
            P("lat", None, None, None, None),
            P(),
        ),
        check_vma=False,
    )
```

```python
import functools
import math

import jax
import jax.numpy as jnp
from jax import lax
from jax.experimental import pallas as pl
from jax.experimental.pallas import tpu as pltpu
from jax.sharding import PartitionSpec as P

D = 192
HEADS = 6
HEAD = 32
ZP = 4
WZ = 2
WLAT = 6
WLON = 12
PW = 2
WIN = 144
LONREL = 23
PAIRS = 144
HALF = WLON // 2
LEVELS = WZ * WLAT
HALF_ROWS = HALF * LEVELS
GROUP = 4
GROUPS = WLON // GROUP
GROUP_ROWS = GROUP * LEVELS
BLOCK = HEADS * GROUP_ROWS
STRIP = LONREL * LEVELS
PADDED = 16
TURN = 0
OFFSETS = 24

EPSILON = 1e-05
SCALE = HEAD ** (-0.5)
HIGH = lax.Precision.HIGH
FULL = lax.Precision.HIGHEST


def dot(left, right, precision=HIGH):
    return lax.dot_general(
        left, right, (((1,), (0,)), ((), ())), precision=precision, preferred_element_type=jnp.float32
    )


def dot_right_transposed(left, right, precision=HIGH):
    return lax.dot_general(
        left, right, (((1,), (1,)), ((), ())), precision=precision, preferred_element_type=jnp.float32
    )


def dot_left_transposed(left, right, precision=HIGH):
    return lax.dot_general(
        left, right, (((0,), (0,)), ((), ())), precision=precision, preferred_element_type=jnp.float32
    )


def whole(count):
    return [pl.BlockSpec(memory_space=pltpu.VMEM)] * count


def hbm(*values):
    return [pltpu.with_memory_space_constraint(value, pltpu.HBM) for value in values]


def fetched(pairs, semaphores):
    copies = [pltpu.make_async_copy(*pair, semaphores.at[place]) for place, pair in enumerate(pairs)]
    for copy in copies:
        copy.start()
    return copies


def pack_half(band_ref, grad_ref, target_ref):
    for a in range(WLAT):
        for x in range(HALF):
            band = band_ref[a, x]
            grad = grad_ref[a, x]
            tiles = (band[:, :128], jnp.concatenate([band[:, 128:], grad[:, 128:]], axis=1), grad[:, :128])
            for z in range(ZP):
                c, i = divmod((z + 1) % ZP, WZ)
                row = x * LEVELS + i * WLAT + a
                for tile in range(3):
                    target_ref[tile, c, row : row + 1, :] = tiles[tile][z : z + 1]


def pack_kernel(features_ref, cotangent_ref, sent_ref, band_ref, grad_ref, semaphores):
    pairs = [(features_ref.at[:, HALF:], band_ref), (cotangent_ref.at[:, HALF:], grad_ref)]
    for copy in fetched(pairs, semaphores):
        copy.wait()
    pack_half(band_ref, grad_ref, sent_ref)


def unpack_kernel(own_ref, returned_ref, out_ref):
    for a in range(WLAT):
        for x in range(WLON):
            source_ref = own_ref if x < HALF else returned_ref
            for z in range(ZP):
                c, i = divmod((z + 1) % ZP, WZ)
                row = (x % HALF) * LEVELS + i * WLAT + a
                out_ref[a, x, z : z + 1, :128] = source_ref[c, row : row + 1, :]
                out_ref[a, x, z : z + 1, 128:] = source_ref[2, row : row + 1, c * 64 : (c + 1) * 64]


def pair_order():
    row = lax.broadcasted_iota(jnp.int32, (LEVELS * PADDED, 1), 0)
    key, query = row // PADDED, row % PADDED
    place = (query // WLAT) * 72 + (key // WLAT) * 36 + (query % WLAT) * WLAT + key % WLAT
    place = jnp.where(query < LEVELS, place, -1)
    return (place == lax.broadcasted_iota(jnp.int32, (LEVELS * PADDED, PAIRS), 1)).astype(jnp.bfloat16)


def offset_order():
    row = lax.broadcasted_iota(jnp.int32, (LEVELS * OFFSETS, 1), 0)
    place = (row % OFFSETS) * LEVELS + row // OFFSETS
    columns = lax.broadcasted_iota(jnp.int32, (LEVELS * OFFSETS, LEVELS * OFFSETS), 1)
    return (place == columns).astype(jnp.bfloat16)


def parts_of(value, count):
    parts = []
    for _ in range(count):
        parts.append(value.astype(jnp.bfloat16))
        value = value - parts[-1].astype(jnp.float32)
    return parts


def moved(value, order, dims, count):
    total = None
    for part in parts_of(value, count):
        product = lax.dot_general(part, order, (dims, ((), ())), preferred_element_type=jnp.float32)
        total = product if total is None else total + product
    return total


def normalized(band):
    average = jnp.mean(band, axis=-1, keepdims=True)
    centred = band - average
    inverse = lax.rsqrt(jnp.mean(centred * centred, axis=-1, keepdims=True) + EPSILON)
    return centred * inverse, inverse


def split_tiles(half_ref):
    tiles = [half_ref[tile].reshape(WIN, 128) for tile in range(3)]
    band = jnp.concatenate([tiles[0], tiles[1][:, : D - 128]], axis=1)
    grad = jnp.concatenate([tiles[2], tiles[1][:, D - 128 :]], axis=1)
    return band, grad


def projections(half_ref, out_ref, gain, shift, weight_q, weight_k, weight_v, out_weight):
    band, grad = split_tiles(half_ref)
    unit, inverse = normalized(band)
    tokens = unit * gain + shift
    out_ref[0] = unit
    out_ref[1] = jnp.broadcast_to(inverse, unit.shape)
    out_ref[2] = tokens
    out_ref[3] = grad
    out_ref[4] = dot(tokens, weight_q, FULL) * SCALE
    out_ref[5] = dot(tokens, weight_k, FULL)
    out_ref[6] = dot(tokens, weight_v)
    out_ref[7] = dot_right_transposed(grad, out_weight)


def prepare_kernel(
    bias_hbm, features_hbm, cotangent_hbm, gain_hbm, shift_hbm, qkv_hbm, out_w_hbm,
    table_ref, projected_ref, affine_ref, parts_ref, pairs_ref, offsets_ref,
    turned_ref, strip_ref, bias_ref, qkv_ref, band_ref, grad_ref, own_ref, semaphores,
):
    copies = fetched(
        [
            (bias_hbm, bias_ref),
            (features_hbm.at[:, :HALF], band_ref),
            (cotangent_hbm.at[:, :HALF], grad_ref),
            (gain_hbm, affine_ref.at[0:1]),
            (shift_hbm, affine_ref.at[1:2]),
            (qkv_hbm, qkv_ref),
            (out_w_hbm, parts_ref.at[3]),
        ],
        semaphores,
    )
    pairs, offsets = pair_order(), offset_order()
    pairs_ref[...], offsets_ref[...] = pairs, offsets
    for copy in copies:
        copy.wait()
    pack_half(band_ref, grad_ref, own_ref)
    for part in range(3):
        parts_ref[part] = qkv_ref[:, part * D : (part + 1) * D]
    projections(own_ref, projected_ref, affine_ref[0:1], affine_ref[1:2], *(parts_ref[part] for part in range(4)))
    spare = jnp.zeros((OFFSETS - LONREL, PAIRS), jnp.float32)
    rows = jnp.concatenate(
        [part for c in range(PW) for h in range(HEADS) for part in (bias_ref[h, :, c, :], spare)], axis=0
    )
    turned = None
    for part in parts_of(rows, 3):
        product = lax.dot_general(pairs, part, (((1,), (1,)), ((), ())), preferred_element_type=jnp.float32)
        turned = product if turned is None else turned + product
    turned_ref[...] = turned
    for block in range(PW * HEADS):
        for key in range(LEVELS):
            strip_ref[block * PADDED : (block + 1) * PADDED, key * OFFSETS : (key + 1) * OFFSETS] = turned_ref[
                key * PADDED : (key + 1) * PADDED, block * OFFSETS : (block + 1) * OFFSETS
            ]
    strips = moved(strip_ref[...], offsets, ((1,), (0,)), 3)
    row = lax.broadcasted_iota(jnp.int32, strips.shape, 0)
    level = (row % PADDED) // WLAT
    key_level = (lax.broadcasted_iota(jnp.int32, strips.shape, 1) % LEVELS) // WLAT
    strips = jnp.where((row >= HEADS * PADDED) | (level == key_level), strips, -jnp.inf)
    for c in range(PW):
        for h in range(HEADS):
            first = (c * HEADS + h) * PADDED
            strip = strips[first : first + LEVELS, :STRIP]
            for g in range(GROUP):
                first = h * GROUP_ROWS + g * LEVELS
                table_ref[c, first : first + LEVELS, g * LEVELS : g * LEVELS + STRIP] = strip


def turn_kernel(strip_ref, pairs_ref, offsets_ref, rows_ref, turned_ref):
    pairs, offsets = pairs_ref[...], offsets_ref[...]
    by_level = moved(strip_ref[...], offsets, ((1,), (1,)), 2)
    for block in range(PW * HEADS):
        for key in range(LEVELS):
            turned_ref[key * PADDED : (key + 1) * PADDED, block * OFFSETS : (block + 1) * OFFSETS] = by_level[
                block * PADDED : (block + 1) * PADDED, key * OFFSETS : (key + 1) * OFFSETS
            ]
    rows = moved(turned_ref[...], pairs, ((0,), (0,)), 2)
    half = HEADS * OFFSETS // 2
    for y in range(2):
        first, second = rows[y * half : (y + 1) * half], rows[(y + 2) * half : (y + 3) * half]
        rows_ref[y, :half] = second[:, :128]
        rows_ref[y, half:] = jnp.concatenate(
            [second[:, 128:], first[:, :36], first[:, 108:], jnp.zeros((half, 40), jnp.float32)], axis=1
        )


def finish_kernel(parity_ref, mine_ref, other_ref, weights_ref, norm_ref, bias_ref, weights_out_ref, norm_out_ref):
    low = parity_ref[0] == 0
    mine, other = mine_ref[...], other_ref[...]
    halves = (jnp.where(low, mine, other), jnp.where(low, other, mine))
    half = HEADS * OFFSETS // 2
    for h in range(HEADS):
        first = (h % 3) * OFFSETS
        left = halves[h // 3][first : first + LONREL]
        right = halves[h // 3][half + first : half + first + LONREL]
        bias_ref[h, :, 1, :] = jnp.concatenate([left, right[:, :16]], axis=1)
        bias_ref[h, :, 0, :] = jnp.concatenate(
            [right[:, 16:52], jnp.zeros((LONREL, 72), jnp.float32), right[:, 52:88]], axis=1
        )
    weights_out_ref[...] = unpacked_chunk(weights_ref[...])
    norm = norm_ref[:4] + norm_ref[4:]
    norm_out_ref[:, :128] = norm[:2]
    norm_out_ref[0:1, 128:] = norm[2:3, :64]
    norm_out_ref[1:2, 128:] = norm[2:3, 64:]


def packed_chunk(chunk):
    beside = jnp.concatenate([chunk[40:, 32 * piece : 32 * (piece + 1)] for piece in range(3)], axis=0)
    beside = jnp.concatenate([beside, jnp.zeros((16, 32), chunk.dtype)], axis=0)
    return jnp.concatenate([chunk[:40], beside], axis=1)


def unpacked_chunk(packed):
    last = jnp.concatenate([packed[8 * piece : 8 * (piece + 1), 96:] for piece in range(3)], axis=1)
    return jnp.concatenate([packed[:, :96], last], axis=0)


ORDER = (
    "S0", "D0", "S1", "P0", "D1", "M0", "V0", "P1", "G0",
    "M1", "V1", "G1", "Q0", "K0", "T0", "Q1", "K1", "T1",
)


def halves_of(value):
    high = value.astype(jnp.bfloat16)
    return high, (value - high.astype(jnp.float32)).astype(jnp.bfloat16)


def product(left, right, dims):
    dims = (dims, ((), ()))

    def one(a, b):
        return lax.dot_general(a, b, dims, preferred_element_type=jnp.float32)

    return one(left[0], right[0]) + one(left[0], right[1]) + one(left[1], right[0])


def full_product(left, right, dims):
    dims = (dims, ((), ()))

    def one(a, b):
        return lax.dot_general(a, b, dims, preferred_element_type=jnp.float32)

    low = one(left[0], right[2]) + one(left[2], right[0]) + one(left[1], right[1])
    return low + one(left[0], right[1]) + one(left[1], right[0]) + one(left[0], right[0])


NORMAL = ((1,), (0,))
RIGHT = ((1,), (1,))
LEFT = ((0,), (0,))


def block_kernel(
    factor, packed,
    borrowed_ref, projected_ref, affine_ref, parts_ref, table_ref,
    grad_own_ref, grad_borrowed_ref, weights_ref, strip_grad_ref, norm_ref,
    table_grad_ref, arrived_ref,
):
    gain, shift = affine_ref[0:1], affine_ref[1:2]
    projections(borrowed_ref, arrived_ref, gain, shift, *(parts_ref[part] for part in range(4)))

    def whole_window(index, c):
        rows = slice(c * HALF_ROWS, (c + 1) * HALF_ROWS)
        return jnp.concatenate([arrived_ref[index, rows], projected_ref[index, rows]], axis=0)

    lane = lax.broadcasted_iota(jnp.int32, (1, D), 1) // HEAD
    head_masks = [(lane == h).astype(jnp.float32).astype(jnp.bfloat16) for h in range(HEADS)]
    head_of_lane = lax.broadcasted_iota(jnp.int32, (WIN, D), 1) // HEAD
    strip_grad_ref[...] = jnp.zeros_like(strip_grad_ref)
    table_grad_ref[...] = jnp.zeros_like(table_grad_ref)

    def masked(parts):
        return tuple(jnp.concatenate([part * mask for mask in head_masks], axis=0) for part in parts)

    def joined(value):
        total = value[:WIN]
        for h in range(1, HEADS):
            total = jnp.where(head_of_lane == h, value[h * WIN : (h + 1) * WIN], total)
        return total

    def score(window, c):
        window["keys"] = parts_of(whole_window(5, c), 3)
        window["queries"] = masked(parts_of(whole_window(4, c), 3))
        window["scores"] = full_product(window["queries"], window["keys"], RIGHT)

    def grad_attend(window, c):
        window["values"] = halves_of(whole_window(6, c))
        window["grads"] = masked(halves_of(whole_window(7, c)))
        window["grad_attention"] = product(window["grads"], window["values"], RIGHT)

    def softmax(window, c):
        biased = []
        for h in range(HEADS):
            for g in range(GROUPS):
                first = h * WIN + g * GROUP_ROWS
                start = (WLON - 1 - GROUP * g) * LEVELS
                bias = table_ref[c, h * GROUP_ROWS : (h + 1) * GROUP_ROWS, start : start + WIN]
                biased.append(window["scores"][first : first + GROUP_ROWS] + bias)
        scores = jnp.concatenate(biased, axis=0)
        exponent = jnp.exp(scores - jnp.max(scores, axis=-1, keepdims=True))
        window["attention"] = exponent * (1.0 / jnp.sum(exponent, axis=-1, keepdims=True))
        window["halves"] = halves_of(window["attention"])

    def mix(window, c):
        window["mixture"] = joined(product(window["halves"], window["values"], NORMAL))

    def value_grad(window, c):
        window["grad_v"] = product(window["halves"], window["grads"], LEFT)

    def score_grad(window, c):
        attention, grad_attention = window["attention"], window["grad_attention"]
        weighted = jnp.sum(attention * grad_attention, axis=-1, keepdims=True)
        window["grad_scores"] = attention * (grad_attention - weighted)
        window["score_halves"] = halves_of(window["grad_scores"])

    def query_grad(window, c):
        window["grad_q"] = joined(product(window["score_halves"], window["keys"][:2], NORMAL))

    def key_grad(window, c):
        window["grad_k"] = product(window["score_halves"], window["queries"][:2], LEFT)

    def strip_grad(window, c):
        for h in range(HEADS):
            table_rows = slice((c * HEADS + h) * GROUP_ROWS, (c * HEADS + h + 1) * GROUP_ROWS)
            for g in range(GROUPS):
                first = h * WIN + g * GROUP_ROWS
                start = (WLON - 1 - GROUP * g) * LEVELS
                table_grad_ref[table_rows, start : start + WIN] += window["grad_scores"][first : first + GROUP_ROWS]
            total = None
            for g in range(GROUP):
                first = (c * HEADS + h) * GROUP_ROWS + g * LEVELS
                part = table_grad_ref[first : first + LEVELS, g * LEVELS : g * LEVELS + STRIP]
                total = part if total is None else total + part
            first = (c * HEADS + h) * PADDED
            strip_grad_ref[first : first + LEVELS, :STRIP] = total

    windows = [{}, {}]
    stages = dict(
        S=score, P=softmax, D=grad_attend, M=mix, V=value_grad, G=score_grad, Q=query_grad, K=key_grad, T=strip_grad
    )
    for name, c in ORDER:
        stages[name](windows[int(c)], int(c))

    def rows_of(name):
        return jnp.concatenate([window[name] for window in windows], axis=0)

    grads = [halves_of(value) for value in (rows_of("grad_q") * SCALE, rows_of("grad_k"), rows_of("grad_v"))]
    tokens, window_grad, unit, inverse = (
        jnp.concatenate([whole_window(index, c) for c in range(PW)], axis=0) for index in (2, 3, 0, 1)
    )
    grad_tokens = sum(product(grads[part], halves_of(parts_ref[part]), RIGHT) for part in range(3))
    grad_unit = grad_tokens * gain
    result = window_grad + inverse * (
        grad_unit
        - jnp.mean(grad_unit, axis=-1, keepdims=True)
        - unit * jnp.mean(grad_unit * unit, axis=-1, keepdims=True)
    )
    for ref, offset in ((grad_borrowed_ref, 0), (grad_own_ref, HALF_ROWS)):
        halves = [result[c * WIN + offset : c * WIN + offset + HALF_ROWS] for c in range(PW)]
        for c in range(PW):
            ref[c] = halves[c][:, :128]
        ref[2] = jnp.concatenate([half[:, 128:] for half in halves], axis=1)
    gain_sum = jnp.sum(grad_tokens * unit, axis=0, keepdims=True) * factor
    shift_sum = jnp.sum(grad_tokens, axis=0, keepdims=True) * factor
    norm_ref[...] = jnp.zeros_like(norm_ref)
    norm_ref[:3] = jnp.concatenate(
        [gain_sum[:, :128], shift_sum[:, :128], jnp.concatenate([gain_sum[:, 128:], shift_sum[:, 128:]], axis=1)], axis=0
    )
    token_halves = halves_of(tokens * factor)
    sums = [product(token_halves, grad, LEFT) for grad in grads]
    sums.append(product(halves_of(rows_of("mixture") * factor), halves_of(window_grad), LEFT))
    for block, total in enumerate(sums):
        if not packed:
            weights_ref[:, block * D : (block + 1) * D] = total
            continue
        for y in range(2):
            for lat in range(4):
                chunk = total[48 * lat : 48 * (lat + 1), 96 * y : 96 * (y + 1)]
                place = turned_by((y, block % 2, block // 2), TURN)
                place = (lat // 2,) + place if lat % 2 == 0 else place + (lat // 2,)
                weights_ref[(lat % 2,) + place] = packed_chunk(chunk)


def bits_of(count):
    return [1 << place for place in range(count.bit_length() - 1)]


def partners(first_bits, second_bits):
    lat_count, lon_count = lax.axis_size("lat"), lax.axis_size("lon")
    pairs = []
    for lat in range(lat_count):
        for lon in range(lon_count):
            lat_bit, lon_bit = first_bits if lat % 2 == 0 else second_bits
            pairs.append((lat * lon_count + lon, (lat ^ lat_bit) * lon_count + (lon ^ lon_bit)))
    return pairs


def side(first_bits, second_bits):
    lat, lon = lax.axis_index("lat"), lax.axis_index("lon")
    first, second = ((lat & lat_bit | lon & lon_bit) != 0 for lat_bit, lon_bit in (first_bits, second_bits))
    return jnp.where(lat & 1 == 0, first, second).astype(jnp.int32)


def exchanged(value, step):
    return lax.ppermute(value, ("lat", "lon"), partners(*step))


def kept_and_given(value, step):
    high = side(*step)
    return (
        lax.dynamic_index_in_dim(value, high, 0, keepdims=False),
        lax.dynamic_index_in_dim(value, 1 - high, 0, keepdims=False),
    )


def exchange_all(values, step):
    flat = [value.reshape(-1, 128) for value in values]
    arrived = exchanged(jnp.concatenate(flat, axis=0), step)
    results, first = [], 0
    for value, rows in zip(values, flat):
        results.append(arrived[first : first + rows.shape[0]].reshape(value.shape))
        first += rows.shape[0]
    return results


def turned_by(items, count):
    return items[count:] + items[:count]


def summing_steps(lat_count, lon_count):
    lat_bits, lon_bits = bits_of(lat_count), turned_by(bits_of(lon_count), TURN)
    core, second, *others = [(bit, 0) for bit in lat_bits]
    lons = [(0, bit) for bit in lon_bits]
    first_order = [second] + others + lons
    second_order = lons[:1] + others + lons[1:] + [second]
    return (core, core), list(zip(first_order, second_order)), (lons[-1], lons[0])


def chunks_by_step(weights, lat_count, lon_count):
    rows, columns = weights.shape[0] // lat_count, weights.shape[1] // lon_count
    lat_places, lon_places = len(bits_of(lat_count)), len(bits_of(lon_count))
    split = weights.reshape((2,) * lat_places + (rows,) + (2,) * lon_places + (columns,))
    core, second, *others = list(range(lat_places))[::-1]
    lons = turned_by(list(range(lat_places + 1, lat_places + 1 + lon_places))[::-1], TURN)
    halves = []
    for place, dims in enumerate(([second] + others + lons, lons[:1] + others + lons[1:] + [second])):
        order = [core] + dims + [lat_places, lat_places + 1 + lon_places]
        halves.append(split.transpose(order)[place])
    places = lat_places + lon_places
    split = jnp.stack(halves).reshape((2,) * places + (rows * columns,))
    words = -(-rows * columns // 1024) * 1024
    split = jnp.pad(split, [(0, 0)] * places + [(0, words - rows * columns)])
    return split.reshape((2,) * places + (words // 128, 128))


def shards(features, cotangent, norm_gain, norm_shift, qkv_weight, out_weight, bias_table):
    lat_count, lon_count = lax.axis_size("lat"), lax.axis_size("lon")
    token_count = ZP * features.shape[1] * features.shape[2] * lat_count * lon_count
    factor = 1.0 / math.sqrt(token_count)
    packed = (lat_count, lon_count) == (4, 8)
    f32 = jnp.float32
    shape = jax.ShapeDtypeStruct
    params = pltpu.CompilerParams(vmem_limit_bytes=48 << 20)
    half_shape = shape((3, PW, HALF_ROWS, 128), f32)
    block_shape = (WLAT, WLON, ZP, D)
    features, cotangent = hbm(features.transpose(1, 2, 0, 3), cotangent.transpose(1, 2, 0, 3))
    half_block = pltpu.VMEM((WLAT, HALF, ZP, D), f32)
    sent = pl.pallas_call(
        pack_kernel,
        out_shape=pltpu.VMEM(half_shape.shape, f32),
        in_specs=[pl.BlockSpec(memory_space=pltpu.HBM)] * 2,
        out_specs=whole(1)[0],
        scratch_shapes=[half_block, half_block, pltpu.SemaphoreType.DMA((2,))],
        compiler_params=params,
    )(features, cotangent)
    borrowed = lax.ppermute(sent, "lon", [(s, (s + 1) % lon_count) for s in range(lon_count)])
    projected_shape = (8, WIN, D)
    in_hbm = pl.BlockSpec(memory_space=pltpu.HBM)
    bias, gain_row, shift_row, qkv_rows, out_rows = hbm(
        bias_table[0].transpose(1, 2, 0, 3), norm_gain[None], norm_shift[None], qkv_weight, out_weight
    )
    table, projected, affine, parts, pairs, offsets = pl.pallas_call(
        prepare_kernel,
        out_shape=(
            pltpu.VMEM((PW, GROUP_ROWS * HEADS, 384), f32),
            pltpu.VMEM(projected_shape, f32),
            pltpu.VMEM((2, D), f32),
            pltpu.VMEM((4, D, D), f32),
            pltpu.VMEM((LEVELS * PADDED, PAIRS), jnp.bfloat16),
            pltpu.VMEM((LEVELS * OFFSETS, LEVELS * OFFSETS), jnp.bfloat16),
        ),
        in_specs=[in_hbm] * 7,
        out_specs=tuple(whole(6)),
        scratch_shapes=[
            pltpu.VMEM((LEVELS * PADDED, PW * HEADS * OFFSETS), f32),
            pltpu.VMEM((PW * HEADS * PADDED, LEVELS * OFFSETS), f32),
            pltpu.VMEM((HEADS, LONREL, PW, PAIRS), f32),
            pltpu.VMEM((D, 3 * D), f32),
            half_block,
            half_block,
            pltpu.VMEM(half_shape.shape, f32),
            pltpu.SemaphoreType.DMA((7,)),
        ],
        compiler_params=params,
    )(bias, features, cotangent, gain_row, shift_row, qkv_rows, out_rows)
    grad_half = shape((3, HALF_ROWS, 128), f32)
    grad_own, grad_borrowed, weights, strips, norm = pl.pallas_call(
        functools.partial(block_kernel, factor, packed),
        out_shape=(
            grad_half,
            grad_half,
            shape((2, 2, 2, 2, 2, 40, 128) if packed else (D, 4 * D), f32),
            shape((PW * HEADS * PADDED, LEVELS * OFFSETS), f32),
            shape((8, 128), f32),
        ),
        in_specs=whole(5),
        out_specs=tuple(whole(5)),
        scratch_shapes=[pltpu.VMEM((PW * BLOCK, 384), f32), pltpu.VMEM(projected_shape, f32)],
        compiler_params=params,
    )(borrowed, projected, affine, parts, table)
    if not packed:
        weights = chunks_by_step(weights, lat_count, lon_count)
    rows_shape = shape((2, HEADS * OFFSETS, 128), f32)
    strip_grad = pl.pallas_call(
        turn_kernel,
        out_shape=rows_shape,
        in_specs=whole(3),
        out_specs=whole(1)[0],
        scratch_shapes=[pltpu.VMEM((LEVELS * PADDED, PW * HEADS * OFFSETS), f32)],
        compiler_params=params,
        cost_estimate=pl.CostEstimate(flops=1_300_000_000, bytes_accessed=400_000, transcendentals=0),
    )(strips, pairs, offsets)
    core_step, steps, strip_step = summing_steps(lat_count, lon_count)
    norm = jnp.where(lax.axis_index("lat") & 2 == 0, norm, jnp.roll(norm, 4, 0))
    strip_grad, given_strip = kept_and_given(strip_grad, strip_step)
    strip_grad = strip_grad + exchanged(given_strip, strip_step)
    shared = steps[-(len(bits_of(lon_count)) - 1) - 1 : -1]
    for step in [core_step] + steps[:-1]:
        kept, given = kept_and_given(weights, step)
        if step in shared:
            if step == shared[0]:
                returned = lax.ppermute(grad_borrowed, "lon", [(s, (s - 1) % lon_count) for s in range(lon_count)])
            more, more_strip, more_norm = exchange_all([given, strip_grad, norm], step)
            strip_grad = strip_grad + more_strip
        else:
            more, more_norm = exchange_all([given, norm], step)
        weights, norm = kept + more, norm + more_norm
    other_strip = exchanged(strip_grad, strip_step)
    kept, given = kept_and_given(weights, steps[-1])
    more, more_norm = exchange_all([given, norm], steps[-1])
    more, returned = lax.optimization_barrier((more, returned))
    weights, norm = kept + more, norm + more_norm
    grad_features = pl.pallas_call(
        unpack_kernel,
        out_shape=shape(block_shape, f32),
        in_specs=whole(2),
        out_specs=whole(1)[0],
        compiler_params=params,
        cost_estimate=pl.CostEstimate(flops=0, bytes_accessed=3_600_000, transcendentals=0),
    )(grad_own, returned).transpose(2, 0, 1, 3)
    chunk = weights if packed else jnp.zeros((40, 128), f32)
    parity = side(*strip_step)[None]
    grad_bias, grad_weights, grad_norm = pl.pallas_call(
        finish_kernel,
        out_shape=(shape((HEADS, LONREL, PW, PAIRS), f32), shape((48, 96), f32), shape((2, D), f32)),
        in_specs=[pl.BlockSpec(memory_space=pltpu.SMEM)] + whole(4),
        out_specs=tuple(whole(3)),
        compiler_params=params,
    )(parity, strip_grad, other_strip, chunk, norm)
    grad_bias = grad_bias.transpose(2, 0, 1, 3)[None]
    if not packed:
        rows, columns = D // lat_count, 4 * D // lon_count
        grad_weights = weights.reshape(-1)[: rows * columns].reshape(rows, columns)
    return (grad_features, grad_weights, grad_bias, grad_norm)


def solution(mesh):
    placed = (
        P(None, "lat", "lon", None),
        P(None, "lat", "lon", None),
        P(),
        P(),
        P(),
        P(),
        P("lat", None, None, None, None),
    )
    return jax.shard_map(
        shards,
        mesh=mesh,
        in_specs=placed,
        out_specs=(
            P(None, "lat", "lon", None),
            P("lat", "lon"),
            P("lat", None, None, None, None),
            P(),
        ),
        check_vma=False,
    )
```
